512 devices in a mesh: lat: 32 (over z_lo, y), lon: 16 (over x, z_hi, core).
Axes of the slice: x: 4, y: 8, z: 8 (z_hi: 2, z_lo: 4; z = z_hi * 4 + z_lo), core: 2. Of those that a mesh axis runs over, the one named last changes fastest.
Arguments:
- saved: bfloat16 [384, 1440, 128], P('lat', 'lon'), may hold values from -6 to 6
- cotangent: bfloat16 [384, 1440, 128], P('lat', 'lon'), may hold values from -6 to 6
- w_in: bfloat16 [128, 512], replicated, may hold values from -0.5 to 0.5
- b_in: float32 [512], replicated, may hold values from -4 to 4
- w_mid: bfloat16 [512, 512], replicated, may hold values from -0.25 to 0.25
- b_mid: float32 [512], replicated, may hold values from -4 to 4
- w_out: bfloat16 [512, 128], replicated, may hold values from -0.25 to 0.25
- spectral_gain: float32 [384, 128], replicated, may hold values from 0.2 to 2
- basis_in: bfloat16 [384, 368, 384], P(None, 'lon', 'lat'), may hold values from -0.3125 to 0.3125
- basis_out: bfloat16 [384, 368, 384], P('lat', 'lon'), may hold values from -0.3125 to 0.3125
Outputs:
- state_grad: float32 [384, 1440, 128], P('lat', 'lon')
The draws below stay inside these ranges and needn't reach their ends.
All inputs are finite; a program needn't handle non-finite values.
Results may differ from the reference program's by a relative error of at most 0.0065.
Values may be sent and summed in bfloat16 or wider, within the bound.
No kernel may reach another device: no remote copies, remote signals or barrier semaphores. Data moves between devices by JAX's collectives and lax.ppermute only.
A program may use at most 64 MiB of HBM per device.

```python
import math
import jax
import jax.numpy as jnp
from jax import lax

NLAT = 384
NLON = 1440
NM = 368
NL = 384
UNITS = 512
CHAN = 128


def level_of(own_key, extent, cuts, smallest, largest):
    gain = 1.0
    for dim, parts in cuts:
        steps = jax.random.uniform(jax.random.fold_in(jax.random.fold_in(own_key, 6), dim), (parts,), jnp.float32, smallest / len(cuts), largest / len(cuts))
        gain = gain * jnp.repeat(jnp.exp(steps), extent[dim] // parts).reshape((-1,) + (1,) * (len(extent) - 1 - dim))
    return gain


def centred(key, dims, deviation, limit, split=(), kind=jnp.bfloat16):
    drawn = deviation * jax.random.normal(key, dims, jnp.float32)
    if split:
        drawn = drawn * level_of(key, dims, split, -0.22, 0.18)
    return jnp.clip(drawn, -limit, limit).astype(kind)


def setup_inputs(seed: int = 0) -> dict:
    streams_of = jax.random.split(jax.random.key(seed), 11)
    saved = centred(streams_of[0], (NLAT, NLON, CHAN), 1.0, 6.0, ((0, 32), (1, 16)))
    cotangent = centred(streams_of[1], (NLAT, NLON, CHAN), 1.0, 6.0, ((0, 32), (1, 16)))
    w_in = centred(streams_of[2], (CHAN, UNITS), CHAN ** -0.5, 0.5)
    b_in = centred(streams_of[3], (UNITS,), 0.7, 4.0, (), jnp.float32)
    w_mid = centred(streams_of[4], (UNITS, UNITS), UNITS ** -0.5, 0.25)
    b_mid = centred(streams_of[5], (UNITS,), 0.7, 4.0, (), jnp.float32)
    w_out = centred(streams_of[6], (UNITS, CHAN), UNITS ** -0.5, 0.25)
    spectral_gain = jnp.clip(jnp.exp(jax.random.uniform(streams_of[7], (NL, CHAN), jnp.float32, math.log(0.2), math.log(2.0))), 0.2, 2.0)
    basis_in = centred(streams_of[8], (NLAT, NM, NL), NLAT ** -0.5, 0.3125, ((1, 16), (2, 32)))
    basis_out = centred(streams_of[9], (NLAT, NM, NL), NL ** -0.5, 0.3125, ((0, 32), (1, 16)))
    return dict(saved=saved, cotangent=cotangent, w_in=w_in, b_in=b_in, w_mid=w_mid, b_mid=b_mid, w_out=w_out, spectral_gain=spectral_gain, basis_in=basis_in, basis_out=basis_out)


def silu_slope(value):
    sigm = jax.nn.sigmoid(value)
    return sigm * (1.0 + value * (1.0 - sigm))


def column_back(saved_rows, cotan_rows, w_in, b_in, w_mid, b_mid, w_out):
    first = jnp.einsum('yc,cu->yu', saved_rows.astype(jnp.float32), w_in.astype(jnp.float32)) + b_in
    act_one = jax.nn.silu(first).astype(jnp.bfloat16)
    second = jnp.einsum('yu,uv->yv', act_one.astype(jnp.float32), w_mid.astype(jnp.float32)) + b_mid
    upward = jnp.einsum('yc,uc->yu', cotan_rows.astype(jnp.float32), w_out.astype(jnp.float32))
    back_two = (upward * silu_slope(second)).astype(jnp.bfloat16)
    inward = jnp.einsum('yv,uv->yu', back_two.astype(jnp.float32), w_mid.astype(jnp.float32))
    back_one = (inward * silu_slope(first)).astype(jnp.bfloat16)
    return cotan_rows.astype(jnp.float32) + jnp.einsum('yu,cu->yc', back_one.astype(jnp.float32), w_in.astype(jnp.float32))


def reference(saved, cotangent, w_in, b_in, w_mid, b_mid, w_out, spectral_gain, basis_in, basis_out):
    def one_latitude(pair):
        return column_back(pair[0], pair[1], w_in, b_in, w_mid, b_mid, w_out)

    grad_grid = lax.map(one_latitude, (saved, cotangent))
    spectrum = jnp.fft.rfft(grad_grid, axis=1)[:, :NM, :]
    fourier = jnp.stack([jnp.real(spectrum), jnp.imag(spectrum)], axis=0).astype(jnp.float32).astype(jnp.bfloat16)
    wave_index = jnp.arange(NL, dtype=jnp.int32)
    gain_rows = spectral_gain[None, :, :]

    def per_mode(mode_index):
        keep = wave_index[None, :] >= mode_index
        table_in = lax.dynamic_index_in_dim(basis_in, mode_index, 1, keepdims=False).astype(jnp.float32)
        table_in = jnp.where(keep, table_in, jnp.zeros_like(table_in))
        table_out = lax.dynamic_index_in_dim(basis_out, mode_index, 1, keepdims=False).astype(jnp.float32)
        table_out = jnp.where(keep, table_out, jnp.zeros_like(table_out))
        column = lax.dynamic_index_in_dim(fourier, mode_index, 2, keepdims=False).astype(jnp.float32)
        spectra = jnp.einsum('xl,rxc->rlc', table_in, column, precision=lax.Precision.HIGHEST)
        filtered = (spectra * gain_rows).astype(jnp.bfloat16).astype(jnp.float32)
        return jnp.einsum('xl,rlc->rxc', table_out, filtered, precision=lax.Precision.HIGHEST)

    modes = lax.map(per_mode, jnp.arange(NM, dtype=jnp.int32))
    coeffs = jnp.transpose(modes[:, 0] + 1j * modes[:, 1], (1, 0, 2))
    coeffs = jnp.pad(coeffs, ((0, 0), (0, NLON // 2 + 1 - NM), (0, 0)))
    return jnp.fft.irfft(coeffs, n=NLON, axis=1).astype(jnp.float32)
```

```python
import numpy as np
import jax
import jax.numpy as jnp
from jax import lax
from jax.experimental import pallas as pl
from jax.experimental.pallas import tpu as pltpu
from jax.sharding import PartitionSpec as P

bf16 = jnp.bfloat16
f32 = jnp.float32

LAT_DEV, LON_DEV = 32, 16
X_DEV, Y_DEV = 12, 90
Y_PAD = 96
NLAT, NLON, NM, NL, CHAN = 384, 1440, 368, 384, 128
M_DEV = 23
X_SUB, C_SUB = 3, 32
CG = CHAN // C_SUB
XG = X_DEV // X_SUB
DEVS = LAT_DEV * LON_DEV
ROWS = 2 * NM
VMEM = 40 * 1024 * 1024


def zonal_tables():
    order = (M_DEV * np.arange(LON_DEV)[None, :] + np.arange(M_DEV)[:, None]).reshape(-1)
    turns = (order[:, None] * np.arange(NLON)[None, :]) % NLON
    angles = turns.astype(np.float64) * (2.0 * np.pi / NLON)
    table = np.stack([np.cos(angles), -np.sin(angles)], 1).reshape(ROWS, NLON)
    weight = np.where(order == 0, 1.0, 2.0) / NLON
    back = (table * np.repeat(weight, 2)[:, None]).T

    def pad_y(t, axis):
        shape = list(t.shape)
        shape[axis : axis + 1] = [LON_DEV, Y_DEV]
        widths = [(0, 0)] * len(shape)
        widths[axis + 1] = (0, Y_PAD - Y_DEV)
        t = np.pad(t.reshape(shape), widths)
        shape = list(t.shape)
        shape[axis : axis + 2] = [LON_DEV * Y_PAD]
        return t.reshape(shape)

    return (
        np.asarray(pad_y(table, 1), dtype=jnp.bfloat16),
        np.asarray(pad_y(back, 0), dtype=jnp.bfloat16),
    )


def order_tables():
    index = np.arange(NL)
    pick_in = np.zeros((NL, LAT_DEV * 24), np.float32)
    pick_in[index, 24 * (index // 12) + index % 12] = 1
    xx, i, xg = np.meshgrid(np.arange(X_SUB), np.arange(LAT_DEV), np.arange(XG), indexing="ij")
    xx, i, xg = xx.reshape(-1), i.reshape(-1), xg.reshape(-1)
    pick_out = np.zeros((NLAT, LAT_DEV * 24), np.float32)
    pick_out[index, 24 * i + 12 + X_SUB * xg + xx] = 1
    natural = np.zeros((NLAT, NLAT), np.float32)
    natural[12 * i + X_SUB * xg + xx, index] = 1
    return (
        np.asarray(pick_in, dtype=jnp.bfloat16),
        np.asarray(pick_out, dtype=jnp.bfloat16),
        np.asarray(natural, dtype=jnp.bfloat16),
    )


def dot(a, b):
    return lax.dot_general(a, b, (((1,), (0,)), ((), ())), preferred_element_type=f32)


def dot_t(a, b):
    return lax.dot_general(a, b, (((1,), (1,)), ((), ())), preferred_element_type=f32)


def sigmoid(v):
    return 0.5 * jnp.tanh(0.5 * v) + 0.5


def network_kernel(saved, cotan, w_in, b_in, w_mid, b_mid, w_out, out, rows_s, rows_c):
    rows_s[...] = jnp.zeros_like(rows_s)
    rows_c[...] = jnp.zeros_like(rows_c)
    for x in range(X_DEV):
        rows_s[x, 0:Y_DEV, :] = saved[x]
        rows_c[x, 0:Y_DEV, :] = cotan[x]
    for xg in range(XG):
        s = rows_s[X_SUB * xg : X_SUB * (xg + 1)].reshape(X_SUB * Y_PAD, CHAN)
        c = rows_c[X_SUB * xg : X_SUB * (xg + 1)].reshape(X_SUB * Y_PAD, CHAN)
        first = dot(s, w_in[...]) + b_in[...]
        sig = sigmoid(first)
        act = first * sig
        slope_one = sig + act * (1.0 - sig)
        second = dot(act.astype(bf16), w_mid[...]) + b_mid[...]
        sig = sigmoid(second)
        slope_two = sig * (1.0 + second * (1.0 - sig))
        back_two = (dot_t(c, w_out[...]) * slope_two).astype(bf16)
        back_one = (dot_t(back_two, w_mid[...]) * slope_one).astype(bf16)
        grad = c.astype(f32) + dot_t(back_one, w_in[...])
        grad = grad.reshape(X_SUB, Y_PAD, CHAN)
        for cg in range(CG):
            parts = [grad[xx][:, C_SUB * cg : C_SUB * (cg + 1)] for xx in range(X_SUB)]
            parts.append(jnp.zeros((Y_PAD, C_SUB), f32))
            out[CG * xg + cg] = jnp.concatenate(parts, axis=1).astype(bf16)


def zonal_kernel(circles, table, out):
    g = circles[...].reshape(LON_DEV * Y_PAD, 128)
    out[0:ROWS, :] = dot(table[...], g).astype(bf16)
    out[ROWS:, :] = jnp.zeros((2 * DEVS - ROWS, 128), bf16)


def legendre_kernel(mode, coeffs, bases, gain, pick_in, pick_out, natural, out, rows):
    m = mode[0]
    rows[...] = coeffs[...].astype(f32)
    packs = [rows[pl.ds(s, 128, stride=8), :] for s in range(2 * CG)]
    stack = []
    for xx in range(X_SUB):
        parts = [
            packs[2 * cg + r][:, C_SUB * xx : C_SUB * (xx + 1)] for r in range(2) for cg in range(CG)
        ]
        stack.append(jnp.concatenate(parts, axis=1))
    fourier = jnp.concatenate(stack, axis=0).astype(bf16)
    fourier = dot(natural[...], fourier).astype(bf16)
    table = dot(pick_in[...], bases[...])
    waves = lax.broadcasted_iota(jnp.int32, (NL, NLAT), 0)
    table = jnp.where(waves >= m, table, 0.0).astype(bf16)
    gains = jnp.concatenate([gain[...], gain[...]], axis=1)
    filtered = (dot(table, fourier) * gains).astype(bf16)
    table = dot(pick_out[...], bases[...])
    waves = lax.broadcasted_iota(jnp.int32, (NLAT, NL), 1)
    table = jnp.where(waves >= m, table, 0.0).astype(bf16)
    result = dot(table, filtered)
    for cg in range(CG):
        for r in range(2):
            first = CHAN * r + C_SUB * cg
            parts = [result[128 * xx : 128 * (xx + 1), first : first + C_SUB] for xx in range(X_SUB)]
            parts.append(jnp.zeros((128, C_SUB), f32))
            rows[pl.ds(2 * cg + r, 128, stride=8), :] = jnp.concatenate(parts, axis=1)
    out[...] = rows[...].astype(bf16)


def inverse_kernel(coeffs, table, out):
    z = coeffs[0:ROWS, :]
    out[...] = dot(table[...], z).astype(bf16).reshape(LON_DEV, Y_PAD, 128)


def grid_kernel(pieces, out):
    for xg in range(XG):
        blocks = [pieces[CG * xg + cg].astype(f32) for cg in range(CG)]
        for xx in range(X_SUB):
            parts = [b[:, C_SUB * xx : C_SUB * (xx + 1)] for b in blocks]
            out[X_SUB * xg + xx] = jnp.concatenate(parts, axis=1)[0:Y_DEV]


def call(kernel, shape, dtype, scratch=(), smem=0, flops=0, moved=0):
    def run(*args):
        specs = [
            pl.BlockSpec(memory_space=pltpu.SMEM if k < smem else pltpu.VMEM) for k in range(len(args))
        ]
        return pl.pallas_call(
            kernel,
            out_shape=jax.ShapeDtypeStruct(shape, dtype),
            in_specs=specs,
            out_specs=pl.BlockSpec(memory_space=pltpu.VMEM),
            scratch_shapes=list(scratch),
            compiler_params=pltpu.CompilerParams(vmem_limit_bytes=VMEM),
            cost_estimate=pl.CostEstimate(flops=flops, bytes_accessed=moved, transcendentals=0),
        )(*args)

    return run


def on_device(
    saved, cotangent, w_in, b_in, w_mid, b_mid, w_out, spectral_gain, basis_in, basis_out
):
    forward, back = zonal_tables()
    pick_in, pick_out, natural = order_tables()
    bases = jnp.concatenate(
        [jnp.transpose(basis_in, (1, 2, 0)), jnp.transpose(basis_out, (1, 0, 2))], axis=1
    )
    bases = jnp.pad(bases, ((0, LAT_DEV - M_DEV), (0, 0), (0, 0)))
    bases = lax.all_to_all(bases, "lat", 0, 0, tiled=True).reshape(LAT_DEV * 24, NL)

    pad = pltpu.VMEM((X_DEV, Y_PAD, CHAN), bf16)
    pieces = call(network_kernel, (LON_DEV, Y_PAD, 128), bf16, (pad, pad), flops=1_700_000_000)(
        saved, cotangent, w_in, b_in.reshape(1, -1), w_mid, b_mid.reshape(1, -1), w_out
    )
    pieces = lax.all_to_all(pieces, "lon", 0, 0, tiled=True)
    coeffs = call(zonal_kernel, (2 * DEVS, 128), bf16, flops=300_000_000)(pieces, jnp.asarray(forward))
    coeffs = lax.all_to_all(coeffs.reshape(DEVS, 2, 128), ("lat", "lon"), 0, 0, tiled=True)
    mode = (M_DEV * lax.axis_index("lon") + lax.axis_index("lat")).astype(jnp.int32).reshape(1)
    coeffs = call(
        legendre_kernel,
        (2 * DEVS, 128),
        bf16,
        (pltpu.VMEM((2 * DEVS, 128), f32),),
        smem=1,
        flops=800_000_000,
    )(
        mode,
        coeffs.reshape(2 * DEVS, 128),
        bases,
        spectral_gain,
        jnp.asarray(pick_in),
        jnp.asarray(pick_out),
        jnp.asarray(natural),
    )
    coeffs = lax.all_to_all(coeffs.reshape(DEVS, 2, 128), ("lat", "lon"), 0, 0, tiled=True)
    pieces = call(inverse_kernel, (LON_DEV, Y_PAD, 128), bf16, flops=300_000_000)(
        coeffs.reshape(2 * DEVS, 128), jnp.asarray(back)
    )
    pieces = lax.all_to_all(pieces, "lon", 0, 0, tiled=True)
    return call(grid_kernel, (X_DEV, Y_DEV, CHAN), f32)(pieces)


def solution(mesh):
    placed = (
        P("lat", "lon", None),
        P("lat", "lon", None),
        P(),
        P(),
        P(),
        P(),
        P(),
        P(),
        P(None, "lon", "lat"),
        P("lat", "lon", None),
    )
    return jax.shard_map(
        on_device, mesh=mesh, in_specs=placed, out_specs=P("lat", "lon", None), check_vma=False
    )
```

```python
import numpy as np
import jax
import jax.numpy as jnp
from jax import lax
from jax.experimental import pallas as pl
from jax.experimental.pallas import tpu as pltpu
from jax.sharding import PartitionSpec as P

bf16 = jnp.bfloat16
f32 = jnp.float32

LAT_DEV, LON_DEV = 32, 16
X_DEV, Y_DEV = 12, 90
Y_PAD = 96
Y_MAIN, Y_EXT = 72, 24
NLAT, NLON, NM, NL, CHAN = 384, 1440, 368, 384, 128
M_DEV = 23
X_SUB, C_SUB = 3, 32
CG = CHAN // C_SUB
XG = X_DEV // X_SUB
DEVS = LAT_DEV * LON_DEV
ROWS = 2 * NM
VMEM = 40 * 1024 * 1024


def zonal_tables():
    order = (M_DEV * np.arange(LON_DEV)[None, :] + np.arange(M_DEV)[:, None]).reshape(-1)
    turns = (order[:, None] * np.arange(NLON)[None, :]) % NLON
    angles = turns.astype(np.float64) * (2.0 * np.pi / NLON)
    table = np.stack([np.cos(angles), -np.sin(angles)], 1).reshape(ROWS, NLON)
    weight = np.where(order == 0, 1.0, 2.0) / NLON
    back = table * np.repeat(weight, 2)[:, None]

    def split_y(t):
        t = np.pad(t.reshape(ROWS, LON_DEV, Y_DEV), ((0, 0), (0, 0), (0, Y_PAD - Y_DEV)))
        main = t[:, :, :Y_MAIN].reshape(ROWS, LON_DEV * Y_MAIN)
        extra = t[:, :, Y_MAIN:].reshape(ROWS, LON_DEV * Y_EXT)
        return np.concatenate([main, extra], 1)

    return (
        np.asarray(split_y(table), dtype=jnp.bfloat16),
        np.ascontiguousarray(split_y(back).T).astype(jnp.bfloat16),
    )


def dot(a, b):
    return lax.dot_general(a, b, (((1,), (0,)), ((), ())), preferred_element_type=f32)


def dot_t(a, b):
    return lax.dot_general(a, b, (((1,), (1,)), ((), ())), preferred_element_type=f32)


def sigmoid(v):
    return 0.5 * jnp.tanh(0.5 * v) + 0.5


def network_kernel(
    saved_h, cotan_h, w_in_h, b_in_h, w_mid_h, b_mid_h, w_out_h, out,
    saved, cotan, w_in, b_in, w_mid, b_mid, w_out, rows_s, rows_c, sems,
):
    pairs = (
        (saved_h, saved), (w_in_h, w_in), (b_in_h, b_in), (w_mid_h, w_mid),
        (b_mid_h, b_mid), (cotan_h, cotan), (w_out_h, w_out),
    )
    copies = [pltpu.make_async_copy(a, b, sems.at[k]) for k, (a, b) in enumerate(pairs)]
    for copy in copies:
        copy.start()
    rows_s[...] = jnp.zeros_like(rows_s)
    rows_c[...] = jnp.zeros_like(rows_c)
    for copy in copies:
        copy.wait()
    for x in range(X_DEV):
        rows_s[x, 0:Y_DEV, :] = saved[x]
        rows_c[x, 0:Y_DEV, :] = cotan[x]
    for xg in range(XG):
        s = rows_s[X_SUB * xg : X_SUB * (xg + 1)].reshape(X_SUB * Y_PAD, CHAN)
        c = rows_c[X_SUB * xg : X_SUB * (xg + 1)].reshape(X_SUB * Y_PAD, CHAN)
        first = dot(s, w_in[...]) + b_in[...]
        sig = sigmoid(first)
        act = first * sig
        slope_one = sig + act * (1.0 - sig)
        second = dot(act.astype(bf16), w_mid[...]) + b_mid[...]
        sig = sigmoid(second)
        slope_two = sig * (1.0 + second * (1.0 - sig))
        back_two = (dot_t(c, w_out[...]) * slope_two).astype(bf16)
        back_one = (dot_t(back_two, w_mid[...]) * slope_one).astype(bf16)
        grad = c.astype(f32) + dot_t(back_one, w_in[...])
        grad = grad.reshape(X_SUB, Y_PAD, CHAN)
        for cg in range(CG):
            parts = [grad[xx][:, C_SUB * cg : C_SUB * (cg + 1)] for xx in range(X_SUB)]
            parts = [p[0:Y_MAIN] for p in parts] + [
                jnp.concatenate([p[Y_MAIN:] for p in parts], axis=0)
            ]
            out[CG * xg + cg] = jnp.concatenate(parts, axis=1).astype(bf16)


def zonal_kernel(circles, table, out):
    main, extra = [], []
    for j in range(LON_DEV):
        piece = circles[j].astype(f32)
        main.append(piece)
        parts = [piece[Y_EXT * xx : Y_EXT * (xx + 1), 96:128] for xx in range(X_SUB)]
        extra.append(jnp.concatenate(parts + [jnp.zeros((Y_EXT, C_SUB), f32)], axis=1))
    g = jnp.concatenate(main + extra, axis=0).astype(bf16)
    out[0:ROWS, :] = dot(table[...], g).astype(bf16)
    out[ROWS:, :] = jnp.zeros((2 * DEVS - ROWS, 128), bf16)


def bases_kernel(mode, bases, out):
    m = mode[0]

    def index(shape, axis):
        return lax.broadcasted_iota(jnp.int32, shape, axis)

    def pick(mask):
        return jnp.where(mask, 1.0, 0.0).astype(bf16)

    wave = index((NL, 1), 0)
    tile = lax.shift_right_logical(wave * 5462, 16)
    rows = pick(index((NL, LAT_DEV * 24), 1) == wave + 12 * tile)
    table = dot(rows, bases[...])
    table = jnp.where(index((NL, NLAT), 0) >= m, table, 0.0).astype(bf16)
    place = index((1, NLAT), 1)
    x = 12 * ((place >> 2) & 31) + X_SUB * (place & 3) + (place >> 7)
    columns = pick(index((NLAT, NLAT), 0) == x)
    out[0] = dot(table, columns).astype(bf16)
    place = index((NLAT, 1), 0)
    row = 24 * ((place >> 2) & 31) + 12 + X_SUB * (place & 3) + (place >> 7)
    rows = pick(index((NLAT, LAT_DEV * 24), 1) == row)
    table = dot(rows, bases[...])
    out[1] = jnp.where(index((NLAT, NL), 1) >= m, table, 0.0).astype(bf16)


def legendre_kernel(coeffs, tables, gain, out, rows):
    rows[...] = coeffs[...].astype(f32)
    packs = [rows[pl.ds(s, 128, stride=8), :] for s in range(2 * CG)]
    stack = []
    for xx in range(X_SUB):
        parts = [
            packs[2 * cg + r][:, C_SUB * xx : C_SUB * (xx + 1)] for r in range(2) for cg in range(CG)
        ]
        stack.append(jnp.concatenate(parts, axis=1))
    fourier = jnp.concatenate(stack, axis=0).astype(bf16)
    gains = jnp.concatenate([gain[...], gain[...]], axis=1)
    filtered = (dot(tables[0], fourier) * gains).astype(bf16)
    result = dot(tables[1], filtered)
    for cg in range(CG):
        for r in range(2):
            first = CHAN * r + C_SUB * cg
            parts = [result[128 * xx : 128 * (xx + 1), first : first + C_SUB] for xx in range(X_SUB)]
            parts.append(jnp.zeros((128, C_SUB), f32))
            rows[pl.ds(2 * cg + r, 128, stride=8), :] = jnp.concatenate(parts, axis=1)
    out[...] = rows[...].astype(bf16)


def inverse_kernel(coeffs, table, out):
    g = dot(table[...], coeffs[0:ROWS, :])
    for j in range(LON_DEV):
        main = g[Y_MAIN * j : Y_MAIN * (j + 1), 0:96]
        first = LON_DEV * Y_MAIN + Y_EXT * j
        extra = g[first : first + Y_EXT]
        parts = [extra[:, C_SUB * xx : C_SUB * (xx + 1)] for xx in range(X_SUB)]
        out[j] = jnp.concatenate([main, jnp.concatenate(parts, axis=0)], axis=1).astype(bf16)


def grid_kernel(pieces, out):
    for xg in range(XG):
        blocks = [pieces[CG * xg + cg].astype(f32) for cg in range(CG)]
        for xx in range(X_SUB):
            main = [b[:, C_SUB * xx : C_SUB * (xx + 1)] for b in blocks]
            extra = [b[Y_EXT * xx : Y_EXT * (xx + 1), 96:128] for b in blocks]
            out[X_SUB * xg + xx, 0:Y_MAIN, :] = jnp.concatenate(main, axis=1)
            out[X_SUB * xg + xx, Y_MAIN:, :] = jnp.concatenate(extra, axis=1)[0 : Y_DEV - Y_MAIN]


def call(kernel, shape, dtype, scratch=(), smem=0, space=pltpu.VMEM, flops=0, moved=0):
    def run(*args):
        specs = [
            pl.BlockSpec(memory_space=pltpu.SMEM if k < smem else space) for k in range(len(args))
        ]
        return pl.pallas_call(
            kernel,
            out_shape=jax.ShapeDtypeStruct(shape, dtype),
            in_specs=specs,
            out_specs=pl.BlockSpec(memory_space=pltpu.VMEM),
            scratch_shapes=list(scratch),
            compiler_params=pltpu.CompilerParams(vmem_limit_bytes=VMEM),
            cost_estimate=pl.CostEstimate(flops=flops, bytes_accessed=moved, transcendentals=0),
        )(*args)

    return run


def on_device(
    saved, cotangent, w_in, b_in, w_mid, b_mid, w_out, spectral_gain, basis_in, basis_out
):
    forward, back = zonal_tables()
    bases = jnp.concatenate(
        [jnp.transpose(basis_in, (1, 2, 0)), jnp.transpose(basis_out, (1, 0, 2))], axis=1
    )
    bases = jnp.pad(bases, ((0, LAT_DEV - M_DEV), (0, 0), (0, 0)))
    bases, saved = lax.optimization_barrier((bases, saved))
    bases = lax.all_to_all(bases, "lat", 0, 0, tiled=True)

    weights = (w_in, b_in.reshape(1, -1), w_mid, b_mid.reshape(1, -1), w_out)
    held = [pltpu.VMEM(a.shape, a.dtype) for a in (saved, cotangent) + weights]
    pad = pltpu.VMEM((X_DEV, Y_PAD, CHAN), bf16)
    pieces = call(
        network_kernel,
        (LON_DEV, Y_MAIN, 128),
        bf16,
        held + [pad, pad, pltpu.SemaphoreType.DMA((7,))],
        space=pltpu.HBM,
        flops=1_700_000_000,
        moved=4_000_000,
    )(saved, cotangent, *weights)
    bases, pieces = lax.optimization_barrier((bases, pieces))
    pieces = lax.all_to_all(pieces, "lon", 0, 0, tiled=True)
    mode = (M_DEV * lax.axis_index("lon") + lax.axis_index("lat")).astype(jnp.int32).reshape(1)
    tables = call(bases_kernel, (2, NL, NLAT), bf16, smem=1, flops=600_000_000, moved=3_000_000)(
        mode, bases.reshape(LAT_DEV * 24, NL)
    )
    coeffs = call(zonal_kernel, (2 * DEVS, 128), bf16, flops=300_000_000)(pieces, jnp.asarray(forward))
    coeffs = lax.all_to_all(coeffs.reshape(DEVS, 2, 128), ("lat", "lon"), 0, 0, tiled=True)
    coeffs = call(
        legendre_kernel,
        (2 * DEVS, 128),
        bf16,
        (pltpu.VMEM((2 * DEVS, 128), f32),),
        flops=200_000_000,
    )(coeffs.reshape(2 * DEVS, 128), tables, spectral_gain)
    coeffs = lax.all_to_all(coeffs.reshape(DEVS, 2, 128), ("lat", "lon"), 0, 0, tiled=True)
    pieces = call(inverse_kernel, (LON_DEV, Y_MAIN, 128), bf16, flops=300_000_000)(
        coeffs.reshape(2 * DEVS, 128), jnp.asarray(back)
    )
    pieces = lax.all_to_all(pieces, "lon", 0, 0, tiled=True)
    return call(grid_kernel, (X_DEV, Y_DEV, CHAN), f32)(pieces)


def solution(mesh):
    placed = (
        P("lat", "lon", None),
        P("lat", "lon", None),
        P(),
        P(),
        P(),
        P(),
        P(),
        P(),
        P(None, "lon", "lat"),
        P("lat", "lon", None),
    )
    return jax.shard_map(
        on_device, mesh=mesh, in_specs=placed, out_specs=P("lat", "lon", None), check_vma=False
    )
```

```python
import numpy as np
import jax
import jax.numpy as jnp
from jax import lax
from jax.experimental import pallas as pl
from jax.experimental.pallas import tpu as pltpu
from jax.sharding import PartitionSpec as P

bf16 = jnp.bfloat16
f32 = jnp.float32

LAT_DEV, LON_DEV = 32, 16
X_DEV, Y_DEV = 12, 90
Y_PAD = 96
Y_MAIN, Y_EXT = 72, 24
NLAT, NLON, NM, NL, CHAN = 384, 1440, 368, 384, 128
M_DEV = 23
X_SUB, C_SUB = 3, 32
CG = CHAN // C_SUB
XG = X_DEV // X_SUB
DEVS = LAT_DEV * LON_DEV
ROWS = 2 * NM
VMEM = 40 * 1024 * 1024
NETWORK_VMEM = 59 * 1024 * 1024


def zonal_tables():
    order = (M_DEV * np.arange(LON_DEV)[None, :] + np.arange(M_DEV)[:, None]).reshape(-1)
    turns = (order[:, None] * np.arange(NLON)[None, :]) % NLON
    angles = turns.astype(np.float64) * (2.0 * np.pi / NLON)
    table = np.stack([np.cos(angles), -np.sin(angles)], 1).reshape(ROWS, NLON)
    weight = np.where(order == 0, 1.0, 2.0) / NLON
    back = table * np.repeat(weight, 2)[:, None]

    def split_y(t):
        t = np.pad(t.reshape(ROWS, LON_DEV, Y_DEV), ((0, 0), (0, 0), (0, Y_PAD - Y_DEV)))
        main = t[:, :, :Y_MAIN].reshape(ROWS, LON_DEV * Y_MAIN)
        extra = t[:, :, Y_MAIN:].reshape(ROWS, LON_DEV * Y_EXT)
        return np.concatenate([main, extra], 1)

    return (
        np.asarray(split_y(table), dtype=jnp.bfloat16),
        np.ascontiguousarray(split_y(back).T).astype(jnp.bfloat16),
    )


def dot(a, b):
    return lax.dot_general(a, b, (((1,), (0,)), ((), ())), preferred_element_type=f32)


def dot_t(a, b):
    return lax.dot_general(a, b, (((1,), (1,)), ((), ())), preferred_element_type=f32)


def sigmoid(v):
    return 0.5 * jnp.tanh(0.5 * v) + 0.5


def network_kernel(
    saved_h, cotan_h, w_in_h, b_in_h, w_mid_h, b_mid_h, w_out_h, out,
    saved, cotan, w_in, b_in, w_mid, b_mid, w_out, rows_s, rows_c, sems,
):
    pairs = (
        (saved_h, saved), (w_in_h, w_in), (b_in_h, b_in), (w_mid_h, w_mid),
        (b_mid_h, b_mid), (cotan_h, cotan), (w_out_h, w_out),
    )
    copies = [pltpu.make_async_copy(a, b, sems.at[k]) for k, (a, b) in enumerate(pairs)]
    for copy in copies:
        copy.start()
    rows_s[...] = jnp.zeros_like(rows_s)
    rows_c[...] = jnp.zeros_like(rows_c)
    for copy in copies:
        copy.wait()
    for x in range(X_DEV):
        rows_s[x, 0:Y_DEV, :] = saved[x]
        rows_c[x, 0:Y_DEV, :] = cotan[x]
    for xg in range(XG):
        s = rows_s[X_SUB * xg : X_SUB * (xg + 1)].reshape(X_SUB * Y_PAD, CHAN)
        c = rows_c[X_SUB * xg : X_SUB * (xg + 1)].reshape(X_SUB * Y_PAD, CHAN)
        first = dot(s, w_in[...]) + b_in[...]
        sig = sigmoid(first)
        act = first * sig
        slope_one = sig + act * (1.0 - sig)
        second = dot(act.astype(bf16), w_mid[...]) + b_mid[...]
        sig = sigmoid(second)
        slope_two = sig * (1.0 + second * (1.0 - sig))
        back_two = (dot_t(c, w_out[...]) * slope_two).astype(bf16)
        back_one = (dot_t(back_two, w_mid[...]) * slope_one).astype(bf16)
        grad = c.astype(f32) + dot_t(back_one, w_in[...])
        grad = grad.reshape(X_SUB, Y_PAD, CHAN)
        for cg in range(CG):
            parts = [grad[xx][:, C_SUB * cg : C_SUB * (cg + 1)] for xx in range(X_SUB)]
            parts = [p[0:Y_MAIN] for p in parts] + [
                jnp.concatenate([p[Y_MAIN:] for p in parts], axis=0)
            ]
            out[CG * xg + cg] = jnp.concatenate(parts, axis=1).astype(bf16)


def zonal_kernel(circles, table, bases, out):
    main, extra = [], []
    for j in range(LON_DEV):
        piece = circles[j].astype(f32)
        main.append(piece)
        parts = [piece[Y_EXT * xx : Y_EXT * (xx + 1), 96:128] for xx in range(X_SUB)]
        extra.append(jnp.concatenate(parts + [jnp.zeros((Y_EXT, C_SUB), f32)], axis=1))
    g = jnp.concatenate(main + extra, axis=0).astype(bf16)
    spectrum = dot(table[...], g)
    for i in range(M_DEV):
        first = 2 * LON_DEV * i
        rest = spectrum[first + 24 : first + 32]
        parts = [rest[:, C_SUB * xx : C_SUB * (xx + 1)] for xx in range(X_SUB)]
        block = [spectrum[first : first + 24, 0:96], jnp.concatenate(parts, axis=0)]
        out[i, :, 0:128] = jnp.concatenate(block, axis=1).astype(bf16)
        out[i, :, 128:512] = bases[i]
    out[M_DEV:] = jnp.zeros((LAT_DEV - M_DEV, 24, 512), bf16)


def regroup_kernel(arrived, out, bases, rows):
    for i in range(LAT_DEV):
        block = arrived[i, :, 0:128].astype(f32)
        parts = [block[8 * xx : 8 * (xx + 1), 96:128] for xx in range(X_SUB)]
        rows[32 * i : 32 * i + 24, :] = block
        rows[32 * i + 24 : 32 * (i + 1), :] = jnp.concatenate(
            parts + [jnp.zeros((8, C_SUB), f32)], axis=1
        )
    for j in range(LON_DEV):
        real = rows[pl.ds(2 * j, LAT_DEV, stride=32), :]
        imag = rows[pl.ds(2 * j + 1, LAT_DEV, stride=32), :]
        parts = [imag[16:32, C_SUB * xx : C_SUB * (xx + 1)] for xx in range(X_SUB)]
        main = jnp.concatenate([real, imag[0:16]], axis=0)[:, 0:96]
        out[j] = jnp.concatenate([main, jnp.concatenate(parts, axis=0)], axis=1).astype(bf16)
    bases[...] = arrived[:, :, 128:512]


def bases_kernel(mode, bases, out):
    m = mode[0]

    def index(shape, axis):
        return lax.broadcasted_iota(jnp.int32, shape, axis)

    def pick(mask):
        return jnp.where(mask, 1.0, 0.0).astype(bf16)

    rows = bases[...].astype(f32).reshape(LAT_DEV * 24, NL).astype(bf16)
    wave = index((NL, 1), 0)
    tile = lax.shift_right_logical(wave * 5462, 16)
    chosen = pick(index((NL, LAT_DEV * 24), 1) == wave + 12 * tile)
    table = dot(chosen, rows)
    table = jnp.where(index((NL, NLAT), 0) >= m, table, 0.0).astype(bf16)
    place = index((1, NLAT), 1)
    x = 12 * (place & 31) + X_SUB * ((place >> 5) & 3) + (place >> 7)
    columns = pick(index((NLAT, NLAT), 0) == x)
    out[0] = dot(table, columns).astype(bf16)
    place = index((NLAT, 1), 0)
    row = 24 * (place & 31) + 12 + X_SUB * ((place >> 5) & 3) + (place >> 7)
    chosen = pick(index((NLAT, LAT_DEV * 24), 1) == row)
    table = dot(chosen, rows)
    out[1] = jnp.where(index((NLAT, NL), 1) >= m, table, 0.0).astype(bf16)


def legendre_kernel(coeffs, tables, gain, out, rows):
    blocks = []
    for j in range(LON_DEV):
        block = coeffs[j].astype(f32)
        parts = [block[16 * xx : 16 * (xx + 1), 96:128] for xx in range(X_SUB)]
        last = jnp.concatenate(parts + [jnp.zeros((16, C_SUB), f32)], axis=1)
        blocks.append((block[0:32], jnp.concatenate([block[32:48], last], axis=0)))
    stack = []
    for xx in range(X_SUB):
        for xg in range(XG):
            parts = [
                blocks[CG * xg + cg][r][:, C_SUB * xx : C_SUB * (xx + 1)]
                for r in range(2)
                for cg in range(CG)
            ]
            stack.append(jnp.concatenate(parts, axis=1))
    fourier = jnp.concatenate(stack, axis=0).astype(bf16)
    gains = jnp.concatenate([gain[...], gain[...]], axis=1)
    filtered = (dot(tables[0], fourier) * gains).astype(bf16)
    result = dot(tables[1], filtered)
    for xg in range(XG):
        for cg in range(CG):
            for r in range(2):
                first = CHAN * r + C_SUB * cg
                parts = [
                    result[32 * (XG * xx + xg) : 32 * (XG * xx + xg + 1), first : first + C_SUB]
                    for xx in range(X_SUB)
                ]
                parts.append(jnp.zeros((LAT_DEV, C_SUB), f32))
                place = 2 * (CG * xg + cg) + r
                rows[pl.ds(place, LAT_DEV, stride=32), :] = jnp.concatenate(parts, axis=1)
    out[...] = rows[...].astype(bf16)


def inverse_kernel(coeffs, table, out):
    g = dot(table[...], coeffs[0:ROWS, :])
    for j in range(LON_DEV):
        main = g[Y_MAIN * j : Y_MAIN * (j + 1), 0:96]
        first = LON_DEV * Y_MAIN + Y_EXT * j
        extra = g[first : first + Y_EXT]
        parts = [extra[:, C_SUB * xx : C_SUB * (xx + 1)] for xx in range(X_SUB)]
        out[j] = jnp.concatenate([main, jnp.concatenate(parts, axis=0)], axis=1).astype(bf16)


def grid_kernel(pieces, out):
    for xg in range(XG):
        blocks = [pieces[CG * xg + cg].astype(f32) for cg in range(CG)]
        for xx in range(X_SUB):
            main = [b[:, C_SUB * xx : C_SUB * (xx + 1)] for b in blocks]
            extra = [b[Y_EXT * xx : Y_EXT * (xx + 1), 96:128] for b in blocks]
            out[X_SUB * xg + xx, 0:Y_MAIN, :] = jnp.concatenate(main, axis=1)
            out[X_SUB * xg + xx, Y_MAIN:, :] = jnp.concatenate(extra, axis=1)[0 : Y_DEV - Y_MAIN]


def call(
    kernel, shape, dtype, scratch=(), smem=0, space=pltpu.VMEM, flops=0, moved=0, limit=VMEM
):
    outs = [jax.ShapeDtypeStruct(s, dtype) for s in (shape if isinstance(shape, list) else [shape])]
    places = [pl.BlockSpec(memory_space=pltpu.VMEM) for _ in outs]
    single = not isinstance(shape, list)

    def run(*args):
        specs = [
            pl.BlockSpec(memory_space=pltpu.SMEM if k < smem else space) for k in range(len(args))
        ]
        return pl.pallas_call(
            kernel,
            out_shape=outs[0] if single else outs,
            in_specs=specs,
            out_specs=places[0] if single else places,
            scratch_shapes=list(scratch),
            compiler_params=pltpu.CompilerParams(vmem_limit_bytes=limit),
            cost_estimate=pl.CostEstimate(flops=flops, bytes_accessed=moved, transcendentals=0),
        )(*args)

    return run


def on_device(
    saved, cotangent, w_in, b_in, w_mid, b_mid, w_out, spectral_gain, basis_in, basis_out
):
    forward, back = zonal_tables()
    weights = (w_in, b_in.reshape(1, -1), w_mid, b_mid.reshape(1, -1), w_out)
    held = [pltpu.VMEM(a.shape, a.dtype) for a in (saved, cotangent) + weights]
    pad = pltpu.VMEM((X_DEV, Y_PAD, CHAN), bf16)
    pieces = call(
        network_kernel,
        (LON_DEV, Y_MAIN, 128),
        bf16,
        held + [pad, pad, pltpu.SemaphoreType.DMA((7,))],
        space=pltpu.HBM,
        flops=1_700_000_000,
        moved=4_000_000,
        limit=NETWORK_VMEM,
    )(saved, cotangent, *weights)
    pieces = lax.all_to_all(pieces, "lon", 0, 0, tiled=True)
    bases = jnp.concatenate(
        [jnp.transpose(basis_in, (1, 2, 0)), jnp.transpose(basis_out, (1, 0, 2))], axis=1
    )
    coeffs = call(zonal_kernel, (LAT_DEV, 24, 512), bf16, flops=300_000_000)(
        pieces, jnp.asarray(forward), bases
    )
    coeffs = lax.all_to_all(coeffs, "lat", 0, 0, tiled=True)
    coeffs, bases = call(
        regroup_kernel,
        [(LON_DEV, 48, 128), (LAT_DEV, 24, NL)],
        bf16,
        (pltpu.VMEM((2 * DEVS, 128), f32),),
    )(coeffs)
    coeffs = lax.all_to_all(coeffs, "lon", 0, 0, tiled=True)
    mode = (M_DEV * lax.axis_index("lon") + lax.axis_index("lat")).astype(jnp.int32).reshape(1)
    tables = call(bases_kernel, (2, NL, NLAT), bf16, smem=1, flops=600_000_000, moved=3_000_000)(
        mode, bases
    )
    coeffs = call(
        legendre_kernel,
        (2 * DEVS, 128),
        bf16,
        (pltpu.VMEM((2 * DEVS, 128), f32),),
        flops=200_000_000,
    )(coeffs, tables, spectral_gain)
    coeffs = lax.all_to_all(coeffs.reshape(DEVS, 2, 128), ("lat", "lon"), 0, 0, tiled=True)
    pieces = call(inverse_kernel, (LON_DEV, Y_MAIN, 128), bf16, flops=300_000_000)(
        coeffs.reshape(2 * DEVS, 128), jnp.asarray(back)
    )
    pieces = lax.all_to_all(pieces, "lon", 0, 0, tiled=True)
    return call(grid_kernel, (X_DEV, Y_DEV, CHAN), f32)(pieces)


def solution(mesh):
    placed = (
        P("lat", "lon", None),
        P("lat", "lon", None),
        P(),
        P(),
        P(),
        P(),
        P(),
        P(),
        P(None, "lon", "lat"),
        P("lat", "lon", None),
    )
    return jax.shard_map(
        on_device, mesh=mesh, in_specs=placed, out_specs=P("lat", "lon", None), check_vma=False
    )
```

```python
import numpy as np
import jax
import jax.numpy as jnp
from jax import lax
from jax.experimental import pallas as pl
from jax.experimental.pallas import tpu as pltpu
from jax.sharding import PartitionSpec as P

bf16 = jnp.bfloat16
f32 = jnp.float32

LAT_DEV, LON_DEV = 32, 16
X_DEV, Y_DEV = 12, 90
Y_PAD = 96
Y_MAIN, Y_EXT = 72, 24
NLAT, NLON, NM, NL, CHAN = 384, 1440, 368, 384, 128
M_DEV = 23
X_SUB, C_SUB = 3, 32
CG = CHAN // C_SUB
XG = X_DEV // X_SUB
DEVS = LAT_DEV * LON_DEV
ROWS = 2 * NM
VMEM = 16 * 1024 * 1024
NETWORK_VMEM = 59 * 1024 * 1024


def zonal_tables():
    order = (M_DEV * np.arange(LON_DEV)[None, :] + np.arange(M_DEV)[:, None]).reshape(-1)
    turns = (order[:, None] * np.arange(NLON)[None, :]) % NLON
    angles = turns.astype(np.float64) * (2.0 * np.pi / NLON)
    table = np.stack([np.cos(angles), -np.sin(angles)], 1).reshape(ROWS, NLON)
    weight = np.where(order == 0, 1.0, 2.0) / NLON
    back = table * np.repeat(weight, 2)[:, None]

    def split_y(t):
        t = np.pad(t.reshape(ROWS, LON_DEV, Y_DEV), ((0, 0), (0, 0), (0, Y_PAD - Y_DEV)))
        main = t[:, :, :Y_MAIN].reshape(ROWS, LON_DEV * Y_MAIN)
        extra = t[:, :, Y_MAIN:].reshape(ROWS, LON_DEV * Y_EXT)
        return np.concatenate([main, extra], 1)

    return (
        np.asarray(split_y(table), dtype=jnp.bfloat16),
        np.ascontiguousarray(split_y(back).T).astype(jnp.bfloat16),
    )


def dot(a, b):
    return lax.dot_general(a, b, (((1,), (0,)), ((), ())), preferred_element_type=f32)


def dot_t(a, b):
    return lax.dot_general(a, b, (((1,), (1,)), ((), ())), preferred_element_type=f32)


def sigmoid(v):
    return 0.5 * jnp.tanh(0.5 * v) + 0.5


def network_kernel(
    saved_h, cotan_h, w_in_h, b_in_h, w_mid_h, b_mid_h, w_out_h, out,
    saved, cotan, w_in, b_in, w_mid, b_mid, w_out, rows_s, rows_c, sems,
):
    pairs = (
        (saved_h, saved), (w_in_h, w_in), (b_in_h, b_in), (w_mid_h, w_mid),
        (b_mid_h, b_mid), (cotan_h, cotan), (w_out_h, w_out),
    )
    copies = [pltpu.make_async_copy(a, b, sems.at[k]) for k, (a, b) in enumerate(pairs)]
    for copy in copies:
        copy.start()
    got = dict(zip(("saved", "w_in", "b_in", "w_mid", "b_mid", "cotan", "w_out"), copies))
    edge = jnp.zeros((X_DEV, 16, CHAN), bf16)
    rows_s[:, Y_PAD - 16 :, :] = edge
    rows_c[:, Y_PAD - 16 :, :] = edge
    got["saved"].wait()
    for x in range(X_DEV):
        rows_s[x, 0:Y_DEV, :] = saved[x]
    got["w_in"].wait()
    got["b_in"].wait()
    for xg in range(XG):
        s = rows_s[X_SUB * xg : X_SUB * (xg + 1)].reshape(X_SUB * Y_PAD, CHAN)
        first = dot(s, w_in[...]) + b_in[...]
        sig = sigmoid(first)
        act = first * sig
        slope_one = sig + act * (1.0 - sig)
        if xg == 0:
            got["w_mid"].wait()
            got["b_mid"].wait()
        second = dot(act.astype(bf16), w_mid[...]) + b_mid[...]
        sig = sigmoid(second)
        slope_two = sig * (1.0 + second * (1.0 - sig))
        if xg == 0:
            got["cotan"].wait()
            got["w_out"].wait()
            for x in range(X_DEV):
                rows_c[x, 0:Y_DEV, :] = cotan[x]
        c = rows_c[X_SUB * xg : X_SUB * (xg + 1)].reshape(X_SUB * Y_PAD, CHAN)
        back_two = (dot_t(c, w_out[...]) * slope_two).astype(bf16)
        back_one = (dot_t(back_two, w_mid[...]) * slope_one).astype(bf16)
        grad = c.astype(f32) + dot_t(back_one, w_in[...])
        grad = grad.reshape(X_SUB, Y_PAD, CHAN)
        for cg in range(CG):
            parts = [grad[xx][:, C_SUB * cg : C_SUB * (cg + 1)] for xx in range(X_SUB)]
            parts = [p[0:Y_MAIN] for p in parts] + [
                jnp.concatenate([p[Y_MAIN:] for p in parts], axis=0)
            ]
            out[CG * xg + cg] = jnp.concatenate(parts, axis=1).astype(bf16)


def zonal_kernel(circles, table, bases, out):
    main, extra = [], []
    for j in range(LON_DEV):
        piece = circles[j].astype(f32)
        main.append(piece)
        parts = [piece[Y_EXT * xx : Y_EXT * (xx + 1), 96:128] for xx in range(X_SUB)]
        extra.append(jnp.concatenate(parts + [jnp.zeros((Y_EXT, C_SUB), f32)], axis=1))
    g = jnp.concatenate(main + extra, axis=0).astype(bf16)
    spectrum = dot(table[...], g)
    for i in range(M_DEV):
        first = 2 * LON_DEV * i
        rest = spectrum[first + 24 : first + 32]
        parts = [rest[:, C_SUB * xx : C_SUB * (xx + 1)] for xx in range(X_SUB)]
        block = [spectrum[first : first + 24, 0:96], jnp.concatenate(parts, axis=0)]
        out[i, :, 0:128] = jnp.concatenate(block, axis=1).astype(bf16)
        out[i, :, 128:512] = bases[i]
    out[M_DEV:] = jnp.zeros((LAT_DEV - M_DEV, 24, 512), bf16)


def regroup_kernel(arrived, out, bases, rows):
    for i in range(LAT_DEV):
        block = arrived[i, :, 0:128].astype(f32)
        parts = [block[8 * xx : 8 * (xx + 1), 96:128] for xx in range(X_SUB)]
        rows[32 * i : 32 * i + 24, :] = block
        rows[32 * i + 24 : 32 * (i + 1), :] = jnp.concatenate(
            parts + [jnp.zeros((8, C_SUB), f32)], axis=1
        )
    for j in range(LON_DEV):
        real = rows[pl.ds(2 * j, LAT_DEV, stride=32), :]
        imag = rows[pl.ds(2 * j + 1, LAT_DEV, stride=32), :]
        parts = [imag[16:32, C_SUB * xx : C_SUB * (xx + 1)] for xx in range(X_SUB)]
        main = jnp.concatenate([real, imag[0:16]], axis=0)[:, 0:96]
        out[j] = jnp.concatenate([main, jnp.concatenate(parts, axis=0)], axis=1).astype(bf16)
    bases[...] = arrived[:, :, 128:512]


def bases_kernel(mode, bases, out):
    m = mode[0]

    def index(shape, axis):
        return lax.broadcasted_iota(jnp.int32, shape, axis)

    def pick(mask):
        return jnp.where(mask, 1.0, 0.0).astype(bf16)

    rows = bases[...].astype(f32).reshape(LAT_DEV * 24, NL).astype(bf16)
    wave = index((NL, 1), 0)
    tile = lax.shift_right_logical(wave * 5462, 16)
    chosen = pick(index((NL, LAT_DEV * 24), 1) == wave + 12 * tile)
    table = dot(chosen, rows)
    table = jnp.where(index((NL, NLAT), 0) >= m, table, 0.0).astype(bf16)
    place = index((1, NLAT), 1)
    x = 12 * (place & 31) + X_SUB * ((place >> 5) & 3) + (place >> 7)
    columns = pick(index((NLAT, NLAT), 0) == x)
    out[0] = dot(table, columns).astype(bf16)
    place = index((NLAT, 1), 0)
    row = 24 * (place & 31) + 12 + X_SUB * ((place >> 5) & 3) + (place >> 7)
    chosen = pick(index((NLAT, LAT_DEV * 24), 1) == row)
    table = dot(chosen, rows)
    out[1] = jnp.where(index((NLAT, NL), 1) >= m, table, 0.0).astype(bf16)


def legendre_kernel(coeffs, tables, gain, out, rows):
    blocks = []
    for j in range(LON_DEV):
        block = coeffs[j].astype(f32)
        parts = [block[16 * xx : 16 * (xx + 1), 96:128] for xx in range(X_SUB)]
        last = jnp.concatenate(parts + [jnp.zeros((16, C_SUB), f32)], axis=1)
        blocks.append((block[0:32], jnp.concatenate([block[32:48], last], axis=0)))
    stack = []
    for xx in range(X_SUB):
        for xg in range(XG):
            parts = [
                blocks[CG * xg + cg][r][:, C_SUB * xx : C_SUB * (xx + 1)]
                for r in range(2)
                for cg in range(CG)
            ]
            stack.append(jnp.concatenate(parts, axis=1))
    fourier = jnp.concatenate(stack, axis=0).astype(bf16)
    gains = jnp.concatenate([gain[...], gain[...]], axis=1)
    filtered = (dot(tables[0], fourier) * gains).astype(bf16)
    result = dot(tables[1], filtered)
    for xg in range(XG):
        for cg in range(CG):
            for r in range(2):
                first = CHAN * r + C_SUB * cg
                parts = [
                    result[32 * (XG * xx + xg) : 32 * (XG * xx + xg + 1), first : first + C_SUB]
                    for xx in range(X_SUB)
                ]
                parts.append(jnp.zeros((LAT_DEV, C_SUB), f32))
                place = 2 * (CG * xg + cg) + r
                rows[pl.ds(place, LAT_DEV, stride=32), :] = jnp.concatenate(parts, axis=1)
    out[...] = rows[...].astype(bf16)


def inverse_kernel(coeffs, table, out):
    g = dot(table[...], coeffs[0:ROWS, :])
    for j in range(LON_DEV):
        main = g[Y_MAIN * j : Y_MAIN * (j + 1), 0:96]
        first = LON_DEV * Y_MAIN + Y_EXT * j
        extra = g[first : first + Y_EXT]
        parts = [extra[:, C_SUB * xx : C_SUB * (xx + 1)] for xx in range(X_SUB)]
        out[j] = jnp.concatenate([main, jnp.concatenate(parts, axis=0)], axis=1).astype(bf16)


def grid_kernel(pieces, out):
    for xg in range(XG):
        blocks = [pieces[CG * xg + cg].astype(f32) for cg in range(CG)]
        for xx in range(X_SUB):
            main = [b[:, C_SUB * xx : C_SUB * (xx + 1)] for b in blocks]
            extra = [b[Y_EXT * xx : Y_EXT * (xx + 1), 96:128] for b in blocks]
            out[X_SUB * xg + xx, 0:Y_MAIN, :] = jnp.concatenate(main, axis=1)
            out[X_SUB * xg + xx, Y_MAIN:, :] = jnp.concatenate(extra, axis=1)[0 : Y_DEV - Y_MAIN]


def call(
    kernel, shape, dtype, scratch=(), smem=0, space=pltpu.VMEM, flops=0, moved=0, limit=VMEM
):
    outs = [jax.ShapeDtypeStruct(s, dtype) for s in (shape if isinstance(shape, list) else [shape])]
    places = [pl.BlockSpec(memory_space=pltpu.VMEM) for _ in outs]
    single = not isinstance(shape, list)

    def run(*args):
        specs = [
            pl.BlockSpec(memory_space=pltpu.SMEM if k < smem else space) for k in range(len(args))
        ]
        return pl.pallas_call(
            kernel,
            out_shape=outs[0] if single else outs,
            in_specs=specs,
            out_specs=places[0] if single else places,
            scratch_shapes=list(scratch),
            compiler_params=pltpu.CompilerParams(vmem_limit_bytes=limit),
            cost_estimate=pl.CostEstimate(flops=flops, bytes_accessed=moved, transcendentals=0),
        )(*args)

    return run


def on_device(
    saved, cotangent, w_in, b_in, w_mid, b_mid, w_out, spectral_gain, basis_in, basis_out
):
    forward, back = zonal_tables()
    weights = (w_in, b_in.reshape(1, -1), w_mid, b_mid.reshape(1, -1), w_out)
    held = [pltpu.VMEM(a.shape, a.dtype) for a in (saved, cotangent) + weights]
    pad = pltpu.VMEM((X_DEV, Y_PAD, CHAN), bf16)
    pieces = call(
        network_kernel,
        (LON_DEV, Y_MAIN, 128),
        bf16,
        held + [pad, pad, pltpu.SemaphoreType.DMA((7,))],
        space=pltpu.HBM,
        flops=1_700_000_000,
        moved=4_000_000,
        limit=NETWORK_VMEM,
    )(saved, cotangent, *weights)
    pieces = lax.all_to_all(pieces, "lon", 0, 0, tiled=True)
    bases = jnp.concatenate(
        [jnp.transpose(basis_in, (1, 2, 0)), jnp.transpose(basis_out, (1, 0, 2))], axis=1
    )
    coeffs = call(zonal_kernel, (LAT_DEV, 24, 512), bf16, flops=300_000_000)(
        pieces, jnp.asarray(forward), bases
    )
    coeffs = lax.all_to_all(coeffs, "lat", 0, 0, tiled=True)
    coeffs, bases = call(
        regroup_kernel,
        [(LON_DEV, 48, 128), (LAT_DEV, 24, NL)],
        bf16,
        (pltpu.VMEM((2 * DEVS, 128), f32),),
    )(coeffs)
    coeffs = lax.all_to_all(coeffs, "lon", 0, 0, tiled=True)
    mode = (M_DEV * lax.axis_index("lon") + lax.axis_index("lat")).astype(jnp.int32).reshape(1)
    tables = call(bases_kernel, (2, NL, NLAT), bf16, smem=1, flops=600_000_000, moved=3_000_000)(
        mode, bases
    )
    coeffs = call(
        legendre_kernel,
        (2 * DEVS, 128),
        bf16,
        (pltpu.VMEM((2 * DEVS, 128), f32),),
        flops=200_000_000,
    )(coeffs, tables, spectral_gain)
    coeffs = lax.all_to_all(coeffs.reshape(DEVS, 2, 128), ("lat", "lon"), 0, 0, tiled=True)
    pieces = call(inverse_kernel, (LON_DEV, Y_MAIN, 128), bf16, flops=300_000_000)(
        coeffs.reshape(2 * DEVS, 128), jnp.asarray(back)
    )
    pieces = lax.all_to_all(pieces, "lon", 0, 0, tiled=True)
    return call(grid_kernel, (X_DEV, Y_DEV, CHAN), f32)(pieces)


def solution(mesh):
    placed = (
        P("lat", "lon", None),
        P("lat", "lon", None),
        P(),
        P(),
        P(),
        P(),
        P(),
        P(),
        P(None, "lon", "lat"),
        P("lat", "lon", None),
    )
    return jax.shard_map(
        on_device, mesh=mesh, in_specs=placed, out_specs=P("lat", "lon", None), check_vma=False
    )
```

```python
import numpy as np
import jax
import jax.numpy as jnp
from jax import lax
from jax.experimental import pallas as pl
from jax.experimental.pallas import tpu as pltpu
from jax.sharding import Mesh, PartitionSpec as P

bf16 = jnp.bfloat16
f32 = jnp.float32

LAT_DEV, LON_DEV = 32, 16
PAIRS = LON_DEV // 2
X_DEV, Y_DEV = 12, 90
Y_PAD = 96
Y_MAIN, Y_EXT = 72, 24
NLAT, NLON, NM, NL, CHAN = 384, 1440, 368, 384, 128
M_DEV = 23
X_SUB, C_SUB = 3, 32
CG = CHAN // C_SUB
XG = X_DEV // X_SUB
DEVS = LAT_DEV * LON_DEV
ROWS = 2 * NM
LON = ("pair", "core")
VMEM = 16 * 1024 * 1024
NETWORK_VMEM = 59 * 1024 * 1024


def zonal_tables():
    order = (M_DEV * np.arange(LON_DEV)[None, :] + np.arange(M_DEV)[:, None]).reshape(-1)
    turns = (order[:, None] * np.arange(NLON)[None, :]) % NLON
    angles = turns.astype(np.float64) * (2.0 * np.pi / NLON)
    table = np.stack([np.cos(angles), -np.sin(angles)], 1).reshape(ROWS, NLON)
    weight = np.where(order == 0, 1.0, 2.0) / NLON
    back = table * np.repeat(weight, 2)[:, None]

    def split_y(t):
        t = np.pad(t.reshape(ROWS, LON_DEV, Y_DEV), ((0, 0), (0, 0), (0, Y_PAD - Y_DEV)))
        main = t[:, :, :Y_MAIN].reshape(ROWS, LON_DEV * Y_MAIN)
        extra = t[:, :, Y_MAIN:].reshape(ROWS, LON_DEV * Y_EXT)
        return np.concatenate([main, extra], 1)

    return (
        np.asarray(split_y(table), dtype=jnp.bfloat16),
        np.ascontiguousarray(split_y(back).T).astype(jnp.bfloat16),
    )


def owner(xg, cg):
    return CG * xg + 2 * (cg % 2) + cg // 2


def dot(a, b):
    return lax.dot_general(a, b, (((1,), (0,)), ((), ())), preferred_element_type=f32)


def dot_t(a, b):
    return lax.dot_general(a, b, (((1,), (1,)), ((), ())), preferred_element_type=f32)


def sigmoid(v):
    return 0.5 * jnp.tanh(0.5 * v) + 0.5


def network_kernel(
    saved_h, cotan_h, w_in_h, b_in_h, w_mid_h, b_mid_h, w_out_h, out,
    saved, cotan, w_in, b_in, w_mid, b_mid, w_out, rows_s, rows_c, sems,
):
    pairs = (
        (saved_h, saved), (w_in_h, w_in), (b_in_h, b_in), (w_mid_h, w_mid),
        (b_mid_h, b_mid), (cotan_h, cotan), (w_out_h, w_out),
    )
    copies = [pltpu.make_async_copy(a, b, sems.at[k]) for k, (a, b) in enumerate(pairs)]
    for copy in copies:
        copy.start()
    got = dict(zip(("saved", "w_in", "b_in", "w_mid", "b_mid", "cotan", "w_out"), copies))
    edge = jnp.zeros((X_DEV, 16, CHAN), bf16)
    rows_s[:, Y_PAD - 16 :, :] = edge
    rows_c[:, Y_PAD - 16 :, :] = edge
    got["saved"].wait()
    for x in range(X_DEV):
        rows_s[x, 0:Y_DEV, :] = saved[x]
    got["w_in"].wait()
    got["b_in"].wait()
    for xg in range(XG):
        s = rows_s[X_SUB * xg : X_SUB * (xg + 1)].reshape(X_SUB * Y_PAD, CHAN)
        first = dot(s, w_in[...]) + b_in[...]
        sig = sigmoid(first)
        act = first * sig
        slope_one = sig + act * (1.0 - sig)
        if xg == 0:
            got["w_mid"].wait()
            got["b_mid"].wait()
        second = dot(act.astype(bf16), w_mid[...]) + b_mid[...]
        sig = sigmoid(second)
        slope_two = sig * (1.0 + second * (1.0 - sig))
        if xg == 0:
            got["cotan"].wait()
            got["w_out"].wait()
            for x in range(X_DEV):
                rows_c[x, 0:Y_DEV, :] = cotan[x]
        c = rows_c[X_SUB * xg : X_SUB * (xg + 1)].reshape(X_SUB * Y_PAD, CHAN)
        back_two = (dot_t(c, w_out[...]) * slope_two).astype(bf16)
        back_one = (dot_t(back_two, w_mid[...]) * slope_one).astype(bf16)
        grad = c.astype(f32) + dot_t(back_one, w_in[...])
        grad = grad.reshape(X_SUB, Y_PAD, CHAN)
        for cg in range(CG):
            parts = [grad[xx][:, C_SUB * cg : C_SUB * (cg + 1)] for xx in range(X_SUB)]
            parts = [p[0:Y_MAIN] for p in parts] + [
                jnp.concatenate([p[Y_MAIN:] for p in parts], axis=0)
            ]
            out[owner(xg, cg)] = jnp.concatenate(parts, axis=1).astype(bf16)


def zonal_kernel(circles, table, bases, out):
    main, extra = [], []
    for j in range(LON_DEV):
        piece = circles[j].astype(f32)
        main.append(piece)
        parts = [piece[Y_EXT * xx : Y_EXT * (xx + 1), 96:128] for xx in range(X_SUB)]
        extra.append(jnp.concatenate(parts + [jnp.zeros((Y_EXT, C_SUB), f32)], axis=1))
    g = jnp.concatenate(main + extra, axis=0).astype(bf16)
    spectrum = dot(table[...], g)
    for i in range(M_DEV):
        first = 2 * LON_DEV * i
        rest = spectrum[first + 24 : first + 32]
        parts = [rest[:, C_SUB * xx : C_SUB * (xx + 1)] for xx in range(X_SUB)]
        block = [spectrum[first : first + 24, 0:96], jnp.concatenate(parts, axis=0)]
        out[i, :, 0:128] = jnp.concatenate(block, axis=1).astype(bf16)
        out[i, :, 128:512] = bases[i]
    out[M_DEV:] = jnp.zeros((LAT_DEV - M_DEV, 24, 512), bf16)


def regroup_kernel(arrived, out, bases, rows):
    for i in range(LAT_DEV):
        block = arrived[i, :, 0:128].astype(f32)
        parts = [block[8 * xx : 8 * (xx + 1), 96:128] for xx in range(X_SUB)]
        rows[32 * i : 32 * i + 24, :] = block
        rows[32 * i + 24 : 32 * (i + 1), :] = jnp.concatenate(
            parts + [jnp.zeros((8, C_SUB), f32)], axis=1
        )
    for k in range(PAIRS):
        quarter = [rows[pl.ds(4 * k + n, LAT_DEV, stride=32), :] for n in range(4)]
        parts = [quarter[3][:, C_SUB * xx : C_SUB * (xx + 1)] for xx in range(X_SUB)]
        main = jnp.concatenate(quarter[0:3], axis=0)[:, 0:96]
        out[k] = jnp.concatenate([main, jnp.concatenate(parts, axis=0)], axis=1).astype(bf16)
    bases[...] = arrived[:, :, 128:512]


def bases_kernel(place, bases, out):
    m = place[0]

    def index(shape, axis):
        return lax.broadcasted_iota(jnp.int32, shape, axis)

    def pick(mask):
        return jnp.where(mask, 1.0, 0.0).astype(bf16)

    rows = bases[...].astype(f32).reshape(LAT_DEV * 24, NL).astype(bf16)
    wave = index((NL, 1), 0)
    tile = lax.shift_right_logical(wave * 5462, 16)
    chosen = pick(index((NL, LAT_DEV * 24), 1) == wave + 12 * tile)
    table = dot(chosen, rows)
    table = jnp.where(index((NL, NLAT), 0) >= m, table, 0.0).astype(bf16)
    spot = index((1, NLAT), 1)
    x = 12 * (spot & 31) + X_SUB * ((spot >> 5) & 3) + (spot >> 7)
    columns = pick(index((NLAT, NLAT), 0) == x)
    out[0] = dot(table, columns).astype(bf16)
    spot = index((NLAT, 1), 0)
    row = 24 * (spot & 31) + 12 + X_SUB * ((spot >> 5) & 3) + (spot >> 7)
    chosen = pick(index((NLAT, LAT_DEV * 24), 1) == row)
    table = dot(chosen, rows)
    out[1] = jnp.where(index((NLAT, NL), 1) >= m, table, 0.0).astype(bf16)


def legendre_kernel(place, coeffs, tables, others, gain, out, rows):
    core = place[1]

    def swapped(pair):
        return jnp.where(core == 0, pair[0], pair[1]), jnp.where(core == 0, pair[1], pair[0])

    blocks = []
    for k in range(PAIRS):
        block = coeffs[k].astype(f32)
        parts = [block[32 * xx : 32 * (xx + 1), 96:128] for xx in range(X_SUB)]
        last = jnp.concatenate(parts + [jnp.zeros((32, C_SUB), f32)], axis=1)
        blocks.append([block[0:32], block[32:64], block[64:96], last])
    modes = []
    for h in range(2):
        stack = []
        for xx in range(X_SUB):
            for xg in range(XG):
                parts = [
                    blocks[2 * xg + cq][2 * h + r][:, C_SUB * xx : C_SUB * (xx + 1)]
                    for r in range(2)
                    for cq in range(2)
                ]
                stack.append(jnp.concatenate(parts, axis=1))
        modes.append(jnp.concatenate(stack, axis=0))
    half = jnp.where(core == 0, gain[:, 0:64], gain[:, 64:128])
    gains = jnp.concatenate([half, half], axis=1)
    results = []
    for fourier, table in zip(swapped(modes), (tables, others)):
        filtered = (dot(table[0], fourier.astype(bf16)) * gains).astype(bf16)
        results.append(dot(table[1], filtered))
    results = swapped(results)
    for k in range(PAIRS):
        xg, cq = k // 2, k % 2
        for h in range(2):
            for r in range(2):
                first = 64 * r + C_SUB * cq
                parts = [
                    results[h][32 * (XG * xx + xg) : 32 * (XG * xx + xg + 1), first : first + C_SUB]
                    for xx in range(X_SUB)
                ]
                parts.append(jnp.zeros((LAT_DEV, C_SUB), f32))
                rows[pl.ds(4 * k + 2 * h + r, LAT_DEV, stride=32), :] = jnp.concatenate(parts, axis=1)
    out[...] = rows[...].astype(bf16)


def inverse_kernel(coeffs, table, out):
    g = dot(table[...], coeffs[0:ROWS, :])
    for j in range(LON_DEV):
        main = g[Y_MAIN * j : Y_MAIN * (j + 1), 0:96]
        first = LON_DEV * Y_MAIN + Y_EXT * j
        extra = g[first : first + Y_EXT]
        parts = [extra[:, C_SUB * xx : C_SUB * (xx + 1)] for xx in range(X_SUB)]
        out[j] = jnp.concatenate([main, jnp.concatenate(parts, axis=0)], axis=1).astype(bf16)


def grid_kernel(pieces, out):
    for xg in range(XG):
        blocks = [pieces[owner(xg, cg)].astype(f32) for cg in range(CG)]
        for xx in range(X_SUB):
            main = [b[:, C_SUB * xx : C_SUB * (xx + 1)] for b in blocks]
            extra = [b[Y_EXT * xx : Y_EXT * (xx + 1), 96:128] for b in blocks]
            out[X_SUB * xg + xx, 0:Y_MAIN, :] = jnp.concatenate(main, axis=1)
            out[X_SUB * xg + xx, Y_MAIN:, :] = jnp.concatenate(extra, axis=1)[0 : Y_DEV - Y_MAIN]


def call(
    kernel, shape, dtype, scratch=(), smem=0, space=pltpu.VMEM, flops=0, moved=0, limit=VMEM
):
    outs = [jax.ShapeDtypeStruct(s, dtype) for s in (shape if isinstance(shape, list) else [shape])]
    places = [pl.BlockSpec(memory_space=pltpu.VMEM) for _ in outs]
    single = not isinstance(shape, list)

    def run(*args):
        specs = [
            pl.BlockSpec(memory_space=pltpu.SMEM if k < smem else space) for k in range(len(args))
        ]
        return pl.pallas_call(
            kernel,
            out_shape=outs[0] if single else outs,
            in_specs=specs,
            out_specs=places[0] if single else places,
            scratch_shapes=list(scratch),
            compiler_params=pltpu.CompilerParams(vmem_limit_bytes=limit),
            cost_estimate=pl.CostEstimate(flops=flops, bytes_accessed=moved, transcendentals=0),
        )(*args)

    return run


def on_device(
    saved, cotangent, w_in, b_in, w_mid, b_mid, w_out, spectral_gain, basis_in, basis_out
):
    forward, back = zonal_tables()
    weights = (w_in, b_in.reshape(1, -1), w_mid, b_mid.reshape(1, -1), w_out)
    held = [pltpu.VMEM(a.shape, a.dtype) for a in (saved, cotangent) + weights]
    pad = pltpu.VMEM((X_DEV, Y_PAD, CHAN), bf16)
    pieces = call(
        network_kernel,
        (LON_DEV, Y_MAIN, 128),
        bf16,
        held + [pad, pad, pltpu.SemaphoreType.DMA((7,))],
        space=pltpu.HBM,
        flops=1_700_000_000,
        moved=4_000_000,
        limit=NETWORK_VMEM,
    )(saved, cotangent, *weights)
    pieces = lax.all_to_all(pieces, LON, 0, 0, tiled=True)
    bases = jnp.concatenate(
        [jnp.transpose(basis_in, (1, 2, 0)), jnp.transpose(basis_out, (1, 0, 2))], axis=1
    )
    coeffs = call(zonal_kernel, (LAT_DEV, 24, 512), bf16, flops=300_000_000)(
        pieces, jnp.asarray(forward), bases
    )
    coeffs = lax.all_to_all(coeffs, "lat", 0, 0, tiled=True)
    coeffs, bases = call(
        regroup_kernel,
        [(PAIRS, 96, 128), (LAT_DEV, 24, NL)],
        bf16,
        (pltpu.VMEM((2 * DEVS, 128), f32),),
    )(coeffs)
    coeffs = lax.all_to_all(coeffs, "pair", 0, 0, tiled=True)
    mode = M_DEV * lax.axis_index(LON) + lax.axis_index("lat")
    place = jnp.stack([mode, lax.axis_index("core")]).astype(jnp.int32)
    tables = call(bases_kernel, (2, NL, NLAT), bf16, smem=1, flops=600_000_000, moved=3_000_000)(
        place, bases
    )
    others = lax.ppermute(tables, "core", [(0, 1), (1, 0)])
    coeffs = call(
        legendre_kernel,
        (2 * DEVS, 128),
        bf16,
        (pltpu.VMEM((2 * DEVS, 128), f32),),
        smem=1,
        flops=200_000_000,
    )(place, coeffs, tables, others, spectral_gain)
    coeffs = lax.all_to_all(coeffs.reshape(DEVS // 2, 4, 128), ("lat", "pair"), 0, 0, tiled=True)
    pieces = call(inverse_kernel, (LON_DEV, Y_MAIN, 128), bf16, flops=300_000_000)(
        coeffs.reshape(2 * DEVS, 128), jnp.asarray(back)
    )
    pieces = lax.all_to_all(pieces, LON, 0, 0, tiled=True)
    return call(grid_kernel, (X_DEV, Y_DEV, CHAN), f32)(pieces)


def solution(mesh):
    grid = P("lat", LON, None)
    placed = (grid, grid, P(), P(), P(), P(), P(), P(), P(None, LON, "lat"), grid)
    fine = Mesh(mesh.devices.reshape(LAT_DEV, PAIRS, 2), ("lat",) + LON)
    return jax.shard_map(on_device, mesh=fine, in_specs=placed, out_specs=grid, check_vma=False)
```

```python
import numpy as np
import jax
import jax.numpy as jnp
from jax import lax
from jax.experimental import pallas as pl
from jax.experimental.pallas import tpu as pltpu
from jax.sharding import Mesh, PartitionSpec as P

bf16 = jnp.bfloat16
f32 = jnp.float32

LAT_DEV, LON_DEV = 32, 16
PAIRS = LON_DEV // 2
X_DEV, Y_DEV = 12, 90
Y_PAD = 96
Y_MAIN, Y_EXT = 72, 24
NLAT, NLON, NM, NL, CHAN = 384, 1440, 368, 384, 128
M_DEV = 23
X_SUB, C_SUB = 3, 32
CG = CHAN // C_SUB
XG = X_DEV // X_SUB
DEVS = LAT_DEV * LON_DEV
ROWS = 2 * NM
LON = ("pair", "core")
VMEM = 16 * 1024 * 1024
NETWORK_VMEM = 59 * 1024 * 1024


def zonal_tables():
    order = (M_DEV * np.arange(LON_DEV)[None, :] + np.arange(M_DEV)[:, None]).reshape(-1)
    turns = (order[:, None] * np.arange(NLON)[None, :]) % NLON
    angles = turns.astype(np.float64) * (2.0 * np.pi / NLON)
    table = np.stack([np.cos(angles), -np.sin(angles)], 1).reshape(ROWS, NLON)
    weight = np.where(order == 0, 1.0, 2.0) / NLON
    back = table * np.repeat(weight, 2)[:, None]

    def split_y(t):
        t = np.pad(t.reshape(ROWS, LON_DEV, Y_DEV), ((0, 0), (0, 0), (0, Y_PAD - Y_DEV)))
        main = t[:, :, :Y_MAIN].reshape(ROWS, LON_DEV * Y_MAIN)
        extra = t[:, :, Y_MAIN:].reshape(ROWS, LON_DEV * Y_EXT)
        return np.concatenate([main, extra], 1)

    return (
        np.asarray(split_y(table), dtype=jnp.bfloat16),
        np.ascontiguousarray(split_y(back).T).astype(jnp.bfloat16),
    )


def owner(xg, cg):
    return CG * xg + 2 * (cg % 2) + cg // 2


def dot(a, b):
    return lax.dot_general(a, b, (((1,), (0,)), ((), ())), preferred_element_type=f32)


def dot_t(a, b):
    return lax.dot_general(a, b, (((1,), (1,)), ((), ())), preferred_element_type=f32)


def sigmoid(v):
    return 0.5 * jnp.tanh(0.5 * v) + 0.5


def network_kernel(
    saved_h, cotan_h, w_in_h, b_in_h, w_mid_h, b_mid_h, w_out_h, out,
    saved, cotan, w_in, b_in, w_mid, b_mid, w_out, rows_s, rows_c, sems,
):
    pairs = (
        (saved_h, saved), (w_in_h, w_in), (b_in_h, b_in), (w_mid_h, w_mid),
        (b_mid_h, b_mid), (cotan_h, cotan), (w_out_h, w_out),
    )
    copies = [pltpu.make_async_copy(a, b, sems.at[k]) for k, (a, b) in enumerate(pairs)]
    for copy in copies:
        copy.start()
    got = dict(zip(("saved", "w_in", "b_in", "w_mid", "b_mid", "cotan", "w_out"), copies))
    edge = jnp.zeros((X_DEV, 16, CHAN), bf16)
    rows_s[:, Y_PAD - 16 :, :] = edge
    rows_c[:, Y_PAD - 16 :, :] = edge
    got["saved"].wait()
    for x in range(X_DEV):
        rows_s[x, 0:Y_DEV, :] = saved[x]
    got["w_in"].wait()
    got["b_in"].wait()
    for xg in range(XG):
        s = rows_s[X_SUB * xg : X_SUB * (xg + 1)].reshape(X_SUB * Y_PAD, CHAN)
        first = dot(s, w_in[...]) + b_in[...]
        sig = sigmoid(first)
        act = first * sig
        slope_one = sig + act * (1.0 - sig)
        if xg == 0:
            got["w_mid"].wait()
            got["b_mid"].wait()
        second = dot(act.astype(bf16), w_mid[...]) + b_mid[...]
        sig = sigmoid(second)
        slope_two = sig * (1.0 + second * (1.0 - sig))
        if xg == 0:
            got["cotan"].wait()
            got["w_out"].wait()
            for x in range(X_DEV):
                rows_c[x, 0:Y_DEV, :] = cotan[x]
        c = rows_c[X_SUB * xg : X_SUB * (xg + 1)].reshape(X_SUB * Y_PAD, CHAN)
        back_two = (dot_t(c, w_out[...]) * slope_two).astype(bf16)
        back_one = (dot_t(back_two, w_mid[...]) * slope_one).astype(bf16)
        grad = c.astype(f32) + dot_t(back_one, w_in[...])
        grad = grad.reshape(X_SUB, Y_PAD, CHAN)
        for cg in range(CG):
            parts = [grad[xx][:, C_SUB * cg : C_SUB * (cg + 1)] for xx in range(X_SUB)]
            parts = [p[0:Y_MAIN] for p in parts] + [
                jnp.concatenate([p[Y_MAIN:] for p in parts], axis=0)
            ]
            out[owner(xg, cg)] = jnp.concatenate(parts, axis=1).astype(bf16)


def zonal_kernel(circles, table, out):
    main, extra = [], []
    for j in range(LON_DEV):
        piece = circles[j].astype(f32)
        main.append(piece)
        parts = [piece[Y_EXT * xx : Y_EXT * (xx + 1), 96:128] for xx in range(X_SUB)]
        extra.append(jnp.concatenate(parts + [jnp.zeros((Y_EXT, C_SUB), f32)], axis=1))
    g = jnp.concatenate(main + extra, axis=0).astype(bf16)
    out[0:ROWS, :] = dot(table[...], g).astype(bf16)
    out[ROWS:, :] = jnp.zeros((2 * DEVS - ROWS, 128), bf16)


def bases_kernel(place, bases, out):
    m = place[0]

    def index(shape, axis):
        return lax.broadcasted_iota(jnp.int32, shape, axis)

    def pick(mask):
        return jnp.where(mask, 1.0, 0.0).astype(bf16)

    rows = bases[...].astype(f32).reshape(LAT_DEV * 24, NL).astype(bf16)
    wave = index((NL, 1), 0)
    tile = lax.shift_right_logical(wave * 5462, 16)
    chosen = pick(index((NL, LAT_DEV * 24), 1) == wave + 12 * tile)
    table = dot(chosen, rows)
    table = jnp.where(index((NL, NLAT), 0) >= m, table, 0.0).astype(bf16)
    spot = index((1, NLAT), 1)
    x = 12 * (spot & 31) + X_SUB * ((spot >> 5) & 3) + (spot >> 7)
    columns = pick(index((NLAT, NLAT), 0) == x)
    out[0] = dot(table, columns).astype(bf16)
    spot = index((NLAT, 1), 0)
    row = 24 * (spot & 31) + 12 + X_SUB * ((spot >> 5) & 3) + (spot >> 7)
    chosen = pick(index((NLAT, LAT_DEV * 24), 1) == row)
    table = dot(chosen, rows)
    out[1] = jnp.where(index((NLAT, NL), 1) >= m, table, 0.0).astype(bf16)


def legendre_kernel(place, coeffs, tables, others, gain, out, rows):
    core = place[1]

    def swapped(pair):
        return jnp.where(core == 0, pair[0], pair[1]), jnp.where(core == 0, pair[1], pair[0])

    rows[...] = coeffs[...].astype(f32)
    blocks = [
        [rows[pl.ds(4 * k + n, LAT_DEV, stride=32), :] for n in range(4)] for k in range(PAIRS)
    ]
    modes = []
    for h in range(2):
        stack = []
        for xx in range(X_SUB):
            for xg in range(XG):
                parts = [
                    blocks[2 * xg + cq][2 * h + r][:, C_SUB * xx : C_SUB * (xx + 1)]
                    for r in range(2)
                    for cq in range(2)
                ]
                stack.append(jnp.concatenate(parts, axis=1))
        modes.append(jnp.concatenate(stack, axis=0))
    half = jnp.where(core == 0, gain[:, 0:64], gain[:, 64:128])
    gains = jnp.concatenate([half, half], axis=1)
    results = []
    for fourier, table in zip(swapped(modes), (tables, others)):
        filtered = (dot(table[0], fourier.astype(bf16)) * gains).astype(bf16)
        results.append(dot(table[1], filtered))
    results = swapped(results)
    for k in range(PAIRS):
        xg, cq = k // 2, k % 2
        for h in range(2):
            for r in range(2):
                first = 64 * r + C_SUB * cq
                parts = [
                    results[h][32 * (XG * xx + xg) : 32 * (XG * xx + xg + 1), first : first + C_SUB]
                    for xx in range(X_SUB)
                ]
                parts.append(jnp.zeros((LAT_DEV, C_SUB), f32))
                rows[pl.ds(4 * k + 2 * h + r, LAT_DEV, stride=32), :] = jnp.concatenate(parts, axis=1)
    out[...] = rows[...].astype(bf16)


def inverse_kernel(coeffs, table, out):
    g = dot(table[...], coeffs[0:ROWS, :])
    for j in range(LON_DEV):
        main = g[Y_MAIN * j : Y_MAIN * (j + 1), 0:96]
        first = LON_DEV * Y_MAIN + Y_EXT * j
        extra = g[first : first + Y_EXT]
        parts = [extra[:, C_SUB * xx : C_SUB * (xx + 1)] for xx in range(X_SUB)]
        out[j] = jnp.concatenate([main, jnp.concatenate(parts, axis=0)], axis=1).astype(bf16)


def grid_kernel(pieces, out):
    for xg in range(XG):
        blocks = [pieces[owner(xg, cg)].astype(f32) for cg in range(CG)]
        for xx in range(X_SUB):
            main = [b[:, C_SUB * xx : C_SUB * (xx + 1)] for b in blocks]
            extra = [b[Y_EXT * xx : Y_EXT * (xx + 1), 96:128] for b in blocks]
            out[X_SUB * xg + xx, 0:Y_MAIN, :] = jnp.concatenate(main, axis=1)
            out[X_SUB * xg + xx, Y_MAIN:, :] = jnp.concatenate(extra, axis=1)[0 : Y_DEV - Y_MAIN]


def call(
    kernel, shape, dtype, scratch=(), smem=0, space=pltpu.VMEM, flops=0, moved=0, limit=VMEM
):
    outs = [jax.ShapeDtypeStruct(s, dtype) for s in (shape if isinstance(shape, list) else [shape])]
    places = [pl.BlockSpec(memory_space=pltpu.VMEM) for _ in outs]
    single = not isinstance(shape, list)

    def run(*args):
        specs = [
            pl.BlockSpec(memory_space=pltpu.SMEM if k < smem else space) for k in range(len(args))
        ]
        return pl.pallas_call(
            kernel,
            out_shape=outs[0] if single else outs,
            in_specs=specs,
            out_specs=places[0] if single else places,
            scratch_shapes=list(scratch),
            compiler_params=pltpu.CompilerParams(vmem_limit_bytes=limit),
            cost_estimate=pl.CostEstimate(flops=flops, bytes_accessed=moved, transcendentals=0),
        )(*args)

    return run


def on_device(
    saved, cotangent, w_in, b_in, w_mid, b_mid, w_out, spectral_gain, basis_in, basis_out
):
    forward, back = zonal_tables()
    bases = jnp.concatenate(
        [jnp.transpose(basis_in, (1, 2, 0)), jnp.transpose(basis_out, (1, 0, 2))], axis=1
    )
    bases = jnp.pad(bases, ((0, LAT_DEV - M_DEV), (0, 0), (0, 0)))
    bases, saved = lax.optimization_barrier((bases, saved))
    bases = lax.all_to_all(bases, "lat", 0, 0, tiled=True)
    weights = (w_in, b_in.reshape(1, -1), w_mid, b_mid.reshape(1, -1), w_out)
    held = [pltpu.VMEM(a.shape, a.dtype) for a in (saved, cotangent) + weights]
    pad = pltpu.VMEM((X_DEV, Y_PAD, CHAN), bf16)
    pieces = call(
        network_kernel,
        (LON_DEV, Y_MAIN, 128),
        bf16,
        held + [pad, pad, pltpu.SemaphoreType.DMA((7,))],
        space=pltpu.HBM,
        flops=1_700_000_000,
        moved=4_000_000,
        limit=NETWORK_VMEM,
    )(saved, cotangent, *weights)
    bases, pieces = lax.optimization_barrier((bases, pieces))
    pieces = lax.all_to_all(pieces, LON, 0, 0, tiled=True)
    mode = M_DEV * lax.axis_index(LON) + lax.axis_index("lat")
    place = jnp.stack([mode, lax.axis_index("core")]).astype(jnp.int32)
    tables = call(bases_kernel, (2, NL, NLAT), bf16, smem=1, flops=600_000_000, moved=3_000_000)(
        place, bases
    )
    others = lax.ppermute(tables, "core", [(0, 1), (1, 0)])
    coeffs = call(zonal_kernel, (2 * DEVS, 128), bf16, flops=300_000_000)(
        pieces, jnp.asarray(forward)
    )
    coeffs = lax.all_to_all(coeffs.reshape(DEVS // 2, 4, 128), ("lat", "pair"), 0, 0, tiled=True)
    coeffs = call(
        legendre_kernel,
        (2 * DEVS, 128),
        bf16,
        (pltpu.VMEM((2 * DEVS, 128), f32),),
        smem=1,
        flops=200_000_000,
    )(place, coeffs.reshape(2 * DEVS, 128), tables, others, spectral_gain)
    coeffs = lax.all_to_all(coeffs.reshape(DEVS // 2, 4, 128), ("lat", "pair"), 0, 0, tiled=True)
    pieces = call(inverse_kernel, (LON_DEV, Y_MAIN, 128), bf16, flops=300_000_000)(
        coeffs.reshape(2 * DEVS, 128), jnp.asarray(back)
    )
    pieces = lax.all_to_all(pieces, LON, 0, 0, tiled=True)
    return call(grid_kernel, (X_DEV, Y_DEV, CHAN), f32)(pieces)


def solution(mesh):
    grid = P("lat", LON, None)
    placed = (grid, grid, P(), P(), P(), P(), P(), P(), P(None, LON, "lat"), grid)
    fine = Mesh(mesh.devices.reshape(LAT_DEV, PAIRS, 2), ("lat",) + LON)
    return jax.shard_map(on_device, mesh=fine, in_specs=placed, out_specs=grid, check_vma=False)
```

```python
import numpy as np
import jax
import jax.numpy as jnp
from jax import lax
from jax.experimental import pallas as pl
from jax.experimental.pallas import tpu as pltpu
from jax.sharding import Mesh, PartitionSpec as P

bf16 = jnp.bfloat16
f32 = jnp.float32

LAT_DEV, LON_DEV = 32, 16
PAIRS = LON_DEV // 2
X_DEV, Y_DEV = 12, 90
Y_PAD = 96
Y_MAIN, Y_EXT = 72, 24
NLAT, NLON, NM, NL, CHAN = 384, 1440, 368, 384, 128
M_DEV = 23
X_SUB, C_SUB = 3, 32
CG = CHAN // C_SUB
XG = X_DEV // X_SUB
DEVS = LAT_DEV * LON_DEV
ROWS = 2 * NM
LON = ("pair", "core")
VMEM = 16 * 1024 * 1024
NETWORK_VMEM = 59 * 1024 * 1024


def zonal_tables():
    order = (M_DEV * np.arange(LON_DEV)[None, :] + np.arange(M_DEV)[:, None]).reshape(-1)
    turns = (order[:, None] * np.arange(NLON)[None, :]) % NLON
    angles = turns.astype(np.float64) * (2.0 * np.pi / NLON)
    table = np.stack([np.cos(angles), -np.sin(angles)], 1).reshape(ROWS, NLON)
    weight = np.where(order == 0, 1.0, 2.0) / NLON
    back = table * np.repeat(weight, 2)[:, None]

    def split_y(t):
        t = np.pad(t.reshape(ROWS, LON_DEV, Y_DEV), ((0, 0), (0, 0), (0, Y_PAD - Y_DEV)))
        main = t[:, :, :Y_MAIN].reshape(ROWS, LON_DEV * Y_MAIN)
        extra = t[:, :, Y_MAIN:].reshape(ROWS, LON_DEV * Y_EXT)
        return np.concatenate([main, extra], 1)

    return (
        np.asarray(split_y(table), dtype=jnp.bfloat16),
        np.ascontiguousarray(split_y(back).T).astype(jnp.bfloat16),
    )


def owner(xg, cg):
    return CG * xg + 2 * (cg % 2) + cg // 2


def dot(a, b):
    return lax.dot_general(a, b, (((1,), (0,)), ((), ())), preferred_element_type=f32)


def dot_t(a, b):
    return lax.dot_general(a, b, (((1,), (1,)), ((), ())), preferred_element_type=f32)


def sigmoid(v):
    return 0.5 * jnp.tanh(0.5 * v) + 0.5


def arrange_kernel(first_h, second_h, out, first, second, rows, sems):
    copies = [
        pltpu.make_async_copy(first_h, first, sems.at[0]),
        pltpu.make_async_copy(second_h, second, sems.at[1]),
    ]
    for copy in copies:
        copy.start()
    out[M_DEV:] = jnp.zeros((LAT_DEV - M_DEV, 24, NL), bf16)
    for half, source in enumerate((first, second)):
        copies[half].wait()
        for k in range(12):
            block = source[k].astype(f32)
            for t in range(3):
                rows[t, pl.ds(12 * half + k, M_DEV, stride=24), :] = block[:, 128 * t : 128 * (t + 1)]
    for m in range(M_DEV):
        for t in range(3):
            out[m, :, 128 * t : 128 * (t + 1)] = rows[t, 24 * m : 24 * (m + 1), :].astype(bf16)


def network_kernel(
    saved_h, cotan_h, w_in_h, b_in_h, w_mid_h, b_mid_h, w_out_h, out,
    saved, cotan, w_in, b_in, w_mid, b_mid, w_out, rows_s, rows_c, sems,
):
    pairs = (
        (saved_h, saved), (w_in_h, w_in), (b_in_h, b_in), (w_mid_h, w_mid),
        (b_mid_h, b_mid), (cotan_h, cotan), (w_out_h, w_out),
    )
    copies = [pltpu.make_async_copy(a, b, sems.at[k]) for k, (a, b) in enumerate(pairs)]
    for copy in copies:
        copy.start()
    got = dict(zip(("saved", "w_in", "b_in", "w_mid", "b_mid", "cotan", "w_out"), copies))
    edge = jnp.zeros((X_DEV, 16, CHAN), bf16)
    rows_s[:, Y_PAD - 16 :, :] = edge
    rows_c[:, Y_PAD - 16 :, :] = edge
    got["saved"].wait()
    for x in range(X_DEV):
        rows_s[x, 0:Y_DEV, :] = saved[x]
    got["w_in"].wait()
    got["b_in"].wait()
    for xg in range(XG):
        s = rows_s[X_SUB * xg : X_SUB * (xg + 1)].reshape(X_SUB * Y_PAD, CHAN)
        first = dot(s, w_in[...]) + b_in[...]
        sig = sigmoid(first)
        act = first * sig
        slope_one = sig + act * (1.0 - sig)
        if xg == 0:
            got["w_mid"].wait()
            got["b_mid"].wait()
        second = dot(act.astype(bf16), w_mid[...]) + b_mid[...]
        sig = sigmoid(second)
        slope_two = sig * (1.0 + second * (1.0 - sig))
        if xg == 0:
            got["cotan"].wait()
            got["w_out"].wait()
            for x in range(X_DEV):
                rows_c[x, 0:Y_DEV, :] = cotan[x]
        c = rows_c[X_SUB * xg : X_SUB * (xg + 1)].reshape(X_SUB * Y_PAD, CHAN)
        back_two = (dot_t(c, w_out[...]) * slope_two).astype(bf16)
        back_one = (dot_t(back_two, w_mid[...]) * slope_one).astype(bf16)
        grad = c.astype(f32) + dot_t(back_one, w_in[...])
        grad = grad.reshape(X_SUB, Y_PAD, CHAN)
        for cg in range(CG):
            parts = [grad[xx][:, C_SUB * cg : C_SUB * (cg + 1)] for xx in range(X_SUB)]
            parts = [p[0:Y_MAIN] for p in parts] + [
                jnp.concatenate([p[Y_MAIN:] for p in parts], axis=0)
            ]
            out[owner(xg, cg)] = jnp.concatenate(parts, axis=1).astype(bf16)


def zonal_kernel(circles, table, out):
    main, extra = [], []
    for j in range(LON_DEV):
        piece = circles[j].astype(f32)
        main.append(piece)
        parts = [piece[Y_EXT * xx : Y_EXT * (xx + 1), 96:128] for xx in range(X_SUB)]
        extra.append(jnp.concatenate(parts + [jnp.zeros((Y_EXT, C_SUB), f32)], axis=1))
    g = jnp.concatenate(main + extra, axis=0).astype(bf16)
    out[0:ROWS, :] = dot(table[...], g).astype(bf16)
    out[ROWS:, :] = jnp.zeros((2 * DEVS - ROWS, 128), bf16)


def bases_kernel(place, bases, out):
    m = place[0]

    def index(shape, axis):
        return lax.broadcasted_iota(jnp.int32, shape, axis)

    def pick(mask):
        return jnp.where(mask, 1.0, 0.0).astype(bf16)

    rows = bases[...].astype(f32).reshape(LAT_DEV * 24, NL).astype(bf16)
    wave = index((NL, 1), 0)
    tile = lax.shift_right_logical(wave * 5462, 16)
    chosen = pick(index((NL, LAT_DEV * 24), 1) == wave + 12 * tile)
    table = dot(chosen, rows)
    table = jnp.where(index((NL, NLAT), 0) >= m, table, 0.0).astype(bf16)
    spot = index((1, NLAT), 1)
    x = 12 * (spot & 31) + X_SUB * ((spot >> 5) & 3) + (spot >> 7)
    columns = pick(index((NLAT, NLAT), 0) == x)
    out[0] = dot(table, columns).astype(bf16)
    spot = index((NLAT, 1), 0)
    row = 24 * (spot & 31) + 12 + X_SUB * ((spot >> 5) & 3) + (spot >> 7)
    chosen = pick(index((NLAT, LAT_DEV * 24), 1) == row)
    table = dot(chosen, rows)
    out[1] = jnp.where(index((NLAT, NL), 1) >= m, table, 0.0).astype(bf16)


def legendre_kernel(place, coeffs, tables, others, gain, out, rows):
    core = place[1]

    def swapped(pair):
        return jnp.where(core == 0, pair[0], pair[1]), jnp.where(core == 0, pair[1], pair[0])

    rows[...] = coeffs[...].astype(f32)
    blocks = [
        [rows[pl.ds(4 * k + n, LAT_DEV, stride=32), :] for n in range(4)] for k in range(PAIRS)
    ]
    modes = []
    for h in range(2):
        stack = []
        for xx in range(X_SUB):
            for xg in range(XG):
                parts = [
                    blocks[2 * xg + cq][2 * h + r][:, C_SUB * xx : C_SUB * (xx + 1)]
                    for r in range(2)
                    for cq in range(2)
                ]
                stack.append(jnp.concatenate(parts, axis=1))
        modes.append(jnp.concatenate(stack, axis=0))
    half = jnp.where(core == 0, gain[:, 0:64], gain[:, 64:128])
    gains = jnp.concatenate([half, half], axis=1)
    results = []
    for fourier, table in zip(swapped(modes), (tables, others)):
        filtered = (dot(table[0], fourier.astype(bf16)) * gains).astype(bf16)
        results.append(dot(table[1], filtered))
    results = swapped(results)
    for k in range(PAIRS):
        xg, cq = k // 2, k % 2
        for h in range(2):
            for r in range(2):
                first = 64 * r + C_SUB * cq
                parts = [
                    results[h][32 * (XG * xx + xg) : 32 * (XG * xx + xg + 1), first : first + C_SUB]
                    for xx in range(X_SUB)
                ]
                parts.append(jnp.zeros((LAT_DEV, C_SUB), f32))
                rows[pl.ds(4 * k + 2 * h + r, LAT_DEV, stride=32), :] = jnp.concatenate(parts, axis=1)
    out[...] = rows[...].astype(bf16)


def inverse_kernel(coeffs, table, out):
    g = dot(table[...], coeffs[0:ROWS, :])
    for j in range(LON_DEV):
        main = g[Y_MAIN * j : Y_MAIN * (j + 1), 0:96]
        first = LON_DEV * Y_MAIN + Y_EXT * j
        extra = g[first : first + Y_EXT]
        parts = [extra[:, C_SUB * xx : C_SUB * (xx + 1)] for xx in range(X_SUB)]
        out[j] = jnp.concatenate([main, jnp.concatenate(parts, axis=0)], axis=1).astype(bf16)


def grid_kernel(pieces, out):
    for xg in range(XG):
        blocks = [pieces[owner(xg, cg)].astype(f32) for cg in range(CG)]
        for xx in range(X_SUB):
            main = [b[:, C_SUB * xx : C_SUB * (xx + 1)] for b in blocks]
            extra = [b[Y_EXT * xx : Y_EXT * (xx + 1), 96:128] for b in blocks]
            out[X_SUB * xg + xx, 0:Y_MAIN, :] = jnp.concatenate(main, axis=1)
            out[X_SUB * xg + xx, Y_MAIN:, :] = jnp.concatenate(extra, axis=1)[0 : Y_DEV - Y_MAIN]


def call(
    kernel, shape, dtype, scratch=(), smem=0, space=pltpu.VMEM, flops=0, moved=0, limit=VMEM
):
    outs = [jax.ShapeDtypeStruct(s, dtype) for s in (shape if isinstance(shape, list) else [shape])]
    places = [pl.BlockSpec(memory_space=pltpu.VMEM) for _ in outs]
    single = not isinstance(shape, list)

    def run(*args):
        specs = [
            pl.BlockSpec(memory_space=pltpu.SMEM if k < smem else space) for k in range(len(args))
        ]
        return pl.pallas_call(
            kernel,
            out_shape=outs[0] if single else outs,
            in_specs=specs,
            out_specs=places[0] if single else places,
            scratch_shapes=list(scratch),
            compiler_params=pltpu.CompilerParams(vmem_limit_bytes=limit),
            cost_estimate=pl.CostEstimate(flops=flops, bytes_accessed=moved, transcendentals=0),
        )(*args)

    return run


def arrange(first, second):
    shape = pltpu.VMEM((12, M_DEV, NL), bf16)
    rows = pltpu.VMEM((3, M_DEV * 24, 128), f32)
    return call(
        arrange_kernel,
        (LAT_DEV, 24, NL),
        bf16,
        (shape, shape, rows, pltpu.SemaphoreType.DMA((2,))),
        space=pltpu.HBM,
        limit=NETWORK_VMEM,
    )(first, second)


def on_device(
    saved, cotangent, w_in, b_in, w_mid, b_mid, w_out, spectral_gain, basis_in, basis_out
):
    forward, back = zonal_tables()
    bases = arrange(jnp.transpose(basis_in, (2, 1, 0)), basis_out)
    bases, saved = lax.optimization_barrier((bases, saved))
    bases = lax.all_to_all(bases, "lat", 0, 0, tiled=True)
    weights = (w_in, b_in.reshape(1, -1), w_mid, b_mid.reshape(1, -1), w_out)
    held = [pltpu.VMEM(a.shape, a.dtype) for a in (saved, cotangent) + weights]
    pad = pltpu.VMEM((X_DEV, Y_PAD, CHAN), bf16)
    pieces = call(
        network_kernel,
        (LON_DEV, Y_MAIN, 128),
        bf16,
        held + [pad, pad, pltpu.SemaphoreType.DMA((7,))],
        space=pltpu.HBM,
        flops=1_700_000_000,
        moved=4_000_000,
        limit=NETWORK_VMEM,
    )(saved, cotangent, *weights)
    bases, pieces = lax.optimization_barrier((bases, pieces))
    pieces = lax.all_to_all(pieces, LON, 0, 0, tiled=True)
    mode = M_DEV * lax.axis_index(LON) + lax.axis_index("lat")
    place = jnp.stack([mode, lax.axis_index("core")]).astype(jnp.int32)
    tables = call(bases_kernel, (2, NL, NLAT), bf16, smem=1, flops=600_000_000, moved=3_000_000)(
        place, bases
    )
    others = lax.ppermute(tables, "core", [(0, 1), (1, 0)])
    coeffs = call(zonal_kernel, (2 * DEVS, 128), bf16, flops=300_000_000)(
        pieces, jnp.asarray(forward)
    )
    others, coeffs = lax.optimization_barrier((others, coeffs))
    coeffs = lax.all_to_all(coeffs.reshape(DEVS // 2, 4, 128), ("lat", "pair"), 0, 0, tiled=True)
    coeffs = call(
        legendre_kernel,
        (2 * DEVS, 128),
        bf16,
        (pltpu.VMEM((2 * DEVS, 128), f32),),
        smem=1,
        flops=200_000_000,
    )(place, coeffs.reshape(2 * DEVS, 128), tables, others, spectral_gain)
    coeffs = lax.all_to_all(coeffs.reshape(DEVS // 2, 4, 128), ("lat", "pair"), 0, 0, tiled=True)
    pieces = call(inverse_kernel, (LON_DEV, Y_MAIN, 128), bf16, flops=300_000_000)(
        coeffs.reshape(2 * DEVS, 128), jnp.asarray(back)
    )
    pieces = lax.all_to_all(pieces, LON, 0, 0, tiled=True)
    return call(grid_kernel, (X_DEV, Y_DEV, CHAN), f32)(pieces)


def solution(mesh):
    grid = P("lat", LON, None)
    placed = (grid, grid, P(), P(), P(), P(), P(), P(), P(None, LON, "lat"), grid)
    fine = Mesh(mesh.devices.reshape(LAT_DEV, PAIRS, 2), ("lat",) + LON)
    return jax.shard_map(on_device, mesh=fine, in_specs=placed, out_specs=grid, check_vma=False)
```

```python
import numpy as np
import jax
import jax.numpy as jnp
from jax import lax
from jax.experimental import pallas as pl
from jax.experimental.pallas import tpu as pltpu
from jax.sharding import Mesh, PartitionSpec as P

bf16 = jnp.bfloat16
f32 = jnp.float32

LAT_DEV, LON_DEV = 32, 16
PAIRS = LON_DEV // 2
X_DEV, Y_DEV = 12, 90
Y_PAD = 96
Y_MAIN, Y_EXT = 72, 24
NLAT, NLON, NM, NL, CHAN = 384, 1440, 368, 384, 128
M_DEV = 23
X_SUB, C_SUB = 3, 32
CG = CHAN // C_SUB
XG = X_DEV // X_SUB
DEVS = LAT_DEV * LON_DEV
ROWS = 2 * NM
LON = ("x", "z_hi", "core")
VMEM = 16 * 1024 * 1024
NETWORK_VMEM = 59 * 1024 * 1024


def zonal_tables():
    order = (M_DEV * np.arange(LON_DEV)[None, :] + np.arange(M_DEV)[:, None]).reshape(-1)
    turns = (order[:, None] * np.arange(NLON)[None, :]) % NLON
    angles = turns.astype(np.float64) * (2.0 * np.pi / NLON)
    table = np.stack([np.cos(angles), -np.sin(angles)], 1).reshape(ROWS, NLON)
    weight = np.where(order == 0, 1.0, 2.0) / NLON
    back = table * np.repeat(weight, 2)[:, None]

    def split_y(t):
        t = np.pad(t.reshape(ROWS, LON_DEV, Y_DEV), ((0, 0), (0, 0), (0, Y_PAD - Y_DEV)))
        main = t[:, :, :Y_MAIN].reshape(ROWS, LON_DEV * Y_MAIN)
        extra = t[:, :, Y_MAIN:].reshape(ROWS, LON_DEV * Y_EXT)
        return np.concatenate([main, extra], 1)

    return (
        np.asarray(split_y(table), dtype=jnp.bfloat16),
        np.ascontiguousarray(split_y(back).T).astype(jnp.bfloat16),
    )


def owner(xg, cg):
    return CG * xg + 2 * (cg % 2) + cg // 2


def dot(a, b):
    return lax.dot_general(a, b, (((1,), (0,)), ((), ())), preferred_element_type=f32)


def dot_t(a, b):
    return lax.dot_general(a, b, (((1,), (1,)), ((), ())), preferred_element_type=f32)


def sigmoid(v):
    return 0.5 * jnp.tanh(0.5 * v) + 0.5


def arrange_kernel(first_h, second_h, out, first, second, rows, sems):
    copies = [
        pltpu.make_async_copy(first_h, first, sems.at[0]),
        pltpu.make_async_copy(second_h, second, sems.at[1]),
    ]
    for copy in copies:
        copy.start()
    out[M_DEV:] = jnp.zeros((LAT_DEV - M_DEV, 24, NL), bf16)
    for half, source in enumerate((first, second)):
        copies[half].wait()
        for k in range(12):
            block = source[k].astype(f32)
            for t in range(3):
                rows[t, pl.ds(12 * half + k, M_DEV, stride=24), :] = block[:, 128 * t : 128 * (t + 1)]
    for m in range(M_DEV):
        for t in range(3):
            out[m, :, 128 * t : 128 * (t + 1)] = rows[t, 24 * m : 24 * (m + 1), :].astype(bf16)


def network_kernel(
    z_hi, saved_h, cotan_h, w_in_h, b_in_h, w_mid_h, b_mid_h, w_out_h, kept, sent,
    saved, cotan, w_in, b_in, w_mid, b_mid, w_out, rows_s, rows_c, sems,
):
    pairs = (
        (saved_h, saved), (w_in_h, w_in), (b_in_h, b_in), (w_mid_h, w_mid),
        (b_mid_h, b_mid), (cotan_h, cotan), (w_out_h, w_out),
    )
    copies = [pltpu.make_async_copy(a, b, sems.at[k]) for k, (a, b) in enumerate(pairs)]
    for copy in copies:
        copy.start()
    got = dict(zip(("saved", "w_in", "b_in", "w_mid", "b_mid", "cotan", "w_out"), copies))
    edge = jnp.zeros((X_DEV, 16, CHAN), bf16)
    rows_s[:, Y_PAD - 16 :, :] = edge
    rows_c[:, Y_PAD - 16 :, :] = edge
    got["saved"].wait()
    for x in range(X_DEV):
        rows_s[x, 0:Y_DEV, :] = saved[x]
    got["w_in"].wait()
    got["b_in"].wait()
    for xg in range(XG):
        s = rows_s[X_SUB * xg : X_SUB * (xg + 1)].reshape(X_SUB * Y_PAD, CHAN)
        first = dot(s, w_in[...]) + b_in[...]
        sig = sigmoid(first)
        act = first * sig
        slope_one = sig + act * (1.0 - sig)
        if xg == 0:
            got["w_mid"].wait()
            got["b_mid"].wait()
        second = dot(act.astype(bf16), w_mid[...]) + b_mid[...]
        sig = sigmoid(second)
        slope_two = sig * (1.0 + second * (1.0 - sig))
        if xg == 0:
            got["cotan"].wait()
            got["w_out"].wait()
            for x in range(X_DEV):
                rows_c[x, 0:Y_DEV, :] = cotan[x]
        c = rows_c[X_SUB * xg : X_SUB * (xg + 1)].reshape(X_SUB * Y_PAD, CHAN)
        back_two = (dot_t(c, w_out[...]) * slope_two).astype(bf16)
        back_one = (dot_t(back_two, w_mid[...]) * slope_one).astype(bf16)
        grad = c.astype(f32) + dot_t(back_one, w_in[...])
        grad = grad.reshape(X_SUB, Y_PAD, CHAN)
        for h in range(2):
            blocks = []
            for cg in (2 * h, 2 * h + 1):
                parts = [grad[xx][:, C_SUB * cg : C_SUB * (cg + 1)] for xx in range(X_SUB)]
                parts = [p[0:Y_MAIN] for p in parts] + [
                    jnp.concatenate([p[Y_MAIN:] for p in parts], axis=0)
                ]
                blocks.append(jnp.concatenate(parts, axis=1))
            low = z_hi[0] == 0
            kept[2 * xg + h] = jnp.where(low, blocks[0], blocks[1]).astype(bf16)
            sent[2 * xg + h] = jnp.where(low, blocks[1], blocks[0]).astype(bf16)


def zonal_kernel(z_hi, circles, table, out):
    main, extra = [], []
    for j in range(LON_DEV):
        x, z, core = j // 4, j // 2 % 2, j % 2
        piece = circles[2 * x + core, z_hi[0] ^ z].astype(f32)
        main.append(piece)
        parts = [piece[Y_EXT * xx : Y_EXT * (xx + 1), 96:128] for xx in range(X_SUB)]
        extra.append(jnp.concatenate(parts + [jnp.zeros((Y_EXT, C_SUB), f32)], axis=1))
    g = jnp.concatenate(main + extra, axis=0).astype(bf16)
    out[0:ROWS, :] = dot(table[...], g).astype(bf16)
    out[ROWS:, :] = jnp.zeros((2 * DEVS - ROWS, 128), bf16)


def bases_kernel(place, bases, out):
    m = place[0]

    def index(shape, axis):
        return lax.broadcasted_iota(jnp.int32, shape, axis)

    def pick(mask):
        return jnp.where(mask, 1.0, 0.0).astype(bf16)

    rows = bases[...].astype(f32).reshape(LAT_DEV * 24, NL).astype(bf16)
    wave = index((NL, 1), 0)
    tile = lax.shift_right_logical(wave * 5462, 16)
    chosen = pick(index((NL, LAT_DEV * 24), 1) == wave + 12 * tile)
    table = dot(chosen, rows)
    table = jnp.where(index((NL, NLAT), 0) >= m, table, 0.0).astype(bf16)
    spot = index((1, NLAT), 1)
    x = 12 * (spot & 31) + X_SUB * ((spot >> 5) & 3) + (spot >> 7)
    columns = pick(index((NLAT, NLAT), 0) == x)
    out[0] = dot(table, columns).astype(bf16)
    spot = index((NLAT, 1), 0)
    row = 24 * (spot & 31) + 12 + X_SUB * ((spot >> 5) & 3) + (spot >> 7)
    chosen = pick(index((NLAT, LAT_DEV * 24), 1) == row)
    table = dot(chosen, rows)
    out[1] = jnp.where(index((NLAT, NL), 1) >= m, table, 0.0).astype(bf16)


def legendre_kernel(place, coeffs, tables, others, gain, out, rows):
    core = place[1]

    def swapped(pair):
        return jnp.where(core == 0, pair[0], pair[1]), jnp.where(core == 0, pair[1], pair[0])

    rows[...] = coeffs[...].astype(f32)
    blocks = [
        [rows[pl.ds(4 * k + n, LAT_DEV, stride=32), :] for n in range(4)] for k in range(PAIRS)
    ]
    modes = []
    for h in range(2):
        stack = []
        for xx in range(X_SUB):
            for xg in range(XG):
                parts = [
                    blocks[2 * xg + cq][2 * h + r][:, C_SUB * xx : C_SUB * (xx + 1)]
                    for r in range(2)
                    for cq in range(2)
                ]
                stack.append(jnp.concatenate(parts, axis=1))
        modes.append(jnp.concatenate(stack, axis=0))
    half = jnp.where(core == 0, gain[:, 0:64], gain[:, 64:128])
    gains = jnp.concatenate([half, half], axis=1)
    results = []
    for fourier, table in zip(swapped(modes), (tables, others)):
        filtered = (dot(table[0], fourier.astype(bf16)) * gains).astype(bf16)
        results.append(dot(table[1], filtered))
    results = swapped(results)
    for k in range(PAIRS):
        xg, cq = k // 2, k % 2
        for h in range(2):
            for r in range(2):
                first = 64 * r + C_SUB * cq
                parts = [
                    results[h][32 * (XG * xx + xg) : 32 * (XG * xx + xg + 1), first : first + C_SUB]
                    for xx in range(X_SUB)
                ]
                parts.append(jnp.zeros((LAT_DEV, C_SUB), f32))
                rows[pl.ds(4 * k + 2 * h + r, LAT_DEV, stride=32), :] = jnp.concatenate(parts, axis=1)
    out[...] = rows[...].astype(bf16)


def inverse_kernel(coeffs, table, out):
    g = dot(table[...], coeffs[0:ROWS, :])
    for j in range(LON_DEV):
        main = g[Y_MAIN * j : Y_MAIN * (j + 1), 0:96]
        first = LON_DEV * Y_MAIN + Y_EXT * j
        extra = g[first : first + Y_EXT]
        parts = [extra[:, C_SUB * xx : C_SUB * (xx + 1)] for xx in range(X_SUB)]
        out[j] = jnp.concatenate([main, jnp.concatenate(parts, axis=0)], axis=1).astype(bf16)


def grid_kernel(pieces, out):
    for xg in range(XG):
        blocks = [pieces[owner(xg, cg)].astype(f32) for cg in range(CG)]
        for xx in range(X_SUB):
            main = [b[:, C_SUB * xx : C_SUB * (xx + 1)] for b in blocks]
            extra = [b[Y_EXT * xx : Y_EXT * (xx + 1), 96:128] for b in blocks]
            out[X_SUB * xg + xx, 0:Y_MAIN, :] = jnp.concatenate(main, axis=1)
            out[X_SUB * xg + xx, Y_MAIN:, :] = jnp.concatenate(extra, axis=1)[0 : Y_DEV - Y_MAIN]


def call(
    kernel, shape, dtype, scratch=(), smem=0, space=pltpu.VMEM, flops=0, moved=0, limit=VMEM
):
    outs = [jax.ShapeDtypeStruct(s, dtype) for s in (shape if isinstance(shape, list) else [shape])]
    places = [pl.BlockSpec(memory_space=pltpu.VMEM) for _ in outs]
    single = not isinstance(shape, list)

    def run(*args):
        specs = [
            pl.BlockSpec(memory_space=pltpu.SMEM if k < smem else space) for k in range(len(args))
        ]
        return pl.pallas_call(
            kernel,
            out_shape=outs[0] if single else outs,
            in_specs=specs,
            out_specs=places[0] if single else places,
            scratch_shapes=list(scratch),
            compiler_params=pltpu.CompilerParams(vmem_limit_bytes=limit),
            cost_estimate=pl.CostEstimate(flops=flops, bytes_accessed=moved, transcendentals=0),
        )(*args)

    return run


def arrange(first, second):
    shape = pltpu.VMEM((12, M_DEV, NL), bf16)
    rows = pltpu.VMEM((3, M_DEV * 24, 128), f32)
    return call(
        arrange_kernel,
        (LAT_DEV, 24, NL),
        bf16,
        (shape, shape, rows, pltpu.SemaphoreType.DMA((2,))),
        space=pltpu.HBM,
        limit=NETWORK_VMEM,
    )(first, second)


def on_device(
    saved, cotangent, w_in, b_in, w_mid, b_mid, w_out, spectral_gain, basis_in, basis_out
):
    forward, back = zonal_tables()
    bases = arrange(jnp.transpose(basis_in, (2, 1, 0)), basis_out)
    bases, saved = lax.optimization_barrier((bases, saved))
    bases = lax.all_to_all(bases, "lat", 0, 0, tiled=True)
    z_hi = lax.axis_index("z_hi").astype(jnp.int32).reshape(1)
    weights = (w_in, b_in.reshape(1, -1), w_mid, b_mid.reshape(1, -1), w_out)
    held = [pltpu.VMEM(a.shape, a.dtype) for a in (saved, cotangent) + weights]
    pad = pltpu.VMEM((X_DEV, Y_PAD, CHAN), bf16)
    kept, sent = call(
        network_kernel,
        [(PAIRS, Y_MAIN, 128), (PAIRS, Y_MAIN, 128)],
        bf16,
        held + [pad, pad, pltpu.SemaphoreType.DMA((7,))],
        smem=1,
        space=pltpu.HBM,
        flops=1_700_000_000,
        moved=4_000_000,
        limit=NETWORK_VMEM,
    )(z_hi, saved, cotangent, *weights)
    sent = lax.ppermute(sent, "z_hi", [(0, 1), (1, 0)])
    pieces = jnp.stack([kept, sent], axis=1)
    bases, pieces = lax.optimization_barrier((bases, pieces))
    pieces = lax.all_to_all(pieces, ("x", "core"), 0, 0, tiled=True)
    mode = M_DEV * lax.axis_index(LON) + lax.axis_index("lat")
    place = jnp.stack([mode, lax.axis_index("core")]).astype(jnp.int32)
    tables = call(bases_kernel, (2, NL, NLAT), bf16, smem=1, flops=600_000_000, moved=3_000_000)(
        place, bases
    )
    others = lax.ppermute(tables, "core", [(0, 1), (1, 0)])
    coeffs = call(zonal_kernel, (2 * DEVS, 128), bf16, smem=1, flops=300_000_000)(
        z_hi, pieces, jnp.asarray(forward)
    )
    coeffs = lax.all_to_all(coeffs.reshape(DEVS // 2, 4, 128), ("lat", "x", "z_hi"), 0, 0, tiled=True)
    coeffs = call(
        legendre_kernel,
        (2 * DEVS, 128),
        bf16,
        (pltpu.VMEM((2 * DEVS, 128), f32),),
        smem=1,
        flops=200_000_000,
    )(place, coeffs.reshape(2 * DEVS, 128), tables, others, spectral_gain)
    coeffs = lax.all_to_all(coeffs.reshape(DEVS // 2, 4, 128), ("lat", "x", "z_hi"), 0, 0, tiled=True)
    pieces = call(inverse_kernel, (LON_DEV, Y_MAIN, 128), bf16, flops=300_000_000)(
        coeffs.reshape(2 * DEVS, 128), jnp.asarray(back)
    )
    pieces = lax.all_to_all(pieces, LON, 0, 0, tiled=True)
    return call(grid_kernel, (X_DEV, Y_DEV, CHAN), f32)(pieces)


def solution(mesh):
    grid = P("lat", LON, None)
    placed = (grid, grid, P(), P(), P(), P(), P(), P(), P(None, LON, "lat"), grid)
    fine = Mesh(mesh.devices.reshape(LAT_DEV, XG, 2, 2), ("lat",) + LON)
    return jax.shard_map(on_device, mesh=fine, in_specs=placed, out_specs=grid, check_vma=False)
```

```python
import numpy as np
import jax
import jax.numpy as jnp
from jax import lax
from jax.experimental import pallas as pl
from jax.experimental.pallas import tpu as pltpu
from jax.sharding import Mesh, PartitionSpec as P

bf16 = jnp.bfloat16
f32 = jnp.float32

LAT_DEV, LON_DEV = 32, 16
PAIRS = LON_DEV // 2
X_DEV, Y_DEV = 12, 90
Y_PAD = 96
Y_MAIN, Y_EXT = 72, 24
NLAT, NLON, NM, NL, CHAN = 384, 1440, 368, 384, 128
M_DEV = 23
X_SUB, C_SUB = 3, 32
CG = CHAN // C_SUB
XG = X_DEV // X_SUB
DEVS = LAT_DEV * LON_DEV
ROWS = 2 * NM
LON = ("x", "z_hi", "core")
VMEM = 16 * 1024 * 1024
NETWORK_VMEM = 59 * 1024 * 1024


def zonal_tables():
    order = (M_DEV * np.arange(LON_DEV)[None, :] + np.arange(M_DEV)[:, None]).reshape(-1)
    turns = (order[:, None] * np.arange(NLON)[None, :]) % NLON
    angles = turns.astype(np.float64) * (2.0 * np.pi / NLON)
    table = np.stack([np.cos(angles), -np.sin(angles)], 1).reshape(ROWS, NLON)
    weight = np.where(order == 0, 1.0, 2.0) / NLON
    back = table * np.repeat(weight, 2)[:, None]

    def split_y(t):
        t = np.pad(t.reshape(ROWS, LON_DEV, Y_DEV), ((0, 0), (0, 0), (0, Y_PAD - Y_DEV)))
        main = t[:, :, :Y_MAIN].reshape(ROWS, LON_DEV * Y_MAIN)
        extra = t[:, :, Y_MAIN:].reshape(ROWS, LON_DEV * Y_EXT)
        return np.concatenate([main, extra], 1)

    return (
        np.asarray(split_y(table), dtype=jnp.bfloat16),
        np.ascontiguousarray(split_y(back).T).astype(jnp.bfloat16),
    )


def owner(xg, cg):
    return CG * xg + 2 * (cg % 2) + cg // 2


def dot(a, b):
    return lax.dot_general(a, b, (((1,), (0,)), ((), ())), preferred_element_type=f32)


def dot_t(a, b):
    return lax.dot_general(a, b, (((1,), (1,)), ((), ())), preferred_element_type=f32)


def sigmoid(v):
    return 0.5 * jnp.tanh(0.5 * v) + 0.5


def arrange_kernel(first_h, second_h, out, first, second, rows, sems):
    copies = [
        pltpu.make_async_copy(first_h, first, sems.at[0]),
        pltpu.make_async_copy(second_h, second, sems.at[1]),
    ]
    for copy in copies:
        copy.start()
    out[M_DEV:] = jnp.zeros((LAT_DEV - M_DEV, 24, NL), bf16)
    for half, source in enumerate((first, second)):
        copies[half].wait()
        for k in range(12):
            block = source[k].astype(f32)
            for t in range(3):
                rows[t, pl.ds(12 * half + k, M_DEV, stride=24), :] = block[:, 128 * t : 128 * (t + 1)]
    for m in range(M_DEV):
        for t in range(3):
            out[m, :, 128 * t : 128 * (t + 1)] = rows[t, 24 * m : 24 * (m + 1), :].astype(bf16)


def network_kernel(
    z_hi, saved_h, cotan_h, w_in_h, b_in_h, w_mid_h, b_mid_h, w_out_h, kept, sent,
    saved, cotan, w_in, b_in, w_mid, b_mid, w_out, rows_s, rows_c, sems,
):
    pairs = (
        (saved_h, saved), (w_in_h, w_in), (b_in_h, b_in), (w_mid_h, w_mid),
        (b_mid_h, b_mid), (cotan_h, cotan), (w_out_h, w_out),
    )
    copies = [pltpu.make_async_copy(a, b, sems.at[k]) for k, (a, b) in enumerate(pairs)]
    for copy in copies:
        copy.start()
    got = dict(zip(("saved", "w_in", "b_in", "w_mid", "b_mid", "cotan", "w_out"), copies))
    edge = jnp.zeros((X_DEV, 16, CHAN), bf16)
    rows_s[:, Y_PAD - 16 :, :] = edge
    rows_c[:, Y_PAD - 16 :, :] = edge
    got["saved"].wait()
    for x in range(X_DEV):
        rows_s[x, 0:Y_DEV, :] = saved[x]
    got["w_in"].wait()
    got["b_in"].wait()
    for xg in range(XG):
        s = rows_s[X_SUB * xg : X_SUB * (xg + 1)].reshape(X_SUB * Y_PAD, CHAN)
        first = dot(s, w_in[...]) + b_in[...]
        sig = sigmoid(first)
        act = first * sig
        slope_one = sig + act * (1.0 - sig)
        if xg == 0:
            got["w_mid"].wait()
            got["b_mid"].wait()
        second = dot(act.astype(bf16), w_mid[...]) + b_mid[...]
        sig = sigmoid(second)
        slope_two = sig * (1.0 + second * (1.0 - sig))
        if xg == 0:
            got["cotan"].wait()
            got["w_out"].wait()
            for x in range(X_DEV):
                rows_c[x, 0:Y_DEV, :] = cotan[x]
        c = rows_c[X_SUB * xg : X_SUB * (xg + 1)].reshape(X_SUB * Y_PAD, CHAN)
        back_two = (dot_t(c, w_out[...]) * slope_two).astype(bf16)
        back_one = (dot_t(back_two, w_mid[...]) * slope_one).astype(bf16)
        grad = c.astype(f32) + dot_t(back_one, w_in[...])
        grad = grad.reshape(X_SUB, Y_PAD, CHAN)
        for h in range(2):
            blocks = []
            for cg in (2 * h, 2 * h + 1):
                parts = [grad[xx][:, C_SUB * cg : C_SUB * (cg + 1)] for xx in range(X_SUB)]
                parts = [p[0:Y_MAIN] for p in parts] + [
                    jnp.concatenate([p[Y_MAIN:] for p in parts], axis=0)
                ]
                blocks.append(jnp.concatenate(parts, axis=1))
            low = z_hi[0] == 0
            kept[2 * xg + h] = jnp.where(low, blocks[0], blocks[1]).astype(bf16)
            sent[2 * xg + h] = jnp.where(low, blocks[1], blocks[0]).astype(bf16)


def join_kernel(kept, sent, out):
    for k in range(PAIRS):
        out[k, 0] = kept[k]
        out[k, 1] = sent[k]


def zonal_kernel(z_hi, circles, table, out):
    main, extra = [], []
    for j in range(LON_DEV):
        x, z, core = j // 4, j // 2 % 2, j % 2
        piece = circles[2 * x + core, z_hi[0] ^ z].astype(f32)
        main.append(piece)
        parts = [piece[Y_EXT * xx : Y_EXT * (xx + 1), 96:128] for xx in range(X_SUB)]
        extra.append(jnp.concatenate(parts + [jnp.zeros((Y_EXT, C_SUB), f32)], axis=1))
    g = jnp.concatenate(main + extra, axis=0).astype(bf16)
    out[0:ROWS, :] = dot(table[...], g).astype(bf16)
    out[ROWS:, :] = jnp.zeros((2 * DEVS - ROWS, 128), bf16)


def bases_kernel(place, bases, out):
    m = place[0]

    def index(shape, axis):
        return lax.broadcasted_iota(jnp.int32, shape, axis)

    def pick(mask):
        return jnp.where(mask, 1.0, 0.0).astype(bf16)

    rows = bases[...].astype(f32).reshape(LAT_DEV * 24, NL).astype(bf16)
    wave = index((NL, 1), 0)
    tile = lax.shift_right_logical(wave * 5462, 16)
    chosen = pick(index((NL, LAT_DEV * 24), 1) == wave + 12 * tile)
    table = dot(chosen, rows)
    table = jnp.where(index((NL, NLAT), 0) >= m, table, 0.0).astype(bf16)
    spot = index((1, NLAT), 1)
    x = 12 * (spot & 31) + X_SUB * ((spot >> 5) & 3) + (spot >> 7)
    columns = pick(index((NLAT, NLAT), 0) == x)
    out[0] = dot(table, columns).astype(bf16)
    spot = index((NLAT, 1), 0)
    row = 24 * (spot & 31) + 12 + X_SUB * ((spot >> 5) & 3) + (spot >> 7)
    chosen = pick(index((NLAT, LAT_DEV * 24), 1) == row)
    table = dot(chosen, rows)
    out[1] = jnp.where(index((NLAT, NL), 1) >= m, table, 0.0).astype(bf16)


def legendre_kernel(place, coeffs, tables_h, others_h, gain, out, rows, tables, others, sems):
    copies = [
        pltpu.make_async_copy(tables_h.at[0], tables.at[0], sems.at[0]),
        pltpu.make_async_copy(others_h.at[0], others.at[0], sems.at[1]),
        pltpu.make_async_copy(tables_h.at[1], tables.at[1], sems.at[2]),
        pltpu.make_async_copy(others_h.at[1], others.at[1], sems.at[3]),
    ]
    for copy in copies:
        copy.start()
    core = place[1]

    def swapped(pair):
        return jnp.where(core == 0, pair[0], pair[1]), jnp.where(core == 0, pair[1], pair[0])

    rows[...] = coeffs[...].astype(f32)
    blocks = [
        [rows[pl.ds(4 * k + n, LAT_DEV, stride=32), :] for n in range(4)] for k in range(PAIRS)
    ]
    modes = []
    for h in range(2):
        stack = []
        for xx in range(X_SUB):
            for xg in range(XG):
                parts = [
                    blocks[2 * xg + cq][2 * h + r][:, C_SUB * xx : C_SUB * (xx + 1)]
                    for r in range(2)
                    for cq in range(2)
                ]
                stack.append(jnp.concatenate(parts, axis=1))
        modes.append(jnp.concatenate(stack, axis=0))
    half = jnp.where(core == 0, gain[:, 0:64], gain[:, 64:128])
    gains = jnp.concatenate([half, half], axis=1)
    fourier = [f.astype(bf16) for f in swapped(modes)]
    for copy in copies[0:2]:
        copy.wait()
    filtered = [(dot(t[0], f) * gains).astype(bf16) for t, f in zip((tables, others), fourier)]
    for copy in copies[2:4]:
        copy.wait()
    results = [dot(t[1], f) for t, f in zip((tables, others), filtered)]
    results = swapped(results)
    for k in range(PAIRS):
        xg, cq = k // 2, k % 2
        for h in range(2):
            for r in range(2):
                first = 64 * r + C_SUB * cq
                parts = [
                    results[h][32 * (XG * xx + xg) : 32 * (XG * xx + xg + 1), first : first + C_SUB]
                    for xx in range(X_SUB)
                ]
                parts.append(jnp.zeros((LAT_DEV, C_SUB), f32))
                rows[pl.ds(4 * k + 2 * h + r, LAT_DEV, stride=32), :] = jnp.concatenate(parts, axis=1)
    out[...] = rows[...].astype(bf16)


def inverse_kernel(coeffs, table, out):
    g = dot(table[...], coeffs[0:ROWS, :])
    for j in range(LON_DEV):
        main = g[Y_MAIN * j : Y_MAIN * (j + 1), 0:96]
        first = LON_DEV * Y_MAIN + Y_EXT * j
        extra = g[first : first + Y_EXT]
        parts = [extra[:, C_SUB * xx : C_SUB * (xx + 1)] for xx in range(X_SUB)]
        out[j] = jnp.concatenate([main, jnp.concatenate(parts, axis=0)], axis=1).astype(bf16)


def grid_kernel(pieces, out):
    for xg in range(XG):
        blocks = [pieces[owner(xg, cg)].astype(f32) for cg in range(CG)]
        for xx in range(X_SUB):
            main = [b[:, C_SUB * xx : C_SUB * (xx + 1)] for b in blocks]
            extra = [b[Y_EXT * xx : Y_EXT * (xx + 1), 96:128] for b in blocks]
            out[X_SUB * xg + xx, 0:Y_MAIN, :] = jnp.concatenate(main, axis=1)
            out[X_SUB * xg + xx, Y_MAIN:, :] = jnp.concatenate(extra, axis=1)[0 : Y_DEV - Y_MAIN]


def call(
    kernel, shape, dtype, scratch=(), smem=0, space=pltpu.VMEM, far=(), flops=0, moved=0, limit=VMEM
):
    outs = [jax.ShapeDtypeStruct(s, dtype) for s in (shape if isinstance(shape, list) else [shape])]
    places = [pl.BlockSpec(memory_space=pltpu.VMEM) for _ in outs]
    single = not isinstance(shape, list)

    def run(*args):
        specs = [
            pl.BlockSpec(memory_space=pltpu.SMEM if k < smem else pltpu.HBM if k in far else space)
            for k in range(len(args))
        ]
        return pl.pallas_call(
            kernel,
            out_shape=outs[0] if single else outs,
            in_specs=specs,
            out_specs=places[0] if single else places,
            scratch_shapes=list(scratch),
            compiler_params=pltpu.CompilerParams(vmem_limit_bytes=limit),
            cost_estimate=pl.CostEstimate(flops=flops, bytes_accessed=moved, transcendentals=0),
        )(*args)

    return run


def arrange(first, second):
    shape = pltpu.VMEM((12, M_DEV, NL), bf16)
    rows = pltpu.VMEM((3, M_DEV * 24, 128), f32)
    return call(
        arrange_kernel,
        (LAT_DEV, 24, NL),
        bf16,
        (shape, shape, rows, pltpu.SemaphoreType.DMA((2,))),
        space=pltpu.HBM,
        limit=NETWORK_VMEM,
    )(first, second)


def on_device(
    saved, cotangent, w_in, b_in, w_mid, b_mid, w_out, spectral_gain, basis_in, basis_out
):
    forward, back = zonal_tables()
    bases = arrange(jnp.transpose(basis_in, (2, 1, 0)), basis_out)
    bases, saved = lax.optimization_barrier((bases, saved))
    bases = lax.all_to_all(bases, "lat", 0, 0, tiled=True)
    z_hi = lax.axis_index("z_hi").astype(jnp.int32).reshape(1)
    weights = (w_in, b_in.reshape(1, -1), w_mid, b_mid.reshape(1, -1), w_out)
    held = [pltpu.VMEM(a.shape, a.dtype) for a in (saved, cotangent) + weights]
    pad = pltpu.VMEM((X_DEV, Y_PAD, CHAN), bf16)
    kept, sent = call(
        network_kernel,
        [(PAIRS, Y_MAIN, 128), (PAIRS, Y_MAIN, 128)],
        bf16,
        held + [pad, pad, pltpu.SemaphoreType.DMA((7,))],
        smem=1,
        space=pltpu.HBM,
        flops=1_700_000_000,
        moved=4_000_000,
        limit=NETWORK_VMEM,
    )(z_hi, saved, cotangent, *weights)
    sent = lax.ppermute(sent, "z_hi", [(0, 1), (1, 0)])
    pieces = call(join_kernel, (PAIRS, 2, Y_MAIN, 128), bf16)(kept, sent)
    bases, pieces = lax.optimization_barrier((bases, pieces))
    pieces = lax.all_to_all(pieces, ("x", "core"), 0, 0, tiled=True)
    pieces, bases = lax.optimization_barrier((pieces, bases))
    mode = M_DEV * lax.axis_index(LON) + lax.axis_index("lat")
    place = jnp.stack([mode, lax.axis_index("core")]).astype(jnp.int32)
    tables = call(bases_kernel, (2, NL, NLAT), bf16, smem=1, flops=600_000_000, moved=3_000_000)(
        place, bases
    )
    others = lax.ppermute(tables, "core", [(0, 1), (1, 0)])
    coeffs = call(zonal_kernel, (2 * DEVS, 128), bf16, smem=1, flops=300_000_000)(
        z_hi, pieces, jnp.asarray(forward)
    )
    coeffs = lax.all_to_all(coeffs.reshape(DEVS // 2, 4, 128), ("lat", "x", "z_hi"), 0, 0, tiled=True)
    coeffs = call(
        legendre_kernel,
        (2 * DEVS, 128),
        bf16,
        (
            pltpu.VMEM((2 * DEVS, 128), f32),
            pltpu.VMEM((2, NL, NLAT), bf16),
            pltpu.VMEM((2, NL, NLAT), bf16),
            pltpu.SemaphoreType.DMA((4,)),
        ),
        smem=1,
        far=(2, 3),
        flops=200_000_000,
    )(place, coeffs.reshape(2 * DEVS, 128), tables, others, spectral_gain)
    coeffs = lax.all_to_all(coeffs.reshape(DEVS // 2, 4, 128), ("lat", "x", "z_hi"), 0, 0, tiled=True)
    pieces = call(inverse_kernel, (LON_DEV, Y_MAIN, 128), bf16, flops=300_000_000)(
        coeffs.reshape(2 * DEVS, 128), jnp.asarray(back)
    )
    pieces = lax.all_to_all(pieces, LON, 0, 0, tiled=True)
    return call(grid_kernel, (X_DEV, Y_DEV, CHAN), f32)(pieces)


def solution(mesh):
    grid = P("lat", LON, None)
    placed = (grid, grid, P(), P(), P(), P(), P(), P(), P(None, LON, "lat"), grid)
    fine = Mesh(mesh.devices.reshape(LAT_DEV, XG, 2, 2), ("lat",) + LON)
    return jax.shard_map(on_device, mesh=fine, in_specs=placed, out_specs=grid, check_vma=False)
```

```python
import numpy as np
import jax
import jax.numpy as jnp
from jax import lax
from jax.experimental import pallas as pl
from jax.experimental.pallas import tpu as pltpu
from jax.sharding import Mesh, PartitionSpec as P

bf16 = jnp.bfloat16
f32 = jnp.float32

LAT_DEV, LON_DEV = 32, 16
PAIRS = LON_DEV // 2
X_DEV, Y_DEV = 12, 90
Y_PAD = 96
Y_MAIN, Y_EXT = 72, 24
NLAT, NLON, NM, NL, CHAN = 384, 1440, 368, 384, 128
M_DEV = 23
X_SUB, C_SUB = 3, 32
CG = CHAN // C_SUB
XG = X_DEV // X_SUB
DEVS = LAT_DEV * LON_DEV
ROWS = 2 * NM
LON = ("pair", "core")
VMEM = 16 * 1024 * 1024
NETWORK_VMEM = 59 * 1024 * 1024


def zonal_tables():
    order = (M_DEV * np.arange(LON_DEV)[None, :] + np.arange(M_DEV)[:, None]).reshape(-1)
    turns = (order[:, None] * np.arange(NLON)[None, :]) % NLON
    angles = turns.astype(np.float64) * (2.0 * np.pi / NLON)
    table = np.stack([np.cos(angles), -np.sin(angles)], 1).reshape(ROWS, NLON)
    weight = np.where(order == 0, 1.0, 2.0) / NLON
    back = table * np.repeat(weight, 2)[:, None]

    def split_y(t):
        t = np.pad(t.reshape(ROWS, LON_DEV, Y_DEV), ((0, 0), (0, 0), (0, Y_PAD - Y_DEV)))
        main = t[:, :, :Y_MAIN].reshape(ROWS, LON_DEV * Y_MAIN)
        extra = t[:, :, Y_MAIN:].reshape(ROWS, LON_DEV * Y_EXT)
        return np.concatenate([main, extra], 1)

    return (
        np.asarray(split_y(table), dtype=jnp.bfloat16),
        np.ascontiguousarray(split_y(back).T).astype(jnp.bfloat16),
    )


def owner(xg, cg):
    return CG * xg + 2 * (cg % 2) + cg // 2


def dot(a, b):
    return lax.dot_general(a, b, (((1,), (0,)), ((), ())), preferred_element_type=f32)


def dot_t(a, b):
    return lax.dot_general(a, b, (((1,), (1,)), ((), ())), preferred_element_type=f32)


def sigmoid(v):
    return 0.5 * jnp.tanh(0.5 * v) + 0.5


def arrange_kernel(first_h, second_h, out, first, second, rows, sems):
    copies = [
        pltpu.make_async_copy(first_h, first, sems.at[0]),
        pltpu.make_async_copy(second_h, second, sems.at[1]),
    ]
    for copy in copies:
        copy.start()
    out[M_DEV:] = jnp.zeros((LAT_DEV - M_DEV, 24, NL), bf16)
    for half, source in enumerate((first, second)):
        copies[half].wait()
        for k in range(12):
            block = source[k].astype(f32)
            for t in range(3):
                rows[t, pl.ds(12 * half + k, M_DEV, stride=24), :] = block[:, 128 * t : 128 * (t + 1)]
    for m in range(M_DEV):
        for t in range(3):
            out[m, :, 128 * t : 128 * (t + 1)] = rows[t, 24 * m : 24 * (m + 1), :].astype(bf16)


def network_kernel(
    saved_h, cotan_h, w_in_h, b_in_h, w_mid_h, b_mid_h, w_out_h, out,
    saved, cotan, w_in, b_in, w_mid, b_mid, w_out, rows_s, rows_c, sems,
):
    pairs = (
        (saved_h, saved), (w_in_h, w_in), (b_in_h, b_in), (w_mid_h, w_mid),
        (b_mid_h, b_mid), (cotan_h, cotan), (w_out_h, w_out),
    )
    copies = [pltpu.make_async_copy(a, b, sems.at[k]) for k, (a, b) in enumerate(pairs)]
    for copy in copies:
        copy.start()
    got = dict(zip(("saved", "w_in", "b_in", "w_mid", "b_mid", "cotan", "w_out"), copies))
    edge = jnp.zeros((X_DEV, 16, CHAN), bf16)
    rows_s[:, Y_PAD - 16 :, :] = edge
    rows_c[:, Y_PAD - 16 :, :] = edge
    got["saved"].wait()
    for x in range(X_DEV):
        rows_s[x, 0:Y_DEV, :] = saved[x]
    got["w_in"].wait()
    got["b_in"].wait()
    for xg in range(XG):
        s = rows_s[X_SUB * xg : X_SUB * (xg + 1)].reshape(X_SUB * Y_PAD, CHAN)
        first = dot(s, w_in[...]) + b_in[...]
        sig = sigmoid(first)
        act = first * sig
        slope_one = sig + act * (1.0 - sig)
        if xg == 0:
            got["w_mid"].wait()
            got["b_mid"].wait()
        second = dot(act.astype(bf16), w_mid[...]) + b_mid[...]
        sig = sigmoid(second)
        slope_two = sig * (1.0 + second * (1.0 - sig))
        if xg == 0:
            got["cotan"].wait()
            got["w_out"].wait()
            for x in range(X_DEV):
                rows_c[x, 0:Y_DEV, :] = cotan[x]
        c = rows_c[X_SUB * xg : X_SUB * (xg + 1)].reshape(X_SUB * Y_PAD, CHAN)
        back_two = (dot_t(c, w_out[...]) * slope_two).astype(bf16)
        back_one = (dot_t(back_two, w_mid[...]) * slope_one).astype(bf16)
        grad = c.astype(f32) + dot_t(back_one, w_in[...])
        grad = grad.reshape(X_SUB, Y_PAD, CHAN)
        for cg in range(CG):
            parts = [grad[xx][:, C_SUB * cg : C_SUB * (cg + 1)] for xx in range(X_SUB)]
            parts = [p[0:Y_MAIN] for p in parts] + [
                jnp.concatenate([p[Y_MAIN:] for p in parts], axis=0)
            ]
            out[owner(xg, cg)] = jnp.concatenate(parts, axis=1).astype(bf16)


def zonal_kernel(circles, table, out):
    main, extra = [], []
    for j in range(LON_DEV):
        piece = circles[j].astype(f32)
        main.append(piece)
        parts = [piece[Y_EXT * xx : Y_EXT * (xx + 1), 96:128] for xx in range(X_SUB)]
        extra.append(jnp.concatenate(parts + [jnp.zeros((Y_EXT, C_SUB), f32)], axis=1))
    g = jnp.concatenate(main + extra, axis=0).astype(bf16)
    out[0:ROWS, :] = dot(table[...], g).astype(bf16)
    out[ROWS:, :] = jnp.zeros((2 * DEVS - ROWS, 128), bf16)


def bases_kernel(place, bases, out):
    m = place[0]

    def index(shape, axis):
        return lax.broadcasted_iota(jnp.int32, shape, axis)

    def pick(mask):
        return jnp.where(mask, 1.0, 0.0).astype(bf16)

    rows = bases[...].astype(f32).reshape(LAT_DEV * 24, NL).astype(bf16)
    wave = index((NL, 1), 0)
    tile = lax.shift_right_logical(wave * 5462, 16)
    chosen = pick(index((NL, LAT_DEV * 24), 1) == wave + 12 * tile)
    table = dot(chosen, rows)
    table = jnp.where(index((NL, NLAT), 0) >= m, table, 0.0).astype(bf16)
    spot = index((1, NLAT), 1)
    x = 12 * (spot & 31) + X_SUB * ((spot >> 5) & 3) + (spot >> 7)
    columns = pick(index((NLAT, NLAT), 0) == x)
    out[0] = dot(table, columns).astype(bf16)
    spot = index((NLAT, 1), 0)
    row = 24 * (spot & 31) + 12 + X_SUB * ((spot >> 5) & 3) + (spot >> 7)
    chosen = pick(index((NLAT, LAT_DEV * 24), 1) == row)
    table = dot(chosen, rows)
    out[1] = jnp.where(index((NLAT, NL), 1) >= m, table, 0.0).astype(bf16)


def legendre_kernel(place, coeffs, tables_h, others_h, gain, out, rows, tables, others, sems):
    copies = [
        pltpu.make_async_copy(tables_h.at[0], tables.at[0], sems.at[0]),
        pltpu.make_async_copy(others_h.at[0], others.at[0], sems.at[1]),
        pltpu.make_async_copy(tables_h.at[1], tables.at[1], sems.at[2]),
        pltpu.make_async_copy(others_h.at[1], others.at[1], sems.at[3]),
    ]
    for copy in copies:
        copy.start()
    core = place[1]

    def swapped(pair):
        return jnp.where(core == 0, pair[0], pair[1]), jnp.where(core == 0, pair[1], pair[0])

    rows[...] = coeffs[...].astype(f32)
    blocks = [
        [rows[pl.ds(4 * k + n, LAT_DEV, stride=32), :] for n in range(4)] for k in range(PAIRS)
    ]
    modes = []
    for h in range(2):
        stack = []
        for xx in range(X_SUB):
            for xg in range(XG):
                parts = [
                    blocks[2 * xg + cq][2 * h + r][:, C_SUB * xx : C_SUB * (xx + 1)]
                    for r in range(2)
                    for cq in range(2)
                ]
                stack.append(jnp.concatenate(parts, axis=1))
        modes.append(jnp.concatenate(stack, axis=0))
    half = jnp.where(core == 0, gain[:, 0:64], gain[:, 64:128])
    gains = jnp.concatenate([half, half], axis=1)
    fourier = [f.astype(bf16) for f in swapped(modes)]
    for copy in copies[0:2]:
        copy.wait()
    filtered = [(dot(t[0], f) * gains).astype(bf16) for t, f in zip((tables, others), fourier)]
    for copy in copies[2:4]:
        copy.wait()
    results = [dot(t[1], f) for t, f in zip((tables, others), filtered)]
    results = swapped(results)
    for k in range(PAIRS):
        xg, cq = k // 2, k % 2
        for h in range(2):
            for r in range(2):
                first = 64 * r + C_SUB * cq
                parts = [
                    results[h][32 * (XG * xx + xg) : 32 * (XG * xx + xg + 1), first : first + C_SUB]
                    for xx in range(X_SUB)
                ]
                parts.append(jnp.zeros((LAT_DEV, C_SUB), f32))
                rows[pl.ds(4 * k + 2 * h + r, LAT_DEV, stride=32), :] = jnp.concatenate(parts, axis=1)
    out[...] = rows[...].astype(bf16)


def inverse_kernel(coeffs, table, out):
    g = dot(table[...], coeffs[0:ROWS, :])
    for j in range(LON_DEV):
        main = g[Y_MAIN * j : Y_MAIN * (j + 1), 0:96]
        first = LON_DEV * Y_MAIN + Y_EXT * j
        extra = g[first : first + Y_EXT]
        parts = [extra[:, C_SUB * xx : C_SUB * (xx + 1)] for xx in range(X_SUB)]
        out[j] = jnp.concatenate([main, jnp.concatenate(parts, axis=0)], axis=1).astype(bf16)


def grid_kernel(pieces, out):
    for xg in range(XG):
        blocks = [pieces[owner(xg, cg)].astype(f32) for cg in range(CG)]
        for xx in range(X_SUB):
            main = [b[:, C_SUB * xx : C_SUB * (xx + 1)] for b in blocks]
            extra = [b[Y_EXT * xx : Y_EXT * (xx + 1), 96:128] for b in blocks]
            out[X_SUB * xg + xx, 0:Y_MAIN, :] = jnp.concatenate(main, axis=1)
            out[X_SUB * xg + xx, Y_MAIN:, :] = jnp.concatenate(extra, axis=1)[0 : Y_DEV - Y_MAIN]


def call(
    kernel, shape, dtype, scratch=(), smem=0, space=pltpu.VMEM, far=(), flops=0, moved=0, limit=VMEM
):
    outs = [jax.ShapeDtypeStruct(s, dtype) for s in (shape if isinstance(shape, list) else [shape])]
    places = [pl.BlockSpec(memory_space=pltpu.VMEM) for _ in outs]
    single = not isinstance(shape, list)

    def run(*args):
        specs = [
            pl.BlockSpec(memory_space=pltpu.SMEM if k < smem else pltpu.HBM if k in far else space)
            for k in range(len(args))
        ]
        return pl.pallas_call(
            kernel,
            out_shape=outs[0] if single else outs,
            in_specs=specs,
            out_specs=places[0] if single else places,
            scratch_shapes=list(scratch),
            compiler_params=pltpu.CompilerParams(vmem_limit_bytes=limit),
            cost_estimate=pl.CostEstimate(flops=flops, bytes_accessed=moved, transcendentals=0),
        )(*args)

    return run


def arrange(first, second):
    shape = pltpu.VMEM((12, M_DEV, NL), bf16)
    rows = pltpu.VMEM((3, M_DEV * 24, 128), f32)
    return call(
        arrange_kernel,
        (LAT_DEV, 24, NL),
        bf16,
        (shape, shape, rows, pltpu.SemaphoreType.DMA((2,))),
        space=pltpu.HBM,
        limit=NETWORK_VMEM,
    )(first, second)


def on_device(
    saved, cotangent, w_in, b_in, w_mid, b_mid, w_out, spectral_gain, basis_in, basis_out
):
    forward, back = zonal_tables()
    bases = arrange(jnp.transpose(basis_in, (2, 1, 0)), basis_out)
    bases, saved = lax.optimization_barrier((bases, saved))
    bases = lax.all_to_all(bases, "lat", 0, 0, tiled=True)
    weights = (w_in, b_in.reshape(1, -1), w_mid, b_mid.reshape(1, -1), w_out)
    held = [pltpu.VMEM(a.shape, a.dtype) for a in (saved, cotangent) + weights]
    pad = pltpu.VMEM((X_DEV, Y_PAD, CHAN), bf16)
    pieces = call(
        network_kernel,
        (LON_DEV, Y_MAIN, 128),
        bf16,
        held + [pad, pad, pltpu.SemaphoreType.DMA((7,))],
        space=pltpu.HBM,
        flops=1_700_000_000,
        moved=4_000_000,
        limit=NETWORK_VMEM,
    )(saved, cotangent, *weights)
    bases, pieces = lax.optimization_barrier((bases, pieces))
    pieces = lax.all_to_all(pieces, LON, 0, 0, tiled=True)
    mode = M_DEV * lax.axis_index(LON) + lax.axis_index("lat")
    place = jnp.stack([mode, lax.axis_index("core")]).astype(jnp.int32)
    tables = call(bases_kernel, (2, NL, NLAT), bf16, smem=1, flops=600_000_000, moved=3_000_000)(
        place, bases
    )
    others = lax.ppermute(tables, "core", [(0, 1), (1, 0)])
    coeffs = call(zonal_kernel, (2 * DEVS, 128), bf16, flops=300_000_000)(
        pieces, jnp.asarray(forward)
    )
    coeffs = lax.all_to_all(coeffs.reshape(DEVS // 2, 4, 128), ("lat", "pair"), 0, 0, tiled=True)
    coeffs = call(
        legendre_kernel,
        (2 * DEVS, 128),
        bf16,
        (
            pltpu.VMEM((2 * DEVS, 128), f32),
            pltpu.VMEM((2, NL, NLAT), bf16),
            pltpu.VMEM((2, NL, NLAT), bf16),
            pltpu.SemaphoreType.DMA((4,)),
        ),
        smem=1,
        far=(2, 3),
        flops=200_000_000,
    )(place, coeffs.reshape(2 * DEVS, 128), tables, others, spectral_gain)
    coeffs = lax.all_to_all(coeffs.reshape(DEVS // 2, 4, 128), ("lat", "pair"), 0, 0, tiled=True)
    pieces = call(inverse_kernel, (LON_DEV, Y_MAIN, 128), bf16, flops=300_000_000)(
        coeffs.reshape(2 * DEVS, 128), jnp.asarray(back)
    )
    pieces = lax.all_to_all(pieces, LON, 0, 0, tiled=True)
    return call(grid_kernel, (X_DEV, Y_DEV, CHAN), f32)(pieces)


def solution(mesh):
    grid = P("lat", LON, None)
    placed = (grid, grid, P(), P(), P(), P(), P(), P(), P(None, LON, "lat"), grid)
    fine = Mesh(mesh.devices.reshape(LAT_DEV, PAIRS, 2), ("lat",) + LON)
    return jax.shard_map(on_device, mesh=fine, in_specs=placed, out_specs=grid, check_vma=False)
```

```python
import numpy as np
import jax
import jax.numpy as jnp
from jax import lax
from jax.experimental import pallas as pl
from jax.experimental.pallas import tpu as pltpu
from jax.sharding import Mesh, PartitionSpec as P

bf16 = jnp.bfloat16
f32 = jnp.float32

LAT_DEV, LON_DEV = 32, 16
QUADS = 4
X_DEV, Y_DEV = 12, 90
Y_PAD = 96
Y_MAIN, Y_EXT = 72, 24
NLAT, NLON, NM, NL, CHAN = 384, 1440, 368, 384, 128
M_DEV = 23
X_SUB, C_SUB = 3, 32
CG = CHAN // C_SUB
XG = X_DEV // X_SUB
DEVS = LAT_DEV * LON_DEV
ROWS = 2 * NM
LON = ("x_hi", "x_lo", "z_hi", "core")
LONG = ("x_lo", "z_hi", "lat")
KEPT = 192
VMEM = 16 * 1024 * 1024
NETWORK_VMEM = 59 * 1024 * 1024


def zonal_tables():
    q, i, e = np.meshgrid(np.arange(4), np.arange(M_DEV), np.arange(4), indexing="ij")
    order = (M_DEV * (8 * (e // 2) + 2 * q + e % 2) + i).reshape(-1)
    turns = (order[:, None] * np.arange(NLON)[None, :]) % NLON
    angles = turns.astype(np.float64) * (2.0 * np.pi / NLON)
    table = np.stack([np.cos(angles), -np.sin(angles)], 1).reshape(ROWS, NLON)
    weight = np.where(order == 0, 1.0, 2.0) / NLON
    back = table * np.repeat(weight, 2)[:, None]

    def split_y(t):
        t = np.pad(t.reshape(QUADS, ROWS // QUADS, NLON), ((0, 0), (0, KEPT - ROWS // QUADS), (0, 0)))
        t = t.reshape(QUADS * KEPT, LON_DEV, Y_DEV)
        t = np.pad(t, ((0, 0), (0, 0), (0, Y_PAD - Y_DEV)))
        main = t[:, :, :Y_MAIN].reshape(QUADS * KEPT, LON_DEV * Y_MAIN)
        extra = t[:, :, Y_MAIN:].reshape(QUADS * KEPT, LON_DEV * Y_EXT)
        return np.concatenate([main, extra], 1)

    return (
        np.asarray(split_y(table), dtype=jnp.bfloat16),
        np.ascontiguousarray(split_y(back).T).astype(jnp.bfloat16),
    )


def owner(xg, cg):
    return 8 * (cg % 2) + 2 * xg + cg // 2


def dot(a, b):
    return lax.dot_general(a, b, (((1,), (0,)), ((), ())), preferred_element_type=f32)


def dot_t(a, b):
    return lax.dot_general(a, b, (((1,), (1,)), ((), ())), preferred_element_type=f32)


def sigmoid(v):
    return 0.5 * jnp.tanh(0.5 * v) + 0.5


def arrange_kernel(first_h, second_h, out, first, second, rows, sems):
    copies = [
        pltpu.make_async_copy(first_h, first, sems.at[0]),
        pltpu.make_async_copy(second_h, second, sems.at[1]),
    ]
    for copy in copies:
        copy.start()
    out[M_DEV:] = jnp.zeros((LAT_DEV - M_DEV, 24, NL), bf16)
    for half, source in enumerate((first, second)):
        copies[half].wait()
        for k in range(12):
            block = source[k].astype(f32)
            for t in range(3):
                rows[t, pl.ds(12 * half + k, M_DEV, stride=24), :] = block[:, 128 * t : 128 * (t + 1)]
    for m in range(M_DEV):
        for t in range(3):
            out[m, :, 128 * t : 128 * (t + 1)] = rows[t, 24 * m : 24 * (m + 1), :].astype(bf16)


def network_kernel(
    saved_h, cotan_h, w_in_h, b_in_h, w_mid_h, b_mid_h, w_out_h, out,
    saved, cotan, w_in, b_in, w_mid, b_mid, w_out, rows_s, rows_c, sems,
):
    pairs = (
        (saved_h, saved), (w_in_h, w_in), (b_in_h, b_in), (w_mid_h, w_mid),
        (b_mid_h, b_mid), (cotan_h, cotan), (w_out_h, w_out),
    )
    copies = [pltpu.make_async_copy(a, b, sems.at[k]) for k, (a, b) in enumerate(pairs)]
    for copy in copies:
        copy.start()
    got = dict(zip(("saved", "w_in", "b_in", "w_mid", "b_mid", "cotan", "w_out"), copies))
    edge = jnp.zeros((X_DEV, 16, CHAN), bf16)
    rows_s[:, Y_PAD - 16 :, :] = edge
    rows_c[:, Y_PAD - 16 :, :] = edge
    got["saved"].wait()
    for x in range(X_DEV):
        rows_s[x, 0:Y_DEV, :] = saved[x]
    got["w_in"].wait()
    got["b_in"].wait()
    for xg in range(XG):
        s = rows_s[X_SUB * xg : X_SUB * (xg + 1)].reshape(X_SUB * Y_PAD, CHAN)
        first = dot(s, w_in[...]) + b_in[...]
        sig = sigmoid(first)
        act = first * sig
        slope_one = sig + act * (1.0 - sig)
        if xg == 0:
            got["w_mid"].wait()
            got["b_mid"].wait()
        second = dot(act.astype(bf16), w_mid[...]) + b_mid[...]
        sig = sigmoid(second)
        slope_two = sig * (1.0 + second * (1.0 - sig))
        if xg == 0:
            got["cotan"].wait()
            got["w_out"].wait()
            for x in range(X_DEV):
                rows_c[x, 0:Y_DEV, :] = cotan[x]
        c = rows_c[X_SUB * xg : X_SUB * (xg + 1)].reshape(X_SUB * Y_PAD, CHAN)
        back_two = (dot_t(c, w_out[...]) * slope_two).astype(bf16)
        back_one = (dot_t(back_two, w_mid[...]) * slope_one).astype(bf16)
        grad = c.astype(f32) + dot_t(back_one, w_in[...])
        grad = grad.reshape(X_SUB, Y_PAD, CHAN)
        for cg in range(CG):
            parts = [grad[xx][:, C_SUB * cg : C_SUB * (cg + 1)] for xx in range(X_SUB)]
            parts = [p[0:Y_MAIN] for p in parts] + [
                jnp.concatenate([p[Y_MAIN:] for p in parts], axis=0)
            ]
            out[owner(xg, cg)] = jnp.concatenate(parts, axis=1).astype(bf16)


def zonal_kernel(circles, table, out):
    main, extra = [], []
    for j in range(LON_DEV):
        piece = circles[j].astype(f32)
        main.append(piece)
        parts = [piece[Y_EXT * xx : Y_EXT * (xx + 1), 96:128] for xx in range(X_SUB)]
        extra.append(jnp.concatenate(parts + [jnp.zeros((Y_EXT, C_SUB), f32)], axis=1))
    g = jnp.concatenate(main + extra, axis=0).astype(bf16)
    spectrum = dot(table[...], g).astype(bf16)
    for q in range(QUADS):
        out[256 * q : 256 * q + KEPT, :] = spectrum[KEPT * q : KEPT * (q + 1)]
        out[256 * q + KEPT : 256 * (q + 1), :] = jnp.zeros((256 - KEPT, 128), bf16)


def bases_kernel(place, bases, out):
    m = place[0]

    def index(shape, axis):
        return lax.broadcasted_iota(jnp.int32, shape, axis)

    def pick(mask):
        return jnp.where(mask, 1.0, 0.0).astype(bf16)

    rows = bases[...].astype(f32).reshape(LAT_DEV * 24, NL).astype(bf16)
    wave = index((NL, 1), 0)
    tile = lax.shift_right_logical(wave * 5462, 16)
    chosen = pick(index((NL, LAT_DEV * 24), 1) == wave + 12 * tile)
    table = dot(chosen, rows)
    table = jnp.where(index((NL, NLAT), 0) >= m, table, 0.0).astype(bf16)
    spot = index((1, NLAT), 1)
    x = 12 * (spot & 31) + X_SUB * ((spot >> 5) & 3) + (spot >> 7)
    columns = pick(index((NLAT, NLAT), 0) == x)
    out[0] = dot(table, columns).astype(bf16)
    spot = index((NLAT, 1), 0)
    row = 24 * (spot & 31) + 12 + X_SUB * ((spot >> 5) & 3) + (spot >> 7)
    chosen = pick(index((NLAT, LAT_DEV * 24), 1) == row)
    table = dot(chosen, rows)
    out[1] = jnp.where(index((NLAT, NL), 1) >= m, table, 0.0).astype(bf16)


def legendre_kernel(place, coeffs, own, core_s, far_s, both_s, gain, out, rows, tables, sems):
    mine = place[1]
    copies = [
        pltpu.make_async_copy(source, tables.at[mine ^ d], sems.at[d])
        for d, source in enumerate((own, core_s, far_s, both_s))
    ]
    for copy in copies:
        copy.start()
    rows[...] = coeffs[...].astype(f32)
    fourier = []
    for e in range(4):
        blocks = [
            [rows[pl.ds(256 * xg + 2 * e + r, LAT_DEV, stride=8), :] for r in range(2)]
            for xg in range(XG)
        ]
        stack = []
        for xx in range(X_SUB):
            for xg in range(XG):
                parts = [blocks[xg][r][:, C_SUB * xx : C_SUB * (xx + 1)] for r in range(2)]
                stack.append(jnp.concatenate(parts, axis=1))
        fourier.append(jnp.concatenate(stack, axis=0).astype(bf16))
    quarter = [gain[:, C_SUB * cg : C_SUB * (cg + 1)] for cg in range(CG)]
    low = jnp.where(mine // 2 == 0, quarter[0], quarter[1])
    high = jnp.where(mine // 2 == 0, quarter[2], quarter[3])
    quarter = jnp.where(mine % 2 == 0, low, high)
    gains = jnp.concatenate([quarter, quarter], axis=1)
    for copy in copies:
        copy.wait()
    filtered = [(dot(tables[e, 0], fourier[e]) * gains).astype(bf16) for e in range(4)]
    results = [dot(tables[e, 1], filtered[e]) for e in range(4)]
    for xg in range(XG):
        for e in range(4):
            for r in range(2):
                parts = [
                    results[e][32 * (XG * xx + xg) : 32 * (XG * xx + xg + 1), C_SUB * r : C_SUB * (r + 1)]
                    for xx in range(X_SUB)
                ]
                parts.append(jnp.zeros((LAT_DEV, C_SUB), f32))
                rows[pl.ds(256 * xg + 2 * e + r, LAT_DEV, stride=8), :] = jnp.concatenate(parts, axis=1)
    out[...] = rows[...].astype(bf16)


def inverse_kernel(coeffs, table, out):
    z = jnp.concatenate([coeffs[256 * q : 256 * q + KEPT, :] for q in range(QUADS)], axis=0)
    g = dot(table[...], z)
    for j in range(LON_DEV):
        main = g[Y_MAIN * j : Y_MAIN * (j + 1), 0:96]
        first = LON_DEV * Y_MAIN + Y_EXT * j
        extra = g[first : first + Y_EXT]
        parts = [extra[:, C_SUB * xx : C_SUB * (xx + 1)] for xx in range(X_SUB)]
        out[j] = jnp.concatenate([main, jnp.concatenate(parts, axis=0)], axis=1).astype(bf16)


def grid_kernel(pieces, out):
    for xg in range(XG):
        blocks = [pieces[owner(xg, cg)].astype(f32) for cg in range(CG)]
        for xx in range(X_SUB):
            main = [b[:, C_SUB * xx : C_SUB * (xx + 1)] for b in blocks]
            extra = [b[Y_EXT * xx : Y_EXT * (xx + 1), 96:128] for b in blocks]
            out[X_SUB * xg + xx, 0:Y_MAIN, :] = jnp.concatenate(main, axis=1)
            out[X_SUB * xg + xx, Y_MAIN:, :] = jnp.concatenate(extra, axis=1)[0 : Y_DEV - Y_MAIN]


def call(
    kernel, shape, dtype, scratch=(), smem=0, space=pltpu.VMEM, far=(), flops=0, moved=0, limit=VMEM
):
    outs = [jax.ShapeDtypeStruct(s, dtype) for s in (shape if isinstance(shape, list) else [shape])]
    places = [pl.BlockSpec(memory_space=pltpu.VMEM) for _ in outs]
    single = not isinstance(shape, list)

    def run(*args):
        specs = [
            pl.BlockSpec(memory_space=pltpu.SMEM if k < smem else pltpu.HBM if k in far else space)
            for k in range(len(args))
        ]
        return pl.pallas_call(
            kernel,
            out_shape=outs[0] if single else outs,
            in_specs=specs,
            out_specs=places[0] if single else places,
            scratch_shapes=list(scratch),
            compiler_params=pltpu.CompilerParams(vmem_limit_bytes=limit),
            cost_estimate=pl.CostEstimate(flops=flops, bytes_accessed=moved, transcendentals=0),
        )(*args)

    return run


def arrange(first, second):
    shape = pltpu.VMEM((12, M_DEV, NL), bf16)
    rows = pltpu.VMEM((3, M_DEV * 24, 128), f32)
    return call(
        arrange_kernel,
        (LAT_DEV, 24, NL),
        bf16,
        (shape, shape, rows, pltpu.SemaphoreType.DMA((2,))),
        space=pltpu.HBM,
        limit=NETWORK_VMEM,
    )(first, second)


def on_device(
    saved, cotangent, w_in, b_in, w_mid, b_mid, w_out, spectral_gain, basis_in, basis_out
):
    forward, back = zonal_tables()
    bases = arrange(jnp.transpose(basis_in, (2, 1, 0)), basis_out)
    bases, saved = lax.optimization_barrier((bases, saved))
    bases = lax.all_to_all(bases, "lat", 0, 0, tiled=True)
    weights = (w_in, b_in.reshape(1, -1), w_mid, b_mid.reshape(1, -1), w_out)
    held = [pltpu.VMEM(a.shape, a.dtype) for a in (saved, cotangent) + weights]
    pad = pltpu.VMEM((X_DEV, Y_PAD, CHAN), bf16)
    pieces = call(
        network_kernel,
        (LON_DEV, Y_MAIN, 128),
        bf16,
        held + [pad, pad, pltpu.SemaphoreType.DMA((7,))],
        space=pltpu.HBM,
        flops=1_700_000_000,
        moved=4_000_000,
        limit=NETWORK_VMEM,
    )(saved, cotangent, *weights)
    bases, pieces = lax.optimization_barrier((bases, pieces))
    pieces = lax.all_to_all(pieces, LON, 0, 0, tiled=True)
    mode = M_DEV * lax.axis_index(LON) + lax.axis_index("lat")
    mine = 2 * lax.axis_index("x_hi") + lax.axis_index("core")
    place = jnp.stack([mode, mine]).astype(jnp.int32)
    tables = call(bases_kernel, (2, NL, NLAT), bf16, smem=1, flops=600_000_000, moved=3_000_000)(
        place, bases
    )
    swap = [(0, 1), (1, 0)]
    shared = (
        tables,
        lax.ppermute(tables, "core", swap),
        lax.ppermute(tables, "x_hi", swap),
        lax.ppermute(tables, ("x_hi", "core"), [(0, 3), (1, 2), (2, 1), (3, 0)]),
    )
    coeffs = call(zonal_kernel, (2 * DEVS, 128), bf16, flops=300_000_000)(
        pieces, jnp.asarray(forward)
    )
    coeffs = lax.all_to_all(coeffs.reshape(DEVS // 4, 8, 128), LONG, 0, 0, tiled=True)
    coeffs = call(
        legendre_kernel,
        (2 * DEVS, 128),
        bf16,
        (
            pltpu.VMEM((2 * DEVS, 128), f32),
            pltpu.VMEM((4, 2, NL, NLAT), bf16),
            pltpu.SemaphoreType.DMA((4,)),
        ),
        smem=1,
        far=(2, 3, 4, 5),
        flops=200_000_000,
    )(place, coeffs.reshape(2 * DEVS, 128), *shared, spectral_gain)
    coeffs, back = lax.optimization_barrier((coeffs, jnp.asarray(back)))
    coeffs = lax.all_to_all(coeffs.reshape(DEVS // 4, 8, 128), LONG, 0, 0, tiled=True)
    pieces = call(inverse_kernel, (LON_DEV, Y_MAIN, 128), bf16, flops=300_000_000)(
        coeffs.reshape(2 * DEVS, 128), back
    )
    pieces = lax.all_to_all(pieces, LON, 0, 0, tiled=True)
    return call(grid_kernel, (X_DEV, Y_DEV, CHAN), f32)(pieces)


def solution(mesh):
    grid = P("lat", LON, None)
    placed = (grid, grid, P(), P(), P(), P(), P(), P(), P(None, LON, "lat"), grid)
    fine = Mesh(mesh.devices.reshape(LAT_DEV, 2, 2, 2, 2), ("lat",) + LON)
    return jax.shard_map(on_device, mesh=fine, in_specs=placed, out_specs=grid, check_vma=False)
```

```python
import numpy as np
import jax
import jax.numpy as jnp
from jax import lax
from jax.experimental import pallas as pl
from jax.experimental.pallas import tpu as pltpu
from jax.sharding import Mesh, PartitionSpec as P

bf16 = jnp.bfloat16
f32 = jnp.float32

LAT_DEV, LON_DEV = 32, 16
QUADS = 4
X_DEV, Y_DEV = 12, 90
Y_PAD = 96
Y_MAIN, Y_EXT = 72, 24
NLAT, NLON, NM, NL, CHAN = 384, 1440, 368, 384, 128
M_DEV = 23
X_SUB, C_SUB = 3, 32
CG = CHAN // C_SUB
XG = X_DEV // X_SUB
DEVS = LAT_DEV * LON_DEV
ROWS = 2 * NM
LON = ("x_hi", "x_lo", "z_hi", "core")
LONG = ("x_lo", "z_hi", "lat")
KEPT = 192
VMEM = 16 * 1024 * 1024
NETWORK_VMEM = 59 * 1024 * 1024


def zonal_tables():
    q, i, e = np.meshgrid(np.arange(4), np.arange(M_DEV), np.arange(4), indexing="ij")
    order = (M_DEV * (8 * (e // 2) + 2 * q + e % 2) + i).reshape(-1)
    turns = (order[:, None] * np.arange(NLON)[None, :]) % NLON
    angles = turns.astype(np.float64) * (2.0 * np.pi / NLON)
    table = np.stack([np.cos(angles), -np.sin(angles)], 1).reshape(ROWS, NLON)
    weight = np.where(order == 0, 1.0, 2.0) / NLON
    back = table * np.repeat(weight, 2)[:, None]

    def split_y(t):
        t = np.pad(t.reshape(QUADS, ROWS // QUADS, NLON), ((0, 0), (0, KEPT - ROWS // QUADS), (0, 0)))
        t = t.reshape(QUADS * KEPT, LON_DEV, Y_DEV)
        t = np.pad(t, ((0, 0), (0, 0), (0, Y_PAD - Y_DEV)))
        main = t[:, :, :Y_MAIN].reshape(QUADS * KEPT, LON_DEV * Y_MAIN)
        extra = t[:, :, Y_MAIN:].reshape(QUADS * KEPT, LON_DEV * Y_EXT)
        return np.concatenate([main, extra], 1)

    return (
        np.asarray(split_y(table), dtype=jnp.bfloat16),
        np.ascontiguousarray(split_y(back).T).astype(jnp.bfloat16),
    )


def owner(xg, cg):
    return 8 * (cg % 2) + 2 * xg + cg // 2


def dot(a, b):
    return lax.dot_general(a, b, (((1,), (0,)), ((), ())), preferred_element_type=f32)


def dot_t(a, b):
    return lax.dot_general(a, b, (((1,), (1,)), ((), ())), preferred_element_type=f32)


def sigmoid(v):
    return 0.5 * jnp.tanh(0.5 * v) + 0.5


def arrange_kernel(first_h, second_h, out, first, second, rows, sems):
    copies = [
        pltpu.make_async_copy(first_h, first, sems.at[0]),
        pltpu.make_async_copy(second_h, second, sems.at[1]),
    ]
    for copy in copies:
        copy.start()
    out[M_DEV:] = jnp.zeros((LAT_DEV - M_DEV, 24, NL), bf16)
    for half, source in enumerate((first, second)):
        copies[half].wait()
        for k in range(12):
            block = source[k].astype(f32)
            for t in range(3):
                rows[t, pl.ds(12 * half + k, M_DEV, stride=24), :] = block[:, 128 * t : 128 * (t + 1)]
    for m in range(M_DEV):
        for t in range(3):
            out[m, :, 128 * t : 128 * (t + 1)] = rows[t, 24 * m : 24 * (m + 1), :].astype(bf16)


def network_kernel(
    saved_h, cotan_h, w_in_h, b_in_h, w_mid_h, b_mid_h, w_out_h, out,
    saved, cotan, w_in, b_in, w_mid, b_mid, w_out, rows_s, rows_c, sems,
):
    pairs = (
        (saved_h, saved), (w_in_h, w_in), (b_in_h, b_in), (w_mid_h, w_mid),
        (b_mid_h, b_mid), (cotan_h, cotan), (w_out_h, w_out),
    )
    copies = [pltpu.make_async_copy(a, b, sems.at[k]) for k, (a, b) in enumerate(pairs)]
    for copy in copies:
        copy.start()
    got = dict(zip(("saved", "w_in", "b_in", "w_mid", "b_mid", "cotan", "w_out"), copies))
    edge = jnp.zeros((X_DEV, 16, CHAN), bf16)
    rows_s[:, Y_PAD - 16 :, :] = edge
    rows_c[:, Y_PAD - 16 :, :] = edge
    got["saved"].wait()
    for x in range(X_DEV):
        rows_s[x, 0:Y_DEV, :] = saved[x]
    got["w_in"].wait()
    got["b_in"].wait()
    for xg in range(XG):
        s = rows_s[X_SUB * xg : X_SUB * (xg + 1)].reshape(X_SUB * Y_PAD, CHAN)
        first = dot(s, w_in[...]) + b_in[...]
        sig = sigmoid(first)
        act = first * sig
        slope_one = sig + act * (1.0 - sig)
        if xg == 0:
            got["w_mid"].wait()
            got["b_mid"].wait()
        second = dot(act.astype(bf16), w_mid[...]) + b_mid[...]
        sig = sigmoid(second)
        slope_two = sig * (1.0 + second * (1.0 - sig))
        if xg == 0:
            got["cotan"].wait()
            got["w_out"].wait()
            for x in range(X_DEV):
                rows_c[x, 0:Y_DEV, :] = cotan[x]
        c = rows_c[X_SUB * xg : X_SUB * (xg + 1)].reshape(X_SUB * Y_PAD, CHAN)
        back_two = (dot_t(c, w_out[...]) * slope_two).astype(bf16)
        back_one = (dot_t(back_two, w_mid[...]) * slope_one).astype(bf16)
        grad = c.astype(f32) + dot_t(back_one, w_in[...])
        grad = grad.reshape(X_SUB, Y_PAD, CHAN)
        for cg in range(CG):
            parts = [grad[xx][:, C_SUB * cg : C_SUB * (cg + 1)] for xx in range(X_SUB)]
            parts = [p[0:Y_MAIN] for p in parts] + [
                jnp.concatenate([p[Y_MAIN:] for p in parts], axis=0)
            ]
            out[owner(xg, cg)] = jnp.concatenate(parts, axis=1).astype(bf16)


def zonal_kernel(circles, table, out):
    main, extra = [], []
    for j in range(LON_DEV):
        piece = circles[j].astype(f32)
        main.append(piece)
        parts = [piece[Y_EXT * xx : Y_EXT * (xx + 1), 96:128] for xx in range(X_SUB)]
        extra.append(jnp.concatenate(parts + [jnp.zeros((Y_EXT, C_SUB), f32)], axis=1))
    g = jnp.concatenate(main + extra, axis=0).astype(bf16)
    spectrum = dot(table[...], g).astype(bf16)
    for q in range(QUADS):
        out[256 * q : 256 * q + KEPT, :] = spectrum[KEPT * q : KEPT * (q + 1)]
        out[256 * q + KEPT : 256 * (q + 1), :] = jnp.zeros((256 - KEPT, 128), bf16)


def bases_kernel(place, bases, out):
    m = place[0]

    def index(shape, axis):
        return lax.broadcasted_iota(jnp.int32, shape, axis)

    def pick(mask):
        return jnp.where(mask, 1.0, 0.0).astype(bf16)

    rows = bases[...].astype(f32).reshape(LAT_DEV * 24, NL).astype(bf16)
    wave = index((NL, 1), 0)
    tile = lax.shift_right_logical(wave * 5462, 16)
    chosen = pick(index((NL, LAT_DEV * 24), 1) == wave + 12 * tile)
    table = dot(chosen, rows)
    table = jnp.where(index((NL, NLAT), 0) >= m, table, 0.0).astype(bf16)
    spot = index((1, NLAT), 1)
    x = 12 * (spot & 31) + X_SUB * ((spot >> 5) & 3) + (spot >> 7)
    columns = pick(index((NLAT, NLAT), 0) == x)
    out[0] = dot(table, columns).astype(bf16)
    spot = index((NLAT, 1), 0)
    row = 24 * (spot & 31) + 12 + X_SUB * ((spot >> 5) & 3) + (spot >> 7)
    chosen = pick(index((NLAT, LAT_DEV * 24), 1) == row)
    table = dot(chosen, rows)
    out[1] = jnp.where(index((NLAT, NL), 1) >= m, table, 0.0).astype(bf16)


def legendre_kernel(place, coeffs, own, core_s, far_s, both_s, gain, out, rows, tables, sems):
    mine = place[1]
    copies = [
        pltpu.make_async_copy(source, tables.at[mine ^ d], sems.at[d])
        for d, source in enumerate((own, core_s, far_s, both_s))
    ]
    for copy in copies:
        copy.start()
    rows[...] = coeffs[...].astype(f32)
    fourier = []
    for e in range(4):
        blocks = [
            [rows[pl.ds(256 * xg + 2 * e + r, LAT_DEV, stride=8), :] for r in range(2)]
            for xg in range(XG)
        ]
        stack = []
        for xx in range(X_SUB):
            for xg in range(XG):
                parts = [blocks[xg][r][:, C_SUB * xx : C_SUB * (xx + 1)] for r in range(2)]
                stack.append(jnp.concatenate(parts, axis=1))
        fourier.append(jnp.concatenate(stack, axis=0).astype(bf16))
    quarter = [gain[:, C_SUB * cg : C_SUB * (cg + 1)] for cg in range(CG)]
    low = jnp.where(mine // 2 == 0, quarter[0], quarter[1])
    high = jnp.where(mine // 2 == 0, quarter[2], quarter[3])
    quarter = jnp.where(mine % 2 == 0, low, high)
    gains = jnp.concatenate([quarter, quarter], axis=1)
    for copy in copies:
        copy.wait()
    filtered = [(dot(tables[e, 0], fourier[e]) * gains).astype(bf16) for e in range(4)]
    results = [dot(tables[e, 1], filtered[e]) for e in range(4)]
    for xg in range(XG):
        for e in range(4):
            for r in range(2):
                parts = [
                    results[e][32 * (XG * xx + xg) : 32 * (XG * xx + xg + 1), C_SUB * r : C_SUB * (r + 1)]
                    for xx in range(X_SUB)
                ]
                parts.append(jnp.zeros((LAT_DEV, C_SUB), f32))
                rows[pl.ds(256 * xg + 2 * e + r, LAT_DEV, stride=8), :] = jnp.concatenate(parts, axis=1)
    out[...] = rows[...].astype(bf16)


def inverse_kernel(coeffs, table, out):
    z = jnp.concatenate([coeffs[256 * q : 256 * q + KEPT, :] for q in range(QUADS)], axis=0)
    g = dot(table[...], z)
    for j in range(LON_DEV):
        main = g[Y_MAIN * j : Y_MAIN * (j + 1), 0:96]
        first = LON_DEV * Y_MAIN + Y_EXT * j
        extra = g[first : first + Y_EXT]
        parts = [extra[:, C_SUB * xx : C_SUB * (xx + 1)] for xx in range(X_SUB)]
        out[j] = jnp.concatenate([main, jnp.concatenate(parts, axis=0)], axis=1).astype(bf16)


def grid_kernel(pieces, out):
    for xg in range(XG):
        blocks = [pieces[owner(xg, cg)].astype(f32) for cg in range(CG)]
        for xx in range(X_SUB):
            main = [b[:, C_SUB * xx : C_SUB * (xx + 1)] for b in blocks]
            extra = [b[Y_EXT * xx : Y_EXT * (xx + 1), 96:128] for b in blocks]
            out[X_SUB * xg + xx, 0:Y_MAIN, :] = jnp.concatenate(main, axis=1)
            out[X_SUB * xg + xx, Y_MAIN:, :] = jnp.concatenate(extra, axis=1)[0 : Y_DEV - Y_MAIN]


def call(
    kernel, shape, dtype, scratch=(), smem=0, space=pltpu.VMEM, far=(), flops=0, moved=0, limit=VMEM
):
    outs = [jax.ShapeDtypeStruct(s, dtype) for s in (shape if isinstance(shape, list) else [shape])]
    places = [pl.BlockSpec(memory_space=pltpu.VMEM) for _ in outs]
    single = not isinstance(shape, list)

    def run(*args):
        specs = [
            pl.BlockSpec(memory_space=pltpu.SMEM if k < smem else pltpu.HBM if k in far else space)
            for k in range(len(args))
        ]
        return pl.pallas_call(
            kernel,
            out_shape=outs[0] if single else outs,
            in_specs=specs,
            out_specs=places[0] if single else places,
            scratch_shapes=list(scratch),
            compiler_params=pltpu.CompilerParams(vmem_limit_bytes=limit),
            cost_estimate=pl.CostEstimate(flops=flops, bytes_accessed=moved, transcendentals=0),
        )(*args)

    return run


def arrange(first, second):
    shape = pltpu.VMEM((12, M_DEV, NL), bf16)
    rows = pltpu.VMEM((3, M_DEV * 24, 128), f32)
    return call(
        arrange_kernel,
        (LAT_DEV, 24, NL),
        bf16,
        (shape, shape, rows, pltpu.SemaphoreType.DMA((2,))),
        space=pltpu.HBM,
        limit=NETWORK_VMEM,
    )(first, second)


def on_device(
    saved, cotangent, w_in, b_in, w_mid, b_mid, w_out, spectral_gain, basis_in, basis_out
):
    forward, back = zonal_tables()
    bases = arrange(jnp.transpose(basis_in, (2, 1, 0)), basis_out)
    bases, saved = lax.optimization_barrier((bases, saved))
    bases = lax.all_to_all(bases, "lat", 0, 0, tiled=True)
    weights = (w_in, b_in.reshape(1, -1), w_mid, b_mid.reshape(1, -1), w_out)
    held = [pltpu.VMEM(a.shape, a.dtype) for a in (saved, cotangent) + weights]
    pad = pltpu.VMEM((X_DEV, Y_PAD, CHAN), bf16)
    pieces = call(
        network_kernel,
        (LON_DEV, Y_MAIN, 128),
        bf16,
        held + [pad, pad, pltpu.SemaphoreType.DMA((7,))],
        space=pltpu.HBM,
        flops=1_700_000_000,
        moved=4_000_000,
        limit=NETWORK_VMEM,
    )(saved, cotangent, *weights)
    bases, pieces = lax.optimization_barrier((bases, pieces))
    pieces = lax.all_to_all(pieces, LON, 0, 0, tiled=True)
    mode = M_DEV * lax.axis_index(LON) + lax.axis_index("lat")
    mine = 2 * lax.axis_index("x_hi") + lax.axis_index("core")
    place = jnp.stack([mode, mine]).astype(jnp.int32)
    tables = call(bases_kernel, (2, NL, NLAT), bf16, smem=1, flops=600_000_000, moved=3_000_000)(
        place, bases
    )
    swap = [(0, 1), (1, 0)]
    far = lax.ppermute(tables, "x_hi", swap)
    shared = (
        tables,
        lax.ppermute(tables, "core", swap),
        far,
        lax.ppermute(far, "core", swap),
    )
    coeffs = call(zonal_kernel, (2 * DEVS, 128), bf16, flops=300_000_000)(
        pieces, jnp.asarray(forward)
    )
    coeffs = lax.all_to_all(coeffs.reshape(DEVS // 4, 8, 128), LONG, 0, 0, tiled=True)
    coeffs = call(
        legendre_kernel,
        (2 * DEVS, 128),
        bf16,
        (
            pltpu.VMEM((2 * DEVS, 128), f32),
            pltpu.VMEM((4, 2, NL, NLAT), bf16),
            pltpu.SemaphoreType.DMA((4,)),
        ),
        smem=1,
        far=(2, 3, 4, 5),
        flops=200_000_000,
    )(place, coeffs.reshape(2 * DEVS, 128), *shared, spectral_gain)
    coeffs, back = lax.optimization_barrier((coeffs, jnp.asarray(back)))
    coeffs = lax.all_to_all(coeffs.reshape(DEVS // 4, 8, 128), LONG, 0, 0, tiled=True)
    pieces = call(inverse_kernel, (LON_DEV, Y_MAIN, 128), bf16, flops=300_000_000)(
        coeffs.reshape(2 * DEVS, 128), back
    )
    pieces = lax.all_to_all(pieces, LON, 0, 0, tiled=True)
    return call(grid_kernel, (X_DEV, Y_DEV, CHAN), f32)(pieces)


def solution(mesh):
    grid = P("lat", LON, None)
    placed = (grid, grid, P(), P(), P(), P(), P(), P(), P(None, LON, "lat"), grid)
    fine = Mesh(mesh.devices.reshape(LAT_DEV, 2, 2, 2, 2), ("lat",) + LON)
    return jax.shard_map(on_device, mesh=fine, in_specs=placed, out_specs=grid, check_vma=False)
```

```python
import numpy as np
import jax
import jax.numpy as jnp
from jax import lax
from jax.experimental import pallas as pl
from jax.experimental.pallas import tpu as pltpu
from jax.sharding import Mesh, PartitionSpec as P

bf16 = jnp.bfloat16
f32 = jnp.float32

LAT_DEV, LON_DEV = 32, 16
QUADS = 4
X_DEV, Y_DEV = 12, 90
Y_PAD = 96
Y_MAIN, Y_EXT = 72, 24
NLAT, NLON, NM, NL, CHAN = 384, 1440, 368, 384, 128
M_DEV = 23
X_SUB, C_SUB = 3, 32
CG = CHAN // C_SUB
XG = X_DEV // X_SUB
DEVS = LAT_DEV * LON_DEV
ROWS = 2 * NM
LON = ("x_hi", "x_lo", "z_hi", "core")
LONG = ("x_lo", "z_hi", "lat")
KEPT = 192
VMEM = 16 * 1024 * 1024
NETWORK_VMEM = 59 * 1024 * 1024


def zonal_tables():
    q, i, e = np.meshgrid(np.arange(4), np.arange(M_DEV), np.arange(4), indexing="ij")
    order = (M_DEV * (8 * (e // 2) + 2 * q + e % 2) + i).reshape(-1)
    turns = (order[:, None] * np.arange(NLON)[None, :]) % NLON
    angles = turns.astype(np.float64) * (2.0 * np.pi / NLON)
    table = np.stack([np.cos(angles), -np.sin(angles)], 1).reshape(ROWS, NLON)
    weight = np.where(order == 0, 1.0, 2.0) / NLON
    back = table * np.repeat(weight, 2)[:, None]

    def split_y(t):
        t = np.pad(t.reshape(QUADS, ROWS // QUADS, NLON), ((0, 0), (0, KEPT - ROWS // QUADS), (0, 0)))
        t = t.reshape(QUADS * KEPT, LON_DEV, Y_DEV)
        t = np.pad(t, ((0, 0), (0, 0), (0, Y_PAD - Y_DEV)))
        main = t[:, :, :Y_MAIN].reshape(QUADS * KEPT, LON_DEV * Y_MAIN)
        extra = t[:, :, Y_MAIN:].reshape(QUADS * KEPT, LON_DEV * Y_EXT)
        return np.concatenate([main, extra], 1)

    return (
        np.asarray(split_y(table), dtype=jnp.bfloat16),
        np.ascontiguousarray(split_y(back).T).astype(jnp.bfloat16),
    )


def owner(xg, cg):
    return 8 * (cg % 2) + 2 * xg + cg // 2


def dot(a, b):
    return lax.dot_general(a, b, (((1,), (0,)), ((), ())), preferred_element_type=f32)


def dot_t(a, b):
    return lax.dot_general(a, b, (((1,), (1,)), ((), ())), preferred_element_type=f32)


def sigmoid(v):
    return 0.5 * jnp.tanh(0.5 * v) + 0.5


def arrange_kernel(first_h, second_h, out, first, second, rows, sems):
    copies = [
        pltpu.make_async_copy(first_h, first, sems.at[0]),
        pltpu.make_async_copy(second_h, second, sems.at[1]),
    ]
    for copy in copies:
        copy.start()
    out[M_DEV:] = jnp.zeros((LAT_DEV - M_DEV, 24, NL), bf16)
    for half, source in enumerate((first, second)):
        copies[half].wait()
        for k in range(12):
            block = source[k].astype(f32)
            for t in range(3):
                rows[t, pl.ds(12 * half + k, M_DEV, stride=24), :] = block[:, 128 * t : 128 * (t + 1)]
    for m in range(M_DEV):
        for t in range(3):
            out[m, :, 128 * t : 128 * (t + 1)] = rows[t, 24 * m : 24 * (m + 1), :].astype(bf16)


def network_kernel(
    saved_h, cotan_h, w_in_h, b_in_h, w_mid_h, b_mid_h, w_out_h, out,
    saved, cotan, w_in, b_in, w_mid, b_mid, w_out, rows_s, rows_c, sems,
):
    pairs = (
        (saved_h, saved), (w_in_h, w_in), (b_in_h, b_in), (w_mid_h, w_mid),
        (b_mid_h, b_mid), (cotan_h, cotan), (w_out_h, w_out),
    )
    copies = [pltpu.make_async_copy(a, b, sems.at[k]) for k, (a, b) in enumerate(pairs)]
    for copy in copies:
        copy.start()
    got = dict(zip(("saved", "w_in", "b_in", "w_mid", "b_mid", "cotan", "w_out"), copies))
    edge = jnp.zeros((X_DEV, 16, CHAN), bf16)
    rows_s[:, Y_PAD - 16 :, :] = edge
    rows_c[:, Y_PAD - 16 :, :] = edge
    got["saved"].wait()
    for x in range(X_DEV):
        rows_s[x, 0:Y_DEV, :] = saved[x]
    got["w_in"].wait()
    got["b_in"].wait()
    for xg in range(XG):
        s = rows_s[X_SUB * xg : X_SUB * (xg + 1)].reshape(X_SUB * Y_PAD, CHAN)
        first = dot(s, w_in[...]) + b_in[...]
        sig = sigmoid(first)
        act = first * sig
        slope_one = sig + act * (1.0 - sig)
        if xg == 0:
            got["w_mid"].wait()
            got["b_mid"].wait()
        second = dot(act.astype(bf16), w_mid[...]) + b_mid[...]
        sig = sigmoid(second)
        slope_two = sig * (1.0 + second * (1.0 - sig))
        if xg == 0:
            got["cotan"].wait()
            got["w_out"].wait()
            for x in range(X_DEV):
                rows_c[x, 0:Y_DEV, :] = cotan[x]
        c = rows_c[X_SUB * xg : X_SUB * (xg + 1)].reshape(X_SUB * Y_PAD, CHAN)
        back_two = (dot_t(c, w_out[...]) * slope_two).astype(bf16)
        back_one = (dot_t(back_two, w_mid[...]) * slope_one).astype(bf16)
        grad = c.astype(f32) + dot_t(back_one, w_in[...])
        grad = grad.reshape(X_SUB, Y_PAD, CHAN)
        for cg in range(CG):
            parts = [grad[xx][:, C_SUB * cg : C_SUB * (cg + 1)] for xx in range(X_SUB)]
            parts = [p[0:Y_MAIN] for p in parts] + [
                jnp.concatenate([p[Y_MAIN:] for p in parts], axis=0)
            ]
            out[owner(xg, cg)] = jnp.concatenate(parts, axis=1).astype(bf16)


def zonal_kernel(circles, table, out):
    main, extra = [], []
    for j in range(LON_DEV):
        piece = circles[j].astype(f32)
        main.append(piece)
        parts = [piece[Y_EXT * xx : Y_EXT * (xx + 1), 96:128] for xx in range(X_SUB)]
        extra.append(jnp.concatenate(parts + [jnp.zeros((Y_EXT, C_SUB), f32)], axis=1))
    g = jnp.concatenate(main + extra, axis=0).astype(bf16)
    spectrum = dot(table[...], g).astype(bf16)
    for q in range(QUADS):
        out[256 * q : 256 * q + KEPT, :] = spectrum[KEPT * q : KEPT * (q + 1)]
        out[256 * q + KEPT : 256 * (q + 1), :] = jnp.zeros((256 - KEPT, 128), bf16)


def bases_kernel(place, bases_h, out, bases, sem):
    copy = pltpu.make_async_copy(bases_h, bases, sem)
    copy.start()
    m = place[0]

    def index(shape, axis):
        return lax.broadcasted_iota(jnp.int32, shape, axis)

    def pick(mask):
        return jnp.where(mask, 1.0, 0.0).astype(bf16)

    copy.wait()
    rows = bases[...].astype(f32).reshape(LAT_DEV * 24, NL).astype(bf16)
    wave = index((NL, 1), 0)
    tile = lax.shift_right_logical(wave * 5462, 16)
    chosen = pick(index((NL, LAT_DEV * 24), 1) == wave + 12 * tile)
    table = dot(chosen, rows)
    table = jnp.where(index((NL, NLAT), 0) >= m, table, 0.0).astype(bf16)
    spot = index((1, NLAT), 1)
    x = 12 * (spot & 31) + X_SUB * ((spot >> 5) & 3) + (spot >> 7)
    columns = pick(index((NLAT, NLAT), 0) == x)
    out[0] = dot(table, columns).astype(bf16)
    spot = index((NLAT, 1), 0)
    row = 24 * (spot & 31) + 12 + X_SUB * ((spot >> 5) & 3) + (spot >> 7)
    chosen = pick(index((NLAT, LAT_DEV * 24), 1) == row)
    table = dot(chosen, rows)
    out[1] = jnp.where(index((NLAT, NL), 1) >= m, table, 0.0).astype(bf16)


def legendre_kernel(place, coeffs, own, core_s, far_s, both_s, gain, out, rows, tables, sems):
    mine = place[1]
    copies = [
        pltpu.make_async_copy(source, tables.at[mine ^ d], sems.at[d])
        for d, source in enumerate((own, core_s, far_s, both_s))
    ]
    for copy in copies:
        copy.start()
    rows[...] = coeffs[...].astype(f32)
    fourier = []
    for e in range(4):
        blocks = [
            [rows[pl.ds(256 * xg + 2 * e + r, LAT_DEV, stride=8), :] for r in range(2)]
            for xg in range(XG)
        ]
        stack = []
        for xx in range(X_SUB):
            for xg in range(XG):
                parts = [blocks[xg][r][:, C_SUB * xx : C_SUB * (xx + 1)] for r in range(2)]
                stack.append(jnp.concatenate(parts, axis=1))
        fourier.append(jnp.concatenate(stack, axis=0).astype(bf16))
    quarter = [gain[:, C_SUB * cg : C_SUB * (cg + 1)] for cg in range(CG)]
    low = jnp.where(mine // 2 == 0, quarter[0], quarter[1])
    high = jnp.where(mine // 2 == 0, quarter[2], quarter[3])
    quarter = jnp.where(mine % 2 == 0, low, high)
    gains = jnp.concatenate([quarter, quarter], axis=1)
    for copy in copies:
        copy.wait()
    filtered = [(dot(tables[e, 0], fourier[e]) * gains).astype(bf16) for e in range(4)]
    results = [dot(tables[e, 1], filtered[e]) for e in range(4)]
    for xg in range(XG):
        for e in range(4):
            for r in range(2):
                parts = [
                    results[e][32 * (XG * xx + xg) : 32 * (XG * xx + xg + 1), C_SUB * r : C_SUB * (r + 1)]
                    for xx in range(X_SUB)
                ]
                parts.append(jnp.zeros((LAT_DEV, C_SUB), f32))
                rows[pl.ds(256 * xg + 2 * e + r, LAT_DEV, stride=8), :] = jnp.concatenate(parts, axis=1)
    out[...] = rows[...].astype(bf16)


def inverse_kernel(coeffs, table, out):
    z = jnp.concatenate([coeffs[256 * q : 256 * q + KEPT, :] for q in range(QUADS)], axis=0)
    g = dot(table[...], z)
    for j in range(LON_DEV):
        main = g[Y_MAIN * j : Y_MAIN * (j + 1), 0:96]
        first = LON_DEV * Y_MAIN + Y_EXT * j
        extra = g[first : first + Y_EXT]
        parts = [extra[:, C_SUB * xx : C_SUB * (xx + 1)] for xx in range(X_SUB)]
        out[j] = jnp.concatenate([main, jnp.concatenate(parts, axis=0)], axis=1).astype(bf16)


def grid_kernel(pieces, out):
    for xg in range(XG):
        blocks = [pieces[owner(xg, cg)].astype(f32) for cg in range(CG)]
        for xx in range(X_SUB):
            main = [b[:, C_SUB * xx : C_SUB * (xx + 1)] for b in blocks]
            extra = [b[Y_EXT * xx : Y_EXT * (xx + 1), 96:128] for b in blocks]
            out[X_SUB * xg + xx, 0:Y_MAIN, :] = jnp.concatenate(main, axis=1)
            out[X_SUB * xg + xx, Y_MAIN:, :] = jnp.concatenate(extra, axis=1)[0 : Y_DEV - Y_MAIN]


def call(
    kernel, shape, dtype, scratch=(), smem=0, space=pltpu.VMEM, far=(), flops=0, moved=0, limit=VMEM
):
    outs = [jax.ShapeDtypeStruct(s, dtype) for s in (shape if isinstance(shape, list) else [shape])]
    places = [pl.BlockSpec(memory_space=pltpu.VMEM) for _ in outs]
    single = not isinstance(shape, list)

    def run(*args):
        specs = [
            pl.BlockSpec(memory_space=pltpu.SMEM if k < smem else pltpu.HBM if k in far else space)
            for k in range(len(args))
        ]
        return pl.pallas_call(
            kernel,
            out_shape=outs[0] if single else outs,
            in_specs=specs,
            out_specs=places[0] if single else places,
            scratch_shapes=list(scratch),
            compiler_params=pltpu.CompilerParams(vmem_limit_bytes=limit),
            cost_estimate=pl.CostEstimate(flops=flops, bytes_accessed=moved, transcendentals=0),
        )(*args)

    return run


def arrange(first, second):
    shape = pltpu.VMEM((12, M_DEV, NL), bf16)
    rows = pltpu.VMEM((3, M_DEV * 24, 128), f32)
    return call(
        arrange_kernel,
        (LAT_DEV, 24, NL),
        bf16,
        (shape, shape, rows, pltpu.SemaphoreType.DMA((2,))),
        space=pltpu.HBM,
        limit=NETWORK_VMEM,
    )(first, second)


def on_device(
    saved, cotangent, w_in, b_in, w_mid, b_mid, w_out, spectral_gain, basis_in, basis_out
):
    forward, back = zonal_tables()
    bases = arrange(jnp.transpose(basis_in, (2, 1, 0)), basis_out)
    bases, saved = lax.optimization_barrier((bases, saved))
    bases = lax.all_to_all(bases, "lat", 0, 0, tiled=True)
    weights = (w_in, b_in.reshape(1, -1), w_mid, b_mid.reshape(1, -1), w_out)
    held = [pltpu.VMEM(a.shape, a.dtype) for a in (saved, cotangent) + weights]
    pad = pltpu.VMEM((X_DEV, Y_PAD, CHAN), bf16)
    pieces = call(
        network_kernel,
        (LON_DEV, Y_MAIN, 128),
        bf16,
        held + [pad, pad, pltpu.SemaphoreType.DMA((7,))],
        space=pltpu.HBM,
        flops=1_700_000_000,
        moved=4_000_000,
        limit=NETWORK_VMEM,
    )(saved, cotangent, *weights)
    bases, pieces = lax.optimization_barrier((bases, pieces))
    pieces = lax.all_to_all(pieces, LON, 0, 0, tiled=True)
    mode = M_DEV * lax.axis_index(LON) + lax.axis_index("lat")
    mine = 2 * lax.axis_index("x_hi") + lax.axis_index("core")
    place = jnp.stack([mode, mine]).astype(jnp.int32)
    tables = call(
        bases_kernel,
        (2, NL, NLAT),
        bf16,
        (pltpu.VMEM((LAT_DEV, 24, NL), bf16), pltpu.SemaphoreType.DMA),
        smem=1,
        far=(1,),
        flops=600_000_000,
        moved=3_000_000,
    )(place, bases)
    swap = [(0, 1), (1, 0)]
    far = lax.ppermute(tables, "x_hi", swap)
    near = lax.ppermute(tables, "core", swap)
    coeffs = call(zonal_kernel, (2 * DEVS, 128), bf16, flops=300_000_000)(
        pieces, jnp.asarray(forward)
    )
    late, _ = lax.optimization_barrier((far, coeffs))
    shared = (tables, near, far, lax.ppermute(late, "core", swap))
    coeffs = lax.all_to_all(coeffs.reshape(DEVS // 4, 8, 128), LONG, 0, 0, tiled=True)
    coeffs = call(
        legendre_kernel,
        (2 * DEVS, 128),
        bf16,
        (
            pltpu.VMEM((2 * DEVS, 128), f32),
            pltpu.VMEM((4, 2, NL, NLAT), bf16),
            pltpu.SemaphoreType.DMA((4,)),
        ),
        smem=1,
        far=(2, 3, 4, 5),
        flops=200_000_000,
    )(place, coeffs.reshape(2 * DEVS, 128), *shared, spectral_gain)
    coeffs, back = lax.optimization_barrier((coeffs, jnp.asarray(back)))
    coeffs = lax.all_to_all(coeffs.reshape(DEVS // 4, 8, 128), LONG, 0, 0, tiled=True)
    pieces = call(inverse_kernel, (LON_DEV, Y_MAIN, 128), bf16, flops=300_000_000)(
        coeffs.reshape(2 * DEVS, 128), back
    )
    pieces = lax.all_to_all(pieces, LON, 0, 0, tiled=True)
    return call(grid_kernel, (X_DEV, Y_DEV, CHAN), f32)(pieces)


def solution(mesh):
    grid = P("lat", LON, None)
    placed = (grid, grid, P(), P(), P(), P(), P(), P(), P(None, LON, "lat"), grid)
    fine = Mesh(mesh.devices.reshape(LAT_DEV, 2, 2, 2, 2), ("lat",) + LON)
    return jax.shard_map(on_device, mesh=fine, in_specs=placed, out_specs=grid, check_vma=False)
```

```python
import numpy as np
import jax
import jax.numpy as jnp
from jax import lax
from jax.experimental import pallas as pl
from jax.experimental.pallas import tpu as pltpu
from jax.sharding import Mesh, PartitionSpec as P

bf16 = jnp.bfloat16
f32 = jnp.float32

LAT_DEV, LON_DEV = 32, 16
PAIRS = LON_DEV // 2
X_DEV, Y_DEV = 12, 90
Y_PAD = 96
Y_MAIN, Y_EXT = 72, 24
NLAT, NLON, NM, NL, CHAN = 384, 1440, 368, 384, 128
M_DEV = 23
X_SUB, C_SUB = 3, 32
CG = CHAN // C_SUB
XG = X_DEV // X_SUB
DEVS = LAT_DEV * LON_DEV
ROWS = 2 * NM
LON = ("pair", "core")
LONG = ("pair", "lat")
KEPT = 96
VMEM = 16 * 1024 * 1024
NETWORK_VMEM = 59 * 1024 * 1024


def zonal_tables():
    k, i, h = np.meshgrid(np.arange(PAIRS), np.arange(M_DEV), np.arange(2), indexing="ij")
    order = (M_DEV * (2 * k + h) + i).reshape(-1)
    turns = (order[:, None] * np.arange(NLON)[None, :]) % NLON
    angles = turns.astype(np.float64) * (2.0 * np.pi / NLON)
    table = np.stack([np.cos(angles), -np.sin(angles)], 1).reshape(ROWS, NLON)
    weight = np.where(order == 0, 1.0, 2.0) / NLON
    back = table * np.repeat(weight, 2)[:, None]

    def split_y(t):
        t = np.pad(t.reshape(PAIRS, ROWS // PAIRS, NLON), ((0, 0), (0, KEPT - ROWS // PAIRS), (0, 0)))
        t = t.reshape(PAIRS * KEPT, LON_DEV, Y_DEV)
        t = np.pad(t, ((0, 0), (0, 0), (0, Y_PAD - Y_DEV)))
        main = t[:, :, :Y_MAIN].reshape(PAIRS * KEPT, LON_DEV * Y_MAIN)
        extra = t[:, :, Y_MAIN:].reshape(PAIRS * KEPT, LON_DEV * Y_EXT)
        return np.concatenate([main, extra], 1)

    return (
        np.asarray(split_y(table), dtype=jnp.bfloat16),
        np.ascontiguousarray(split_y(back).T).astype(jnp.bfloat16),
    )


def owner(xg, cg):
    return CG * xg + 2 * (cg % 2) + cg // 2


def dot(a, b):
    return lax.dot_general(a, b, (((1,), (0,)), ((), ())), preferred_element_type=f32)


def dot_t(a, b):
    return lax.dot_general(a, b, (((1,), (1,)), ((), ())), preferred_element_type=f32)


def sigmoid(v):
    return 0.5 * jnp.tanh(0.5 * v) + 0.5


def arrange_kernel(first_h, second_h, out, first, second, rows, sems):
    copies = [
        pltpu.make_async_copy(first_h, first, sems.at[0]),
        pltpu.make_async_copy(second_h, second, sems.at[1]),
    ]
    for copy in copies:
        copy.start()
    out[M_DEV:] = jnp.zeros((LAT_DEV - M_DEV, 24, NL), bf16)
    for half, source in enumerate((first, second)):
        copies[half].wait()
        for k in range(12):
            block = source[k].astype(f32)
            for t in range(3):
                rows[t, pl.ds(12 * half + k, M_DEV, stride=24), :] = block[:, 128 * t : 128 * (t + 1)]
    for m in range(M_DEV):
        for t in range(3):
            out[m, :, 128 * t : 128 * (t + 1)] = rows[t, 24 * m : 24 * (m + 1), :].astype(bf16)


def network_kernel(
    saved_h, cotan_h, w_in_h, b_in_h, w_mid_h, b_mid_h, w_out_h, out,
    saved, cotan, w_in, b_in, w_mid, b_mid, w_out, rows_s, rows_c, sems,
):
    pairs = (
        (saved_h, saved), (w_in_h, w_in), (b_in_h, b_in), (w_mid_h, w_mid),
        (b_mid_h, b_mid), (cotan_h, cotan), (w_out_h, w_out),
    )
    copies = [pltpu.make_async_copy(a, b, sems.at[k]) for k, (a, b) in enumerate(pairs)]
    for copy in copies:
        copy.start()
    got = dict(zip(("saved", "w_in", "b_in", "w_mid", "b_mid", "cotan", "w_out"), copies))
    edge = jnp.zeros((X_DEV, 16, CHAN), bf16)
    rows_s[:, Y_PAD - 16 :, :] = edge
    rows_c[:, Y_PAD - 16 :, :] = edge
    got["saved"].wait()
    for x in range(X_DEV):
        rows_s[x, 0:Y_DEV, :] = saved[x]
    got["w_in"].wait()
    got["b_in"].wait()
    for xg in range(XG):
        s = rows_s[X_SUB * xg : X_SUB * (xg + 1)].reshape(X_SUB * Y_PAD, CHAN)
        first = dot(s, w_in[...]) + b_in[...]
        sig = sigmoid(first)
        act = first * sig
        slope_one = sig + act * (1.0 - sig)
        if xg == 0:
            got["w_mid"].wait()
            got["b_mid"].wait()
        second = dot(act.astype(bf16), w_mid[...]) + b_mid[...]
        sig = sigmoid(second)
        slope_two = sig * (1.0 + second * (1.0 - sig))
        if xg == 0:
            got["cotan"].wait()
            got["w_out"].wait()
            for x in range(X_DEV):
                rows_c[x, 0:Y_DEV, :] = cotan[x]
        c = rows_c[X_SUB * xg : X_SUB * (xg + 1)].reshape(X_SUB * Y_PAD, CHAN)
        back_two = (dot_t(c, w_out[...]) * slope_two).astype(bf16)
        back_one = (dot_t(back_two, w_mid[...]) * slope_one).astype(bf16)
        grad = c.astype(f32) + dot_t(back_one, w_in[...])
        grad = grad.reshape(X_SUB, Y_PAD, CHAN)
        for cg in range(CG):
            parts = [grad[xx][:, C_SUB * cg : C_SUB * (cg + 1)] for xx in range(X_SUB)]
            parts = [p[0:Y_MAIN] for p in parts] + [
                jnp.concatenate([p[Y_MAIN:] for p in parts], axis=0)
            ]
            out[owner(xg, cg)] = jnp.concatenate(parts, axis=1).astype(bf16)


def zonal_kernel(circles, table, out):
    main, extra = [], []
    for j in range(LON_DEV):
        piece = circles[j].astype(f32)
        main.append(piece)
        parts = [piece[Y_EXT * xx : Y_EXT * (xx + 1), 96:128] for xx in range(X_SUB)]
        extra.append(jnp.concatenate(parts + [jnp.zeros((Y_EXT, C_SUB), f32)], axis=1))
    g = jnp.concatenate(main + extra, axis=0).astype(bf16)
    spectrum = dot(table[...], g).astype(bf16)
    for k in range(PAIRS):
        out[128 * k : 128 * k + KEPT, :] = spectrum[KEPT * k : KEPT * (k + 1)]
        out[128 * k + KEPT : 128 * (k + 1), :] = jnp.zeros((128 - KEPT, 128), bf16)


def bases_kernel(place, bases, out):
    m = place[0]

    def index(shape, axis):
        return lax.broadcasted_iota(jnp.int32, shape, axis)

    def pick(mask):
        return jnp.where(mask, 1.0, 0.0).astype(bf16)

    rows = bases[...].astype(f32).reshape(LAT_DEV * 24, NL).astype(bf16)
    wave = index((NL, 1), 0)
    tile = lax.shift_right_logical(wave * 5462, 16)
    chosen = pick(index((NL, LAT_DEV * 24), 1) == wave + 12 * tile)
    table = dot(chosen, rows)
    table = jnp.where(index((NL, NLAT), 0) >= m, table, 0.0).astype(bf16)
    spot = index((1, NLAT), 1)
    x = 12 * (spot & 31) + X_SUB * ((spot >> 5) & 3) + (spot >> 7)
    columns = pick(index((NLAT, NLAT), 0) == x)
    out[0] = dot(table, columns).astype(bf16)
    spot = index((NLAT, 1), 0)
    row = 24 * (spot & 31) + 12 + X_SUB * ((spot >> 5) & 3) + (spot >> 7)
    chosen = pick(index((NLAT, LAT_DEV * 24), 1) == row)
    table = dot(chosen, rows)
    out[1] = jnp.where(index((NLAT, NL), 1) >= m, table, 0.0).astype(bf16)


def legendre_kernel(place, coeffs, tables, others, gain, out, rows):
    core = place[1]

    def swapped(pair):
        return jnp.where(core == 0, pair[0], pair[1]), jnp.where(core == 0, pair[1], pair[0])

    rows[...] = coeffs[...].astype(f32)
    blocks = [
        [rows[pl.ds(128 * k + n, LAT_DEV, stride=4), :] for n in range(4)] for k in range(PAIRS)
    ]
    modes = []
    for h in range(2):
        stack = []
        for xx in range(X_SUB):
            for xg in range(XG):
                parts = [
                    blocks[2 * xg + cq][2 * h + r][:, C_SUB * xx : C_SUB * (xx + 1)]
                    for r in range(2)
                    for cq in range(2)
                ]
                stack.append(jnp.concatenate(parts, axis=1))
        modes.append(jnp.concatenate(stack, axis=0))
    half = jnp.where(core == 0, gain[:, 0:64], gain[:, 64:128])
    gains = jnp.concatenate([half, half], axis=1)
    results = []
    for fourier, table in zip(swapped(modes), (tables, others)):
        filtered = (dot(table[0], fourier.astype(bf16)) * gains).astype(bf16)
        results.append(dot(table[1], filtered))
    results = swapped(results)
    for k in range(PAIRS):
        xg, cq = k // 2, k % 2
        for h in range(2):
            for r in range(2):
                first = 64 * r + C_SUB * cq
                parts = [
                    results[h][32 * (XG * xx + xg) : 32 * (XG * xx + xg + 1), first : first + C_SUB]
                    for xx in range(X_SUB)
                ]
                parts.append(jnp.zeros((LAT_DEV, C_SUB), f32))
                rows[pl.ds(128 * k + 2 * h + r, LAT_DEV, stride=4), :] = jnp.concatenate(parts, axis=1)
    out[...] = rows[...].astype(bf16)


def inverse_kernel(coeffs, table, out):
    z = jnp.concatenate([coeffs[128 * k : 128 * k + KEPT, :] for k in range(PAIRS)], axis=0)
    g = dot(table[...], z)
    for j in range(LON_DEV):
        main = g[Y_MAIN * j : Y_MAIN * (j + 1), 0:96]
        first = LON_DEV * Y_MAIN + Y_EXT * j
        extra = g[first : first + Y_EXT]
        parts = [extra[:, C_SUB * xx : C_SUB * (xx + 1)] for xx in range(X_SUB)]
        out[j] = jnp.concatenate([main, jnp.concatenate(parts, axis=0)], axis=1).astype(bf16)


def grid_kernel(pieces, out):
    for xg in range(XG):
        blocks = [pieces[owner(xg, cg)].astype(f32) for cg in range(CG)]
        for xx in range(X_SUB):
            main = [b[:, C_SUB * xx : C_SUB * (xx + 1)] for b in blocks]
            extra = [b[Y_EXT * xx : Y_EXT * (xx + 1), 96:128] for b in blocks]
            out[X_SUB * xg + xx, 0:Y_MAIN, :] = jnp.concatenate(main, axis=1)
            out[X_SUB * xg + xx, Y_MAIN:, :] = jnp.concatenate(extra, axis=1)[0 : Y_DEV - Y_MAIN]


def call(
    kernel, shape, dtype, scratch=(), smem=0, space=pltpu.VMEM, flops=0, moved=0, limit=VMEM
):
    outs = [jax.ShapeDtypeStruct(s, dtype) for s in (shape if isinstance(shape, list) else [shape])]
    places = [pl.BlockSpec(memory_space=pltpu.VMEM) for _ in outs]
    single = not isinstance(shape, list)

    def run(*args):
        specs = [
            pl.BlockSpec(memory_space=pltpu.SMEM if k < smem else space) for k in range(len(args))
        ]
        return pl.pallas_call(
            kernel,
            out_shape=outs[0] if single else outs,
            in_specs=specs,
            out_specs=places[0] if single else places,
            scratch_shapes=list(scratch),
            compiler_params=pltpu.CompilerParams(vmem_limit_bytes=limit),
            cost_estimate=pl.CostEstimate(flops=flops, bytes_accessed=moved, transcendentals=0),
        )(*args)

    return run


def arrange(first, second):
    shape = pltpu.VMEM((12, M_DEV, NL), bf16)
    rows = pltpu.VMEM((3, M_DEV * 24, 128), f32)
    return call(
        arrange_kernel,
        (LAT_DEV, 24, NL),
        bf16,
        (shape, shape, rows, pltpu.SemaphoreType.DMA((2,))),
        space=pltpu.HBM,
        limit=NETWORK_VMEM,
    )(first, second)


def on_device(
    saved, cotangent, w_in, b_in, w_mid, b_mid, w_out, spectral_gain, basis_in, basis_out
):
    forward, back = zonal_tables()
    bases = arrange(jnp.transpose(basis_in, (2, 1, 0)), basis_out)
    bases, saved = lax.optimization_barrier((bases, saved))
    bases = lax.all_to_all(bases, "lat", 0, 0, tiled=True)
    weights = (w_in, b_in.reshape(1, -1), w_mid, b_mid.reshape(1, -1), w_out)
    held = [pltpu.VMEM(a.shape, a.dtype) for a in (saved, cotangent) + weights]
    pad = pltpu.VMEM((X_DEV, Y_PAD, CHAN), bf16)
    pieces = call(
        network_kernel,
        (LON_DEV, Y_MAIN, 128),
        bf16,
        held + [pad, pad, pltpu.SemaphoreType.DMA((7,))],
        space=pltpu.HBM,
        flops=1_700_000_000,
        moved=4_000_000,
        limit=NETWORK_VMEM,
    )(saved, cotangent, *weights)
    bases, pieces = lax.optimization_barrier((bases, pieces))
    pieces = lax.all_to_all(pieces, LON, 0, 0, tiled=True)
    mode = M_DEV * lax.axis_index(LON) + lax.axis_index("lat")
    place = jnp.stack([mode, lax.axis_index("core")]).astype(jnp.int32)
    tables = call(bases_kernel, (2, NL, NLAT), bf16, smem=1, flops=600_000_000, moved=3_000_000)(
        place, bases
    )
    others = lax.ppermute(tables, "core", [(0, 1), (1, 0)])
    coeffs = call(zonal_kernel, (2 * DEVS, 128), bf16, flops=300_000_000)(
        pieces, jnp.asarray(forward)
    )
    coeffs = lax.all_to_all(coeffs.reshape(DEVS // 2, 4, 128), LONG, 0, 0, tiled=True)
    coeffs = call(
        legendre_kernel,
        (2 * DEVS, 128),
        bf16,
        (pltpu.VMEM((2 * DEVS, 128), f32),),
        smem=1,
        flops=200_000_000,
    )(place, coeffs.reshape(2 * DEVS, 128), tables, others, spectral_gain)
    coeffs, back = lax.optimization_barrier((coeffs, jnp.asarray(back)))
    coeffs = lax.all_to_all(coeffs.reshape(DEVS // 2, 4, 128), LONG, 0, 0, tiled=True)
    pieces = call(inverse_kernel, (LON_DEV, Y_MAIN, 128), bf16, flops=300_000_000)(
        coeffs.reshape(2 * DEVS, 128), back
    )
    pieces = lax.all_to_all(pieces, LON, 0, 0, tiled=True)
    return call(grid_kernel, (X_DEV, Y_DEV, CHAN), f32)(pieces)


def solution(mesh):
    grid = P("lat", LON, None)
    placed = (grid, grid, P(), P(), P(), P(), P(), P(), P(None, LON, "lat"), grid)
    fine = Mesh(mesh.devices.reshape(LAT_DEV, PAIRS, 2), ("lat",) + LON)
    return jax.shard_map(on_device, mesh=fine, in_specs=placed, out_specs=grid, check_vma=False)
```

```python
import numpy as np
import jax
import jax.numpy as jnp
from jax import lax
from jax.experimental import pallas as pl
from jax.experimental.pallas import tpu as pltpu
from jax.sharding import Mesh, PartitionSpec as P

bf16 = jnp.bfloat16
f32 = jnp.float32

LAT_DEV, LON_DEV = 32, 16
QUADS = 4
X_DEV, Y_DEV = 12, 90
Y_PAD = 96
Y_MAIN, Y_EXT = 72, 24
NLAT, NLON, NM, NL, CHAN = 384, 1440, 368, 384, 128
M_DEV = 23
X_SUB, C_SUB = 3, 32
CG = CHAN // C_SUB
XG = X_DEV // X_SUB
DEVS = LAT_DEV * LON_DEV
ROWS = 2 * NM
LON = ("x_hi", "x_lo", "z_hi", "core")
LONG = ("x_lo", "z_hi", "lat")
KEPT = 192
VMEM = 16 * 1024 * 1024
NETWORK_VMEM = 59 * 1024 * 1024


def zonal_tables():
    q, i, e = np.meshgrid(np.arange(4), np.arange(M_DEV), np.arange(4), indexing="ij")
    order = (M_DEV * (8 * (e // 2) + 2 * q + e % 2) + i).reshape(-1)
    turns = (order[:, None] * np.arange(NLON)[None, :]) % NLON
    angles = turns.astype(np.float64) * (2.0 * np.pi / NLON)
    table = np.stack([np.cos(angles), -np.sin(angles)], 1).reshape(ROWS, NLON)
    weight = np.where(order == 0, 1.0, 2.0) / NLON
    back = table * np.repeat(weight, 2)[:, None]

    def split_y(t):
        t = np.pad(t.reshape(QUADS, ROWS // QUADS, NLON), ((0, 0), (0, KEPT - ROWS // QUADS), (0, 0)))
        t = t.reshape(QUADS * KEPT, LON_DEV, Y_DEV)
        t = np.pad(t, ((0, 0), (0, 0), (0, Y_PAD - Y_DEV)))
        main = t[:, :, :Y_MAIN].reshape(QUADS * KEPT, LON_DEV * Y_MAIN)
        extra = t[:, :, Y_MAIN:].reshape(QUADS * KEPT, LON_DEV * Y_EXT)
        return np.concatenate([main, extra], 1)

    return (
        np.asarray(split_y(table), dtype=jnp.bfloat16),
        np.ascontiguousarray(split_y(back).T).astype(jnp.bfloat16),
    )


def owner(xg, cg):
    return 8 * (cg % 2) + 2 * xg + cg // 2


def dot(a, b):
    return lax.dot_general(a, b, (((1,), (0,)), ((), ())), preferred_element_type=f32)


def dot_t(a, b):
    return lax.dot_general(a, b, (((1,), (1,)), ((), ())), preferred_element_type=f32)


def sigmoid(v):
    return 0.5 * jnp.tanh(0.5 * v) + 0.5


def arrange_kernel(first_h, second_h, out, first, second, rows, sems):
    copies = [
        pltpu.make_async_copy(first_h, first, sems.at[0]),
        pltpu.make_async_copy(second_h, second, sems.at[1]),
    ]
    for copy in copies:
        copy.start()
    out[M_DEV:] = jnp.zeros((LAT_DEV - M_DEV, 24, NL), bf16)
    for half, source in enumerate((first, second)):
        copies[half].wait()
        for k in range(12):
            block = source[k].astype(f32)
            for t in range(3):
                rows[t, pl.ds(12 * half + k, M_DEV, stride=24), :] = block[:, 128 * t : 128 * (t + 1)]
    for m in range(M_DEV):
        for t in range(3):
            out[m, :, 128 * t : 128 * (t + 1)] = rows[t, 24 * m : 24 * (m + 1), :].astype(bf16)


def network_kernel(
    saved_h, cotan_h, w_in_h, b_in_h, w_mid_h, b_mid_h, w_out_h, out,
    saved, cotan, w_in, b_in, w_mid, b_mid, w_out, rows_s, rows_c, sems,
):
    pairs = (
        (saved_h, saved), (w_in_h, w_in), (b_in_h, b_in), (w_mid_h, w_mid),
        (b_mid_h, b_mid), (cotan_h, cotan), (w_out_h, w_out),
    )
    copies = [pltpu.make_async_copy(a, b, sems.at[k]) for k, (a, b) in enumerate(pairs)]
    for copy in copies:
        copy.start()
    got = dict(zip(("saved", "w_in", "b_in", "w_mid", "b_mid", "cotan", "w_out"), copies))
    edge = jnp.zeros((X_DEV, 16, CHAN), bf16)
    rows_s[:, Y_PAD - 16 :, :] = edge
    rows_c[:, Y_PAD - 16 :, :] = edge
    got["saved"].wait()
    for x in range(X_DEV):
        rows_s[x, 0:Y_DEV, :] = saved[x]
    got["w_in"].wait()
    got["b_in"].wait()
    for xg in range(XG):
        s = rows_s[X_SUB * xg : X_SUB * (xg + 1)].reshape(X_SUB * Y_PAD, CHAN)
        first = dot(s, w_in[...]) + b_in[...]
        sig = sigmoid(first)
        act = first * sig
        slope_one = sig + act * (1.0 - sig)
        if xg == 0:
            got["w_mid"].wait()
            got["b_mid"].wait()
        second = dot(act.astype(bf16), w_mid[...]) + b_mid[...]
        sig = sigmoid(second)
        slope_two = sig * (1.0 + second * (1.0 - sig))
        if xg == 0:
            got["cotan"].wait()
            got["w_out"].wait()
            for x in range(X_DEV):
                rows_c[x, 0:Y_DEV, :] = cotan[x]
        c = rows_c[X_SUB * xg : X_SUB * (xg + 1)].reshape(X_SUB * Y_PAD, CHAN)
        back_two = (dot_t(c, w_out[...]) * slope_two).astype(bf16)
        back_one = (dot_t(back_two, w_mid[...]) * slope_one).astype(bf16)
        grad = c.astype(f32) + dot_t(back_one, w_in[...])
        grad = grad.reshape(X_SUB, Y_PAD, CHAN)
        for cg in range(CG):
            parts = [grad[xx][:, C_SUB * cg : C_SUB * (cg + 1)] for xx in range(X_SUB)]
            parts = [p[0:Y_MAIN] for p in parts] + [
                jnp.concatenate([p[Y_MAIN:] for p in parts], axis=0)
            ]
            out[owner(xg, cg)] = jnp.concatenate(parts, axis=1).astype(bf16)


def zonal_kernel(circles, table, out):
    main, extra = [], []
    for j in range(LON_DEV):
        piece = circles[j].astype(f32)
        main.append(piece)
        parts = [piece[Y_EXT * xx : Y_EXT * (xx + 1), 96:128] for xx in range(X_SUB)]
        extra.append(jnp.concatenate(parts + [jnp.zeros((Y_EXT, C_SUB), f32)], axis=1))
    g = jnp.concatenate(main + extra, axis=0).astype(bf16)
    spectrum = dot(table[...], g).astype(bf16)
    for q in range(QUADS):
        out[256 * q : 256 * q + KEPT, :] = spectrum[KEPT * q : KEPT * (q + 1)]
        out[256 * q + KEPT : 256 * (q + 1), :] = jnp.zeros((256 - KEPT, 128), bf16)


def bases_kernel(place, bases, first, second):
    m = place[0]

    def index(shape, axis):
        return lax.broadcasted_iota(jnp.int32, shape, axis)

    def pick(mask):
        return jnp.where(mask, 1.0, 0.0).astype(bf16)

    rows = bases[...].astype(f32).reshape(LAT_DEV * 24, NL).astype(bf16)
    wave = index((NL, 1), 0)
    tile = lax.shift_right_logical(wave * 5462, 16)
    chosen = pick(index((NL, LAT_DEV * 24), 1) == wave + 12 * tile)
    table = dot(chosen, rows)
    table = jnp.where(index((NL, NLAT), 0) >= m, table, 0.0).astype(bf16)
    spot = index((1, NLAT), 1)
    x = 12 * (spot & 31) + X_SUB * ((spot >> 5) & 3) + (spot >> 7)
    columns = pick(index((NLAT, NLAT), 0) == x)
    first[...] = dot(table, columns).astype(bf16)
    spot = index((NLAT, 1), 0)
    row = 24 * (spot & 31) + 12 + X_SUB * ((spot >> 5) & 3) + (spot >> 7)
    chosen = pick(index((NLAT, LAT_DEV * 24), 1) == row)
    table = dot(chosen, rows)
    second[...] = jnp.where(index((NLAT, NL), 1) >= m, table, 0.0).astype(bf16)


def legendre_kernel(place, coeffs, *rest):
    sources, (gain, out, rows, tables, sems) = rest[:8], rest[8:]
    mine = place[1]
    copies = [
        pltpu.make_async_copy(source, tables.at[mine ^ (n // 2), n % 2], sems.at[n])
        for n, source in enumerate(sources)
    ]
    for copy in copies:
        copy.start()
    rows[...] = coeffs[...].astype(f32)
    fourier = []
    for e in range(4):
        blocks = [
            [rows[pl.ds(256 * xg + 2 * e + r, LAT_DEV, stride=8), :] for r in range(2)]
            for xg in range(XG)
        ]
        stack = []
        for xx in range(X_SUB):
            for xg in range(XG):
                parts = [blocks[xg][r][:, C_SUB * xx : C_SUB * (xx + 1)] for r in range(2)]
                stack.append(jnp.concatenate(parts, axis=1))
        fourier.append(jnp.concatenate(stack, axis=0).astype(bf16))
    quarter = [gain[:, C_SUB * cg : C_SUB * (cg + 1)] for cg in range(CG)]
    low = jnp.where(mine // 2 == 0, quarter[0], quarter[1])
    high = jnp.where(mine // 2 == 0, quarter[2], quarter[3])
    quarter = jnp.where(mine % 2 == 0, low, high)
    gains = jnp.concatenate([quarter, quarter], axis=1)
    for copy in copies:
        copy.wait()
    filtered = [(dot(tables[e, 0], fourier[e]) * gains).astype(bf16) for e in range(4)]
    results = [dot(tables[e, 1], filtered[e]) for e in range(4)]
    for xg in range(XG):
        for e in range(4):
            for r in range(2):
                parts = [
                    results[e][32 * (XG * xx + xg) : 32 * (XG * xx + xg + 1), C_SUB * r : C_SUB * (r + 1)]
                    for xx in range(X_SUB)
                ]
                parts.append(jnp.zeros((LAT_DEV, C_SUB), f32))
                rows[pl.ds(256 * xg + 2 * e + r, LAT_DEV, stride=8), :] = jnp.concatenate(parts, axis=1)
    out[...] = rows[...].astype(bf16)


def inverse_kernel(coeffs, table, out):
    z = jnp.concatenate([coeffs[256 * q : 256 * q + KEPT, :] for q in range(QUADS)], axis=0)
    g = dot(table[...], z)
    for j in range(LON_DEV):
        main = g[Y_MAIN * j : Y_MAIN * (j + 1), 0:96]
        first = LON_DEV * Y_MAIN + Y_EXT * j
        extra = g[first : first + Y_EXT]
        parts = [extra[:, C_SUB * xx : C_SUB * (xx + 1)] for xx in range(X_SUB)]
        out[j] = jnp.concatenate([main, jnp.concatenate(parts, axis=0)], axis=1).astype(bf16)


def grid_kernel(pieces, out):
    for xg in range(XG):
        blocks = [pieces[owner(xg, cg)].astype(f32) for cg in range(CG)]
        for xx in range(X_SUB):
            main = [b[:, C_SUB * xx : C_SUB * (xx + 1)] for b in blocks]
            extra = [b[Y_EXT * xx : Y_EXT * (xx + 1), 96:128] for b in blocks]
            out[X_SUB * xg + xx, 0:Y_MAIN, :] = jnp.concatenate(main, axis=1)
            out[X_SUB * xg + xx, Y_MAIN:, :] = jnp.concatenate(extra, axis=1)[0 : Y_DEV - Y_MAIN]


def call(
    kernel, shape, dtype, scratch=(), smem=0, space=pltpu.VMEM, far=(), flops=0, moved=0, limit=VMEM
):
    outs = [jax.ShapeDtypeStruct(s, dtype) for s in (shape if isinstance(shape, list) else [shape])]
    places = [pl.BlockSpec(memory_space=pltpu.VMEM) for _ in outs]
    single = not isinstance(shape, list)

    def run(*args):
        specs = [
            pl.BlockSpec(memory_space=pltpu.SMEM if k < smem else pltpu.HBM if k in far else space)
            for k in range(len(args))
        ]
        return pl.pallas_call(
            kernel,
            out_shape=outs[0] if single else outs,
            in_specs=specs,
            out_specs=places[0] if single else places,
            scratch_shapes=list(scratch),
            compiler_params=pltpu.CompilerParams(vmem_limit_bytes=limit),
            cost_estimate=pl.CostEstimate(flops=flops, bytes_accessed=moved, transcendentals=0),
        )(*args)

    return run


def arrange(first, second):
    shape = pltpu.VMEM((12, M_DEV, NL), bf16)
    rows = pltpu.VMEM((3, M_DEV * 24, 128), f32)
    return call(
        arrange_kernel,
        (LAT_DEV, 24, NL),
        bf16,
        (shape, shape, rows, pltpu.SemaphoreType.DMA((2,))),
        space=pltpu.HBM,
        limit=NETWORK_VMEM,
    )(first, second)


def on_device(
    saved, cotangent, w_in, b_in, w_mid, b_mid, w_out, spectral_gain, basis_in, basis_out
):
    forward, back = zonal_tables()
    bases = arrange(jnp.transpose(basis_in, (2, 1, 0)), basis_out)
    bases, saved = lax.optimization_barrier((bases, saved))
    bases = lax.all_to_all(bases, "lat", 0, 0, tiled=True)
    weights = (w_in, b_in.reshape(1, -1), w_mid, b_mid.reshape(1, -1), w_out)
    held = [pltpu.VMEM(a.shape, a.dtype) for a in (saved, cotangent) + weights]
    pad = pltpu.VMEM((X_DEV, Y_PAD, CHAN), bf16)
    pieces = call(
        network_kernel,
        (LON_DEV, Y_MAIN, 128),
        bf16,
        held + [pad, pad, pltpu.SemaphoreType.DMA((7,))],
        space=pltpu.HBM,
        flops=1_700_000_000,
        moved=4_000_000,
        limit=NETWORK_VMEM,
    )(saved, cotangent, *weights)
    bases, pieces = lax.optimization_barrier((bases, pieces))
    pieces = lax.all_to_all(pieces, LON, 0, 0, tiled=True)
    mode = M_DEV * lax.axis_index(LON) + lax.axis_index("lat")
    mine = 2 * lax.axis_index("x_hi") + lax.axis_index("core")
    place = jnp.stack([mode, mine]).astype(jnp.int32)
    tables = call(
        bases_kernel, [(NL, NLAT), (NLAT, NL)], bf16, smem=1, flops=600_000_000, moved=3_000_000
    )(place, bases)
    swap = [(0, 1), (1, 0)]
    near = [lax.ppermute(t, "core", swap) for t in tables]
    far = [lax.ppermute(t, "x_hi", swap) for t in tables]
    both = [lax.ppermute(t, "core", swap) for t in far]
    shared = (*tables, *near, *far, *both)
    coeffs = call(zonal_kernel, (2 * DEVS, 128), bf16, flops=300_000_000)(
        pieces, jnp.asarray(forward)
    )
    coeffs = lax.all_to_all(coeffs.reshape(DEVS // 4, 8, 128), LONG, 0, 0, tiled=True)
    coeffs = call(
        legendre_kernel,
        (2 * DEVS, 128),
        bf16,
        (
            pltpu.VMEM((2 * DEVS, 128), f32),
            pltpu.VMEM((4, 2, NL, NLAT), bf16),
            pltpu.SemaphoreType.DMA((8,)),
        ),
        smem=1,
        far=tuple(range(2, 10)),
        limit=57 * 1024 * 1024,
        flops=200_000_000,
    )(place, coeffs.reshape(2 * DEVS, 128), *shared, spectral_gain)
    coeffs, back = lax.optimization_barrier((coeffs, jnp.asarray(back)))
    coeffs = lax.all_to_all(coeffs.reshape(DEVS // 4, 8, 128), LONG, 0, 0, tiled=True)
    pieces = call(inverse_kernel, (LON_DEV, Y_MAIN, 128), bf16, flops=300_000_000)(
        coeffs.reshape(2 * DEVS, 128), back
    )
    pieces = lax.all_to_all(pieces, LON, 0, 0, tiled=True)
    return call(grid_kernel, (X_DEV, Y_DEV, CHAN), f32)(pieces)


def solution(mesh):
    grid = P("lat", LON, None)
    placed = (grid, grid, P(), P(), P(), P(), P(), P(), P(None, LON, "lat"), grid)
    fine = Mesh(mesh.devices.reshape(LAT_DEV, 2, 2, 2, 2), ("lat",) + LON)
    return jax.shard_map(on_device, mesh=fine, in_specs=placed, out_specs=grid, check_vma=False)
```

```python
import numpy as np
import jax
import jax.numpy as jnp
from jax import lax
from jax.experimental import pallas as pl
from jax.experimental.pallas import tpu as pltpu
from jax.sharding import Mesh, PartitionSpec as P

bf16 = jnp.bfloat16
f32 = jnp.float32

LAT_DEV, LON_DEV = 32, 16
QUADS = 4
X_DEV, Y_DEV = 12, 90
Y_PAD = 96
Y_MAIN, Y_EXT = 72, 24
NLAT, NLON, NM, NL, CHAN = 384, 1440, 368, 384, 128
M_DEV = 23
X_SUB, C_SUB = 3, 32
CG = CHAN // C_SUB
XG = X_DEV // X_SUB
DEVS = LAT_DEV * LON_DEV
ROWS = 2 * NM
LON = ("x_hi", "x_lo", "z_hi", "core")
LONG = ("x_lo", "z_hi", "lat")
KEPT = 192
VMEM = 16 * 1024 * 1024
NETWORK_VMEM = 59 * 1024 * 1024


def zonal_tables():
    q, i, e = np.meshgrid(np.arange(4), np.arange(M_DEV), np.arange(4), indexing="ij")
    order = (M_DEV * (8 * (e // 2) + 2 * q + e % 2) + i).reshape(-1)
    turns = (order[:, None] * np.arange(NLON)[None, :]) % NLON
    angles = turns.astype(np.float64) * (2.0 * np.pi / NLON)
    table = np.stack([np.cos(angles), -np.sin(angles)], 1).reshape(ROWS, NLON)
    weight = np.where(order == 0, 1.0, 2.0) / NLON
    back = table * np.repeat(weight, 2)[:, None]

    def split_y(t):
        t = np.pad(t.reshape(QUADS, ROWS // QUADS, NLON), ((0, 0), (0, KEPT - ROWS // QUADS), (0, 0)))
        t = t.reshape(QUADS * KEPT, LON_DEV, Y_DEV)
        t = np.pad(t, ((0, 0), (0, 0), (0, Y_PAD - Y_DEV)))
        main = t[:, :, :Y_MAIN].reshape(QUADS * KEPT, LON_DEV * Y_MAIN)
        extra = t[:, :, Y_MAIN:].reshape(QUADS * KEPT, LON_DEV * Y_EXT)
        return np.concatenate([main, extra], 1)

    return (
        np.asarray(split_y(table), dtype=jnp.bfloat16),
        np.ascontiguousarray(split_y(back).T).astype(jnp.bfloat16),
    )


def owner(xg, cg):
    return 8 * (cg % 2) + 2 * xg + cg // 2


def dot(a, b):
    return lax.dot_general(a, b, (((1,), (0,)), ((), ())), preferred_element_type=f32)


def dot_t(a, b):
    return lax.dot_general(a, b, (((1,), (1,)), ((), ())), preferred_element_type=f32)


def sigmoid(v):
    return 0.5 * jnp.tanh(0.5 * v) + 0.5


def arrange_kernel(first_h, second_h, out, first, second, rows, sems):
    copies = [
        pltpu.make_async_copy(first_h, first, sems.at[0]),
        pltpu.make_async_copy(second_h, second, sems.at[1]),
    ]
    for copy in copies:
        copy.start()
    out[M_DEV:] = jnp.zeros((LAT_DEV - M_DEV, 24, NL), bf16)
    for half, source in enumerate((first, second)):
        copies[half].wait()
        for k in range(12):
            block = source[k].astype(f32)
            for t in range(3):
                rows[t, pl.ds(12 * half + k, M_DEV, stride=24), :] = block[:, 128 * t : 128 * (t + 1)]
    for m in range(M_DEV):
        for t in range(3):
            out[m, :, 128 * t : 128 * (t + 1)] = rows[t, 24 * m : 24 * (m + 1), :].astype(bf16)


def network_kernel(
    saved_h, cotan_h, w_in_h, b_in_h, w_mid_h, b_mid_h, w_out_h, out,
    saved, cotan, w_in, b_in, w_mid, b_mid, w_out, rows_s, rows_c, sems,
):
    pairs = (
        (saved_h, saved), (w_in_h, w_in), (b_in_h, b_in), (w_mid_h, w_mid),
        (b_mid_h, b_mid), (cotan_h, cotan), (w_out_h, w_out),
    )
    copies = [pltpu.make_async_copy(a, b, sems.at[k]) for k, (a, b) in enumerate(pairs)]
    for copy in copies:
        copy.start()
    got = dict(zip(("saved", "w_in", "b_in", "w_mid", "b_mid", "cotan", "w_out"), copies))
    edge = jnp.zeros((X_DEV, 16, CHAN), bf16)
    rows_s[:, Y_PAD - 16 :, :] = edge
    rows_c[:, Y_PAD - 16 :, :] = edge
    got["saved"].wait()
    for x in range(X_DEV):
        rows_s[x, 0:Y_DEV, :] = saved[x]
    got["w_in"].wait()
    got["b_in"].wait()
    for xg in range(XG):
        s = rows_s[X_SUB * xg : X_SUB * (xg + 1)].reshape(X_SUB * Y_PAD, CHAN)
        first = dot(s, w_in[...]) + b_in[...]
        sig = sigmoid(first)
        act = first * sig
        slope_one = sig + act * (1.0 - sig)
        if xg == 0:
            got["w_mid"].wait()
            got["b_mid"].wait()
        second = dot(act.astype(bf16), w_mid[...]) + b_mid[...]
        sig = sigmoid(second)
        slope_two = sig * (1.0 + second * (1.0 - sig))
        if xg == 0:
            got["cotan"].wait()
            got["w_out"].wait()
            for x in range(X_DEV):
                rows_c[x, 0:Y_DEV, :] = cotan[x]
        c = rows_c[X_SUB * xg : X_SUB * (xg + 1)].reshape(X_SUB * Y_PAD, CHAN)
        back_two = (dot_t(c, w_out[...]) * slope_two).astype(bf16)
        back_one = (dot_t(back_two, w_mid[...]) * slope_one).astype(bf16)
        grad = c.astype(f32) + dot_t(back_one, w_in[...])
        grad = grad.reshape(X_SUB, Y_PAD, CHAN)
        for cg in range(CG):
            parts = [grad[xx][:, C_SUB * cg : C_SUB * (cg + 1)] for xx in range(X_SUB)]
            parts = [p[0:Y_MAIN] for p in parts] + [
                jnp.concatenate([p[Y_MAIN:] for p in parts], axis=0)
            ]
            out[owner(xg, cg)] = jnp.concatenate(parts, axis=1).astype(bf16)


def zonal_kernel(circles, table, out):
    main, extra = [], []
    for j in range(LON_DEV):
        piece = circles[j].astype(f32)
        main.append(piece)
        parts = [piece[Y_EXT * xx : Y_EXT * (xx + 1), 96:128] for xx in range(X_SUB)]
        extra.append(jnp.concatenate(parts + [jnp.zeros((Y_EXT, C_SUB), f32)], axis=1))
    g = jnp.concatenate(main + extra, axis=0).astype(bf16)
    spectrum = dot(table[...], g).astype(bf16)
    for q in range(QUADS):
        out[256 * q : 256 * q + KEPT, :] = spectrum[KEPT * q : KEPT * (q + 1)]
        out[256 * q + KEPT : 256 * (q + 1), :] = jnp.zeros((256 - KEPT, 128), bf16)


def bases_kernel(place, bases, pair, first, second):
    m = place[0]

    def index(shape, axis):
        return lax.broadcasted_iota(jnp.int32, shape, axis)

    def pick(mask):
        return jnp.where(mask, 1.0, 0.0).astype(bf16)

    rows = bases[...].astype(f32).reshape(LAT_DEV * 24, NL).astype(bf16)
    wave = index((NL, 1), 0)
    tile = lax.shift_right_logical(wave * 5462, 16)
    chosen = pick(index((NL, LAT_DEV * 24), 1) == wave + 12 * tile)
    table = dot(chosen, rows)
    table = jnp.where(index((NL, NLAT), 0) >= m, table, 0.0).astype(bf16)
    spot = index((1, NLAT), 1)
    x = 12 * (spot & 31) + X_SUB * ((spot >> 5) & 3) + (spot >> 7)
    columns = pick(index((NLAT, NLAT), 0) == x)
    first[...] = dot(table, columns).astype(bf16)
    pair[0] = first[...]
    spot = index((NLAT, 1), 0)
    row = 24 * (spot & 31) + 12 + X_SUB * ((spot >> 5) & 3) + (spot >> 7)
    chosen = pick(index((NLAT, LAT_DEV * 24), 1) == row)
    table = dot(chosen, rows)
    second[...] = jnp.where(index((NLAT, NL), 1) >= m, table, 0.0).astype(bf16)
    pair[1] = second[...]


def legendre_kernel(place, coeffs, *rest):
    sources, (gain, out, rows, tables, sems) = rest[:6], rest[6:]
    mine = place[1]
    slots = [tables.at[mine], tables.at[mine ^ 1]]
    slots += [tables.at[mine ^ d, n] for d in (2, 3) for n in range(2)]
    copies = [
        pltpu.make_async_copy(source, slot, sems.at[n])
        for n, (source, slot) in enumerate(zip(sources, slots))
    ]
    for copy in copies:
        copy.start()
    rows[...] = coeffs[...].astype(f32)
    fourier = []
    for e in range(4):
        blocks = [
            [rows[pl.ds(256 * xg + 2 * e + r, LAT_DEV, stride=8), :] for r in range(2)]
            for xg in range(XG)
        ]
        stack = []
        for xx in range(X_SUB):
            for xg in range(XG):
                parts = [blocks[xg][r][:, C_SUB * xx : C_SUB * (xx + 1)] for r in range(2)]
                stack.append(jnp.concatenate(parts, axis=1))
        fourier.append(jnp.concatenate(stack, axis=0).astype(bf16))
    quarter = [gain[:, C_SUB * cg : C_SUB * (cg + 1)] for cg in range(CG)]
    low = jnp.where(mine // 2 == 0, quarter[0], quarter[1])
    high = jnp.where(mine // 2 == 0, quarter[2], quarter[3])
    quarter = jnp.where(mine % 2 == 0, low, high)
    gains = jnp.concatenate([quarter, quarter], axis=1)
    for copy in copies:
        copy.wait()
    filtered = [(dot(tables[e, 0], fourier[e]) * gains).astype(bf16) for e in range(4)]
    results = [dot(tables[e, 1], filtered[e]) for e in range(4)]
    for xg in range(XG):
        for e in range(4):
            for r in range(2):
                parts = [
                    results[e][32 * (XG * xx + xg) : 32 * (XG * xx + xg + 1), C_SUB * r : C_SUB * (r + 1)]
                    for xx in range(X_SUB)
                ]
                parts.append(jnp.zeros((LAT_DEV, C_SUB), f32))
                rows[pl.ds(256 * xg + 2 * e + r, LAT_DEV, stride=8), :] = jnp.concatenate(parts, axis=1)
    out[...] = rows[...].astype(bf16)


def inverse_kernel(coeffs, table, out):
    z = jnp.concatenate([coeffs[256 * q : 256 * q + KEPT, :] for q in range(QUADS)], axis=0)
    g = dot(table[...], z)
    for j in range(LON_DEV):
        main = g[Y_MAIN * j : Y_MAIN * (j + 1), 0:96]
        first = LON_DEV * Y_MAIN + Y_EXT * j
        extra = g[first : first + Y_EXT]
        parts = [extra[:, C_SUB * xx : C_SUB * (xx + 1)] for xx in range(X_SUB)]
        out[j] = jnp.concatenate([main, jnp.concatenate(parts, axis=0)], axis=1).astype(bf16)


def grid_kernel(pieces, out):
    for xg in range(XG):
        blocks = [pieces[owner(xg, cg)].astype(f32) for cg in range(CG)]
        for xx in range(X_SUB):
            main = [b[:, C_SUB * xx : C_SUB * (xx + 1)] for b in blocks]
            extra = [b[Y_EXT * xx : Y_EXT * (xx + 1), 96:128] for b in blocks]
            out[X_SUB * xg + xx, 0:Y_MAIN, :] = jnp.concatenate(main, axis=1)
            out[X_SUB * xg + xx, Y_MAIN:, :] = jnp.concatenate(extra, axis=1)[0 : Y_DEV - Y_MAIN]


def call(
    kernel, shape, dtype, scratch=(), smem=0, space=pltpu.VMEM, far=(), flops=0, moved=0, limit=VMEM
):
    outs = [jax.ShapeDtypeStruct(s, dtype) for s in (shape if isinstance(shape, list) else [shape])]
    places = [pl.BlockSpec(memory_space=pltpu.VMEM) for _ in outs]
    single = not isinstance(shape, list)

    def run(*args):
        specs = [
            pl.BlockSpec(memory_space=pltpu.SMEM if k < smem else pltpu.HBM if k in far else space)
            for k in range(len(args))
        ]
        return pl.pallas_call(
            kernel,
            out_shape=outs[0] if single else outs,
            in_specs=specs,
            out_specs=places[0] if single else places,
            scratch_shapes=list(scratch),
            compiler_params=pltpu.CompilerParams(vmem_limit_bytes=limit),
            cost_estimate=pl.CostEstimate(flops=flops, bytes_accessed=moved, transcendentals=0),
        )(*args)

    return run


def arrange(first, second):
    shape = pltpu.VMEM((12, M_DEV, NL), bf16)
    rows = pltpu.VMEM((3, M_DEV * 24, 128), f32)
    return call(
        arrange_kernel,
        (LAT_DEV, 24, NL),
        bf16,
        (shape, shape, rows, pltpu.SemaphoreType.DMA((2,))),
        space=pltpu.HBM,
        limit=NETWORK_VMEM,
    )(first, second)


def on_device(
    saved, cotangent, w_in, b_in, w_mid, b_mid, w_out, spectral_gain, basis_in, basis_out
):
    forward, back = zonal_tables()
    bases = arrange(jnp.transpose(basis_in, (2, 1, 0)), basis_out)
    bases, saved = lax.optimization_barrier((bases, saved))
    bases = lax.all_to_all(bases, "lat", 0, 0, tiled=True)
    weights = (w_in, b_in.reshape(1, -1), w_mid, b_mid.reshape(1, -1), w_out)
    held = [pltpu.VMEM(a.shape, a.dtype) for a in (saved, cotangent) + weights]
    pad = pltpu.VMEM((X_DEV, Y_PAD, CHAN), bf16)
    pieces = call(
        network_kernel,
        (LON_DEV, Y_MAIN, 128),
        bf16,
        held + [pad, pad, pltpu.SemaphoreType.DMA((7,))],
        space=pltpu.HBM,
        flops=1_700_000_000,
        moved=4_000_000,
        limit=NETWORK_VMEM,
    )(saved, cotangent, *weights)
    bases, pieces = lax.optimization_barrier((bases, pieces))
    pieces = lax.all_to_all(pieces, LON, 0, 0, tiled=True)
    mode = M_DEV * lax.axis_index(LON) + lax.axis_index("lat")
    mine = 2 * lax.axis_index("x_hi") + lax.axis_index("core")
    place = jnp.stack([mode, mine]).astype(jnp.int32)
    pair, *tables = call(
        bases_kernel, [(2, NL, NLAT), (NL, NLAT), (NLAT, NL)], bf16, smem=1, flops=600_000_000, moved=3_000_000
    )(place, bases)
    swap = [(0, 1), (1, 0)]
    near = lax.ppermute(pair, "core", swap)
    far = [lax.ppermute(t, "x_hi", swap) for t in tables]
    both = [lax.ppermute(t, "core", swap) for t in far]
    shared = (pair, near, *far, *both)
    coeffs = call(zonal_kernel, (2 * DEVS, 128), bf16, flops=300_000_000)(
        pieces, jnp.asarray(forward)
    )
    coeffs = lax.all_to_all(coeffs.reshape(DEVS // 4, 8, 128), LONG, 0, 0, tiled=True)
    coeffs = call(
        legendre_kernel,
        (2 * DEVS, 128),
        bf16,
        (
            pltpu.VMEM((2 * DEVS, 128), f32),
            pltpu.VMEM((4, 2, NL, NLAT), bf16),
            pltpu.SemaphoreType.DMA((6,)),
        ),
        smem=1,
        far=tuple(range(2, 8)),
        flops=200_000_000,
    )(place, coeffs.reshape(2 * DEVS, 128), *shared, spectral_gain)
    coeffs, back = lax.optimization_barrier((coeffs, jnp.asarray(back)))
    coeffs = lax.all_to_all(coeffs.reshape(DEVS // 4, 8, 128), LONG, 0, 0, tiled=True)
    pieces = call(inverse_kernel, (LON_DEV, Y_MAIN, 128), bf16, flops=300_000_000)(
        coeffs.reshape(2 * DEVS, 128), back
    )
    pieces = lax.all_to_all(pieces, LON, 0, 0, tiled=True)
    return call(grid_kernel, (X_DEV, Y_DEV, CHAN), f32)(pieces)


def solution(mesh):
    grid = P("lat", LON, None)
    placed = (grid, grid, P(), P(), P(), P(), P(), P(), P(None, LON, "lat"), grid)
    fine = Mesh(mesh.devices.reshape(LAT_DEV, 2, 2, 2, 2), ("lat",) + LON)
    return jax.shard_map(on_device, mesh=fine, in_specs=placed, out_specs=grid, check_vma=False)
```

```python
import numpy as np
import jax
import jax.numpy as jnp
from jax import lax
from jax.experimental import pallas as pl
from jax.experimental.pallas import tpu as pltpu
from jax.sharding import Mesh, PartitionSpec as P

bf16 = jnp.bfloat16
f32 = jnp.float32

LAT_DEV, LON_DEV = 32, 16
PAIRS = LON_DEV // 2
X_DEV, Y_DEV = 12, 90
Y_PAD = 96
Y_MAIN, Y_EXT = 72, 24
NLAT, NLON, NM, NL, CHAN = 384, 1440, 368, 384, 128
M_DEV = 23
X_SUB, C_SUB = 3, 32
CG = CHAN // C_SUB
XG = X_DEV // X_SUB
DEVS = LAT_DEV * LON_DEV
ROWS = 2 * NM
LON = ("pair", "core")
LONG = ("pair", "lat")
KEPT = 96
VMEM = 16 * 1024 * 1024
NETWORK_VMEM = 59 * 1024 * 1024


def zonal_tables():
    k, i, h = np.meshgrid(np.arange(PAIRS), np.arange(M_DEV), np.arange(2), indexing="ij")
    order = (M_DEV * (2 * k + h) + i).reshape(-1)
    turns = (order[:, None] * np.arange(NLON)[None, :]) % NLON
    angles = turns.astype(np.float64) * (2.0 * np.pi / NLON)
    table = np.stack([np.cos(angles), -np.sin(angles)], 1).reshape(ROWS, NLON)
    weight = np.where(order == 0, 1.0, 2.0) / NLON
    back = table * np.repeat(weight, 2)[:, None]

    def split_y(t):
        t = np.pad(t.reshape(PAIRS, ROWS // PAIRS, NLON), ((0, 0), (0, KEPT - ROWS // PAIRS), (0, 0)))
        t = t.reshape(PAIRS * KEPT, LON_DEV, Y_DEV)
        t = np.pad(t, ((0, 0), (0, 0), (0, Y_PAD - Y_DEV)))
        main = t[:, :, :Y_MAIN].reshape(PAIRS * KEPT, LON_DEV * Y_MAIN)
        extra = t[:, :, Y_MAIN:].reshape(PAIRS * KEPT, LON_DEV * Y_EXT)
        return np.concatenate([main, extra], 1)

    return (
        np.asarray(split_y(table), dtype=jnp.bfloat16),
        np.ascontiguousarray(split_y(back).T).astype(jnp.bfloat16),
    )


def owner(xg, cg):
    return CG * xg + 2 * (cg % 2) + cg // 2


def dot(a, b):
    return lax.dot_general(a, b, (((1,), (0,)), ((), ())), preferred_element_type=f32)


def dot_t(a, b):
    return lax.dot_general(a, b, (((1,), (1,)), ((), ())), preferred_element_type=f32)


def sigmoid(v):
    return 0.5 * jnp.tanh(0.5 * v) + 0.5


def arrange_kernel(first_h, second_h, out, first, second, rows, sems):
    copies = [
        pltpu.make_async_copy(first_h, first, sems.at[0]),
        pltpu.make_async_copy(second_h, second, sems.at[1]),
    ]
    for copy in copies:
        copy.start()
    out[M_DEV:] = jnp.zeros((LAT_DEV - M_DEV, 24, NL), bf16)
    for half, source in enumerate((first, second)):
        copies[half].wait()
        for k in range(12):
            block = source[k].astype(f32)
            for t in range(3):
                rows[t, pl.ds(12 * half + k, M_DEV, stride=24), :] = block[:, 128 * t : 128 * (t + 1)]
    for m in range(M_DEV):
        for t in range(3):
            out[m, :, 128 * t : 128 * (t + 1)] = rows[t, 24 * m : 24 * (m + 1), :].astype(bf16)


def network_kernel(
    saved_h, cotan_h, w_in_h, b_in_h, w_mid_h, b_mid_h, w_out_h, out,
    saved, cotan, w_in, b_in, w_mid, b_mid, w_out, rows_s, rows_c, sems,
):
    pairs = (
        (saved_h, saved), (w_in_h, w_in), (b_in_h, b_in), (w_mid_h, w_mid),
        (b_mid_h, b_mid), (cotan_h, cotan), (w_out_h, w_out),
    )
    copies = [pltpu.make_async_copy(a, b, sems.at[k]) for k, (a, b) in enumerate(pairs)]
    for copy in copies:
        copy.start()
    got = dict(zip(("saved", "w_in", "b_in", "w_mid", "b_mid", "cotan", "w_out"), copies))
    edge = jnp.zeros((X_DEV, 16, CHAN), bf16)
    rows_s[:, Y_PAD - 16 :, :] = edge
    rows_c[:, Y_PAD - 16 :, :] = edge
    got["saved"].wait()
    for x in range(X_DEV):
        rows_s[x, 0:Y_DEV, :] = saved[x]
    got["w_in"].wait()
    got["b_in"].wait()
    for xg in range(XG):
        s = rows_s[X_SUB * xg : X_SUB * (xg + 1)].reshape(X_SUB * Y_PAD, CHAN)
        first = dot(s, w_in[...]) + b_in[...]
        sig = sigmoid(first)
        act = first * sig
        slope_one = sig + act * (1.0 - sig)
        if xg == 0:
            got["w_mid"].wait()
            got["b_mid"].wait()
        second = dot(act.astype(bf16), w_mid[...]) + b_mid[...]
        sig = sigmoid(second)
        slope_two = sig * (1.0 + second * (1.0 - sig))
        if xg == 0:
            got["cotan"].wait()
            got["w_out"].wait()
            for x in range(X_DEV):
                rows_c[x, 0:Y_DEV, :] = cotan[x]
        c = rows_c[X_SUB * xg : X_SUB * (xg + 1)].reshape(X_SUB * Y_PAD, CHAN)
        back_two = (dot_t(c, w_out[...]) * slope_two).astype(bf16)
        back_one = (dot_t(back_two, w_mid[...]) * slope_one).astype(bf16)
        grad = c.astype(f32) + dot_t(back_one, w_in[...])
        grad = grad.reshape(X_SUB, Y_PAD, CHAN)
        for cg in range(CG):
            parts = [grad[xx][:, C_SUB * cg : C_SUB * (cg + 1)] for xx in range(X_SUB)]
            parts = [p[0:Y_MAIN] for p in parts] + [
                jnp.concatenate([p[Y_MAIN:] for p in parts], axis=0)
            ]
            out[owner(xg, cg)] = jnp.concatenate(parts, axis=1).astype(bf16)


def zonal_kernel(circles, table, out):
    main, extra = [], []
    for j in range(LON_DEV):
        piece = circles[j].astype(f32)
        main.append(piece)
        parts = [piece[Y_EXT * xx : Y_EXT * (xx + 1), 96:128] for xx in range(X_SUB)]
        extra.append(jnp.concatenate(parts + [jnp.zeros((Y_EXT, C_SUB), f32)], axis=1))
    g = jnp.concatenate(main + extra, axis=0).astype(bf16)
    spectrum = dot(table[...], g).astype(bf16)
    for k in range(PAIRS):
        out[128 * k : 128 * k + KEPT, :] = spectrum[KEPT * k : KEPT * (k + 1)]
        out[128 * k + KEPT : 128 * (k + 1), :] = jnp.zeros((128 - KEPT, 128), bf16)


def bases_kernel(place, bases, first, second):
    m = place[0]

    def index(shape, axis):
        return lax.broadcasted_iota(jnp.int32, shape, axis)

    def pick(mask):
        return jnp.where(mask, 1.0, 0.0).astype(bf16)

    rows = bases[...].astype(f32).reshape(LAT_DEV * 24, NL).astype(bf16)
    wave = index((NL, 1), 0)
    tile = lax.shift_right_logical(wave * 5462, 16)
    chosen = pick(index((NL, LAT_DEV * 24), 1) == wave + 12 * tile)
    table = dot(chosen, rows)
    table = jnp.where(index((NL, NLAT), 0) >= m, table, 0.0).astype(bf16)
    spot = index((1, NLAT), 1)
    x = 12 * (spot & 31) + X_SUB * ((spot >> 5) & 3) + (spot >> 7)
    columns = pick(index((NLAT, NLAT), 0) == x)
    first[...] = dot(table, columns).astype(bf16)
    spot = index((NLAT, 1), 0)
    row = 24 * (spot & 31) + 12 + X_SUB * ((spot >> 5) & 3) + (spot >> 7)
    chosen = pick(index((NLAT, LAT_DEV * 24), 1) == row)
    table = dot(chosen, rows)
    second[...] = jnp.where(index((NLAT, NL), 1) >= m, table, 0.0).astype(bf16)


def legendre_kernel(place, coeffs, *rest):
    tables, others, (gain, out, rows) = rest[0:2], rest[2:4], rest[4:]
    core = place[1]

    def swapped(pair):
        return jnp.where(core == 0, pair[0], pair[1]), jnp.where(core == 0, pair[1], pair[0])

    rows[...] = coeffs[...].astype(f32)
    blocks = [
        [rows[pl.ds(128 * k + n, LAT_DEV, stride=4), :] for n in range(4)] for k in range(PAIRS)
    ]
    modes = []
    for h in range(2):
        stack = []
        for xx in range(X_SUB):
            for xg in range(XG):
                parts = [
                    blocks[2 * xg + cq][2 * h + r][:, C_SUB * xx : C_SUB * (xx + 1)]
                    for r in range(2)
                    for cq in range(2)
                ]
                stack.append(jnp.concatenate(parts, axis=1))
        modes.append(jnp.concatenate(stack, axis=0))
    half = jnp.where(core == 0, gain[:, 0:64], gain[:, 64:128])
    gains = jnp.concatenate([half, half], axis=1)
    results = []
    for fourier, table in zip(swapped(modes), (tables, others)):
        filtered = (dot(table[0][...], fourier.astype(bf16)) * gains).astype(bf16)
        results.append(dot(table[1][...], filtered))
    results = swapped(results)
    for k in range(PAIRS):
        xg, cq = k // 2, k % 2
        for h in range(2):
            for r in range(2):
                first = 64 * r + C_SUB * cq
                parts = [
                    results[h][32 * (XG * xx + xg) : 32 * (XG * xx + xg + 1), first : first + C_SUB]
                    for xx in range(X_SUB)
                ]
                parts.append(jnp.zeros((LAT_DEV, C_SUB), f32))
                rows[pl.ds(128 * k + 2 * h + r, LAT_DEV, stride=4), :] = jnp.concatenate(parts, axis=1)
    out[...] = rows[...].astype(bf16)


def inverse_kernel(coeffs, table, out):
    z = jnp.concatenate([coeffs[128 * k : 128 * k + KEPT, :] for k in range(PAIRS)], axis=0)
    g = dot(table[...], z)
    for j in range(LON_DEV):
        main = g[Y_MAIN * j : Y_MAIN * (j + 1), 0:96]
        first = LON_DEV * Y_MAIN + Y_EXT * j
        extra = g[first : first + Y_EXT]
        parts = [extra[:, C_SUB * xx : C_SUB * (xx + 1)] for xx in range(X_SUB)]
        out[j] = jnp.concatenate([main, jnp.concatenate(parts, axis=0)], axis=1).astype(bf16)


def grid_kernel(pieces, out):
    for xg in range(XG):
        blocks = [pieces[owner(xg, cg)].astype(f32) for cg in range(CG)]
        for xx in range(X_SUB):
            main = [b[:, C_SUB * xx : C_SUB * (xx + 1)] for b in blocks]
            extra = [b[Y_EXT * xx : Y_EXT * (xx + 1), 96:128] for b in blocks]
            out[X_SUB * xg + xx, 0:Y_MAIN, :] = jnp.concatenate(main, axis=1)
            out[X_SUB * xg + xx, Y_MAIN:, :] = jnp.concatenate(extra, axis=1)[0 : Y_DEV - Y_MAIN]


def call(
    kernel, shape, dtype, scratch=(), smem=0, space=pltpu.VMEM, flops=0, moved=0, limit=VMEM
):
    outs = [jax.ShapeDtypeStruct(s, dtype) for s in (shape if isinstance(shape, list) else [shape])]
    places = [pl.BlockSpec(memory_space=pltpu.VMEM) for _ in outs]
    single = not isinstance(shape, list)

    def run(*args):
        specs = [
            pl.BlockSpec(memory_space=pltpu.SMEM if k < smem else space) for k in range(len(args))
        ]
        return pl.pallas_call(
            kernel,
            out_shape=outs[0] if single else outs,
            in_specs=specs,
            out_specs=places[0] if single else places,
            scratch_shapes=list(scratch),
            compiler_params=pltpu.CompilerParams(vmem_limit_bytes=limit),
            cost_estimate=pl.CostEstimate(flops=flops, bytes_accessed=moved, transcendentals=0),
        )(*args)

    return run


def arrange(first, second):
    shape = pltpu.VMEM((12, M_DEV, NL), bf16)
    rows = pltpu.VMEM((3, M_DEV * 24, 128), f32)
    return call(
        arrange_kernel,
        (LAT_DEV, 24, NL),
        bf16,
        (shape, shape, rows, pltpu.SemaphoreType.DMA((2,))),
        space=pltpu.HBM,
        limit=NETWORK_VMEM,
    )(first, second)


def on_device(
    saved, cotangent, w_in, b_in, w_mid, b_mid, w_out, spectral_gain, basis_in, basis_out
):
    forward, back = zonal_tables()
    bases = arrange(jnp.transpose(basis_in, (2, 1, 0)), basis_out)
    bases, saved = lax.optimization_barrier((bases, saved))
    bases = lax.all_to_all(bases, "lat", 0, 0, tiled=True)
    weights = (w_in, b_in.reshape(1, -1), w_mid, b_mid.reshape(1, -1), w_out)
    held = [pltpu.VMEM(a.shape, a.dtype) for a in (saved, cotangent) + weights]
    pad = pltpu.VMEM((X_DEV, Y_PAD, CHAN), bf16)
    pieces = call(
        network_kernel,
        (LON_DEV, Y_MAIN, 128),
        bf16,
        held + [pad, pad, pltpu.SemaphoreType.DMA((7,))],
        space=pltpu.HBM,
        flops=1_700_000_000,
        moved=4_000_000,
        limit=NETWORK_VMEM,
    )(saved, cotangent, *weights)
    bases, pieces = lax.optimization_barrier((bases, pieces))
    pieces = lax.all_to_all(pieces, LON, 0, 0, tiled=True)
    mode = M_DEV * lax.axis_index(LON) + lax.axis_index("lat")
    place = jnp.stack([mode, lax.axis_index("core")]).astype(jnp.int32)
    tables = call(
        bases_kernel, [(NL, NLAT), (NLAT, NL)], bf16, smem=1, flops=600_000_000, moved=3_000_000
    )(place, bases)
    others = [lax.ppermute(t, "core", [(0, 1), (1, 0)]) for t in tables]
    coeffs = call(zonal_kernel, (2 * DEVS, 128), bf16, flops=300_000_000)(
        pieces, jnp.asarray(forward)
    )
    coeffs = lax.all_to_all(coeffs.reshape(DEVS // 2, 4, 128), LONG, 0, 0, tiled=True)
    coeffs = call(
        legendre_kernel,
        (2 * DEVS, 128),
        bf16,
        (pltpu.VMEM((2 * DEVS, 128), f32),),
        smem=1,
        flops=200_000_000,
    )(place, coeffs.reshape(2 * DEVS, 128), *tables, *others, spectral_gain)
    coeffs, back = lax.optimization_barrier((coeffs, jnp.asarray(back)))
    coeffs = lax.all_to_all(coeffs.reshape(DEVS // 2, 4, 128), LONG, 0, 0, tiled=True)
    pieces = call(inverse_kernel, (LON_DEV, Y_MAIN, 128), bf16, flops=300_000_000)(
        coeffs.reshape(2 * DEVS, 128), back
    )
    pieces = lax.all_to_all(pieces, LON, 0, 0, tiled=True)
    return call(grid_kernel, (X_DEV, Y_DEV, CHAN), f32)(pieces)


def solution(mesh):
    grid = P("lat", LON, None)
    placed = (grid, grid, P(), P(), P(), P(), P(), P(), P(None, LON, "lat"), grid)
    fine = Mesh(mesh.devices.reshape(LAT_DEV, PAIRS, 2), ("lat",) + LON)
    return jax.shard_map(on_device, mesh=fine, in_specs=placed, out_specs=grid, check_vma=False)
```

```python
import numpy as np
import jax
import jax.numpy as jnp
from jax import lax
from jax.experimental import pallas as pl
from jax.experimental.pallas import tpu as pltpu
from jax.sharding import Mesh, PartitionSpec as P

bf16 = jnp.bfloat16
f32 = jnp.float32

LAT_DEV, LON_DEV = 32, 16
PAIRS = LON_DEV // 2
X_DEV, Y_DEV = 12, 90
Y_PAD = 96
Y_MAIN, Y_EXT = 72, 24
NLAT, NLON, NM, NL, CHAN = 384, 1440, 368, 384, 128
M_DEV = 23
X_SUB, C_SUB = 3, 32
CG = CHAN // C_SUB
XG = X_DEV // X_SUB
DEVS = LAT_DEV * LON_DEV
ROWS = 2 * NM
LON = ("pair", "core")
LONG = ("pair", "lat")
KEPT = 96
VMEM = 16 * 1024 * 1024
NETWORK_VMEM = 59 * 1024 * 1024


def zonal_tables():
    k, i, h = np.meshgrid(np.arange(PAIRS), np.arange(M_DEV), np.arange(2), indexing="ij")
    order = (M_DEV * (2 * k + h) + i).reshape(-1)
    turns = (order[:, None] * np.arange(NLON)[None, :]) % NLON
    angles = turns.astype(np.float64) * (2.0 * np.pi / NLON)
    table = np.stack([np.cos(angles), -np.sin(angles)], 1).reshape(ROWS, NLON)
    weight = np.where(order == 0, 1.0, 2.0) / NLON
    back = table * np.repeat(weight, 2)[:, None]

    def split_y(t):
        t = np.pad(t.reshape(PAIRS, ROWS // PAIRS, NLON), ((0, 0), (0, KEPT - ROWS // PAIRS), (0, 0)))
        t = t.reshape(PAIRS * KEPT, LON_DEV, Y_DEV)
        t = np.pad(t, ((0, 0), (0, 0), (0, Y_PAD - Y_DEV)))
        main = t[:, :, :Y_MAIN].reshape(PAIRS * KEPT, LON_DEV * Y_MAIN)
        extra = t[:, :, Y_MAIN:].reshape(PAIRS * KEPT, LON_DEV * Y_EXT)
        return np.concatenate([main, extra], 1)

    return (
        np.asarray(split_y(table), dtype=jnp.bfloat16),
        np.ascontiguousarray(split_y(back).T).astype(jnp.bfloat16),
    )


def owner(xg, cg):
    return CG * xg + 2 * (cg % 2) + cg // 2


def dot(a, b):
    return lax.dot_general(a, b, (((1,), (0,)), ((), ())), preferred_element_type=f32)


def dot_t(a, b):
    return lax.dot_general(a, b, (((1,), (1,)), ((), ())), preferred_element_type=f32)


def sigmoid(v):
    return 0.5 * jnp.tanh(0.5 * v) + 0.5


def network_kernel(
    saved_h, cotan_h, w_in_h, b_in_h, w_mid_h, b_mid_h, w_out_h, out,
    saved, cotan, w_in, b_in, w_mid, b_mid, w_out, rows_s, rows_c, sems,
):
    pairs = (
        (saved_h, saved), (w_in_h, w_in), (b_in_h, b_in), (w_mid_h, w_mid),
        (b_mid_h, b_mid), (cotan_h, cotan), (w_out_h, w_out),
    )
    copies = [pltpu.make_async_copy(a, b, sems.at[k]) for k, (a, b) in enumerate(pairs)]
    for copy in copies:
        copy.start()
    got = dict(zip(("saved", "w_in", "b_in", "w_mid", "b_mid", "cotan", "w_out"), copies))
    edge = jnp.zeros((X_DEV, 16, CHAN), bf16)
    rows_s[:, Y_PAD - 16 :, :] = edge
    rows_c[:, Y_PAD - 16 :, :] = edge
    got["saved"].wait()
    for x in range(X_DEV):
        rows_s[x, 0:Y_DEV, :] = saved[x]
    got["w_in"].wait()
    got["b_in"].wait()
    for xg in range(XG):
        s = rows_s[X_SUB * xg : X_SUB * (xg + 1)].reshape(X_SUB * Y_PAD, CHAN)
        first = dot(s, w_in[...]) + b_in[...]
        sig = sigmoid(first)
        act = first * sig
        slope_one = sig + act * (1.0 - sig)
        if xg == 0:
            got["w_mid"].wait()
            got["b_mid"].wait()
        second = dot(act.astype(bf16), w_mid[...]) + b_mid[...]
        sig = sigmoid(second)
        slope_two = sig * (1.0 + second * (1.0 - sig))
        if xg == 0:
            got["cotan"].wait()
            got["w_out"].wait()
            for x in range(X_DEV):
                rows_c[x, 0:Y_DEV, :] = cotan[x]
        c = rows_c[X_SUB * xg : X_SUB * (xg + 1)].reshape(X_SUB * Y_PAD, CHAN)
        back_two = (dot_t(c, w_out[...]) * slope_two).astype(bf16)
        back_one = (dot_t(back_two, w_mid[...]) * slope_one).astype(bf16)
        grad = c.astype(f32) + dot_t(back_one, w_in[...])
        grad = grad.reshape(X_SUB, Y_PAD, CHAN)
        for cg in range(CG):
            parts = [grad[xx][:, C_SUB * cg : C_SUB * (cg + 1)] for xx in range(X_SUB)]
            parts = [p[0:Y_MAIN] for p in parts] + [
                jnp.concatenate([p[Y_MAIN:] for p in parts], axis=0)
            ]
            out[owner(xg, cg)] = jnp.concatenate(parts, axis=1).astype(bf16)


def zonal_kernel(circles, table, out):
    main, extra = [], []
    for j in range(LON_DEV):
        piece = circles[j].astype(f32)
        main.append(piece)
        parts = [piece[Y_EXT * xx : Y_EXT * (xx + 1), 96:128] for xx in range(X_SUB)]
        extra.append(jnp.concatenate(parts + [jnp.zeros((Y_EXT, C_SUB), f32)], axis=1))
    g = jnp.concatenate(main + extra, axis=0).astype(bf16)
    spectrum = dot(table[...], g).astype(bf16)
    for k in range(PAIRS):
        out[128 * k : 128 * k + KEPT, :] = spectrum[KEPT * k : KEPT * (k + 1)]
        out[128 * k + KEPT : 128 * (k + 1), :] = jnp.zeros((128 - KEPT, 128), bf16)


def bases_kernel(place, bases, out):
    m = place[0]

    def index(shape, axis):
        return lax.broadcasted_iota(jnp.int32, shape, axis)

    def pick(mask):
        return jnp.where(mask, 1.0, 0.0).astype(bf16)

    rows = bases[...].astype(f32).reshape(LAT_DEV * 24, NL).astype(bf16)
    wave = index((NL, 1), 0)
    tile = lax.shift_right_logical(wave * 5462, 16)
    chosen = pick(index((NL, LAT_DEV * 24), 1) == wave + 12 * tile)
    table = dot(chosen, rows)
    table = jnp.where(index((NL, NLAT), 0) >= m, table, 0.0).astype(bf16)
    spot = index((1, NLAT), 1)
    x = 12 * (spot & 31) + X_SUB * ((spot >> 5) & 3) + (spot >> 7)
    columns = pick(index((NLAT, NLAT), 0) == x)
    out[0] = dot(table, columns).astype(bf16)
    spot = index((NLAT, 1), 0)
    row = 24 * (spot & 31) + 12 + X_SUB * ((spot >> 5) & 3) + (spot >> 7)
    chosen = pick(index((NLAT, LAT_DEV * 24), 1) == row)
    table = dot(chosen, rows)
    out[1] = jnp.where(index((NLAT, NL), 1) >= m, table, 0.0).astype(bf16)


def legendre_kernel(place, coeffs, tables, others, gain, out, rows):
    core = place[1]

    def swapped(pair):
        return jnp.where(core == 0, pair[0], pair[1]), jnp.where(core == 0, pair[1], pair[0])

    rows[...] = coeffs[...].astype(f32)
    blocks = [
        [rows[pl.ds(128 * k + n, LAT_DEV, stride=4), :] for n in range(4)] for k in range(PAIRS)
    ]
    modes = []
    for h in range(2):
        stack = []
        for xx in range(X_SUB):
            for xg in range(XG):
                parts = [
                    blocks[2 * xg + cq][2 * h + r][:, C_SUB * xx : C_SUB * (xx + 1)]
                    for r in range(2)
                    for cq in range(2)
                ]
                stack.append(jnp.concatenate(parts, axis=1))
        modes.append(jnp.concatenate(stack, axis=0))
    half = jnp.where(core == 0, gain[:, 0:64], gain[:, 64:128])
    gains = jnp.concatenate([half, half], axis=1)
    results = []
    for fourier, table in zip(swapped(modes), (tables, others)):
        filtered = (dot(table[0], fourier.astype(bf16)) * gains).astype(bf16)
        results.append(dot(table[1], filtered))
    results = swapped(results)
    for k in range(PAIRS):
        xg, cq = k // 2, k % 2
        for h in range(2):
            for r in range(2):
                first = 64 * r + C_SUB * cq
                parts = [
                    results[h][32 * (XG * xx + xg) : 32 * (XG * xx + xg + 1), first : first + C_SUB]
                    for xx in range(X_SUB)
                ]
                parts.append(jnp.zeros((LAT_DEV, C_SUB), f32))
                rows[pl.ds(128 * k + 2 * h + r, LAT_DEV, stride=4), :] = jnp.concatenate(parts, axis=1)
    out[...] = rows[...].astype(bf16)


def inverse_kernel(coeffs, table, out):
    z = jnp.concatenate([coeffs[128 * k : 128 * k + KEPT, :] for k in range(PAIRS)], axis=0)
    g = dot(table[...], z)
    for j in range(LON_DEV):
        main = g[Y_MAIN * j : Y_MAIN * (j + 1), 0:96]
        first = LON_DEV * Y_MAIN + Y_EXT * j
        extra = g[first : first + Y_EXT]
        parts = [extra[:, C_SUB * xx : C_SUB * (xx + 1)] for xx in range(X_SUB)]
        out[j] = jnp.concatenate([main, jnp.concatenate(parts, axis=0)], axis=1).astype(bf16)


def grid_kernel(pieces, out):
    for xg in range(XG):
        blocks = [pieces[owner(xg, cg)].astype(f32) for cg in range(CG)]
        for xx in range(X_SUB):
            main = [b[:, C_SUB * xx : C_SUB * (xx + 1)] for b in blocks]
            extra = [b[Y_EXT * xx : Y_EXT * (xx + 1), 96:128] for b in blocks]
            out[X_SUB * xg + xx, 0:Y_MAIN, :] = jnp.concatenate(main, axis=1)
            out[X_SUB * xg + xx, Y_MAIN:, :] = jnp.concatenate(extra, axis=1)[0 : Y_DEV - Y_MAIN]


def call(
    kernel, shape, dtype, scratch=(), smem=0, space=pltpu.VMEM, flops=0, moved=0, limit=VMEM
):
    outs = [jax.ShapeDtypeStruct(s, dtype) for s in (shape if isinstance(shape, list) else [shape])]
    places = [pl.BlockSpec(memory_space=pltpu.VMEM) for _ in outs]
    single = not isinstance(shape, list)

    def run(*args):
        specs = [
            pl.BlockSpec(memory_space=pltpu.SMEM if k < smem else space) for k in range(len(args))
        ]
        return pl.pallas_call(
            kernel,
            out_shape=outs[0] if single else outs,
            in_specs=specs,
            out_specs=places[0] if single else places,
            scratch_shapes=list(scratch),
            compiler_params=pltpu.CompilerParams(vmem_limit_bytes=limit),
            cost_estimate=pl.CostEstimate(flops=flops, bytes_accessed=moved, transcendentals=0),
        )(*args)

    return run


def on_device(
    saved, cotangent, w_in, b_in, w_mid, b_mid, w_out, spectral_gain, basis_in, basis_out
):
    forward, back = zonal_tables()
    bases = jnp.concatenate(
        [jnp.transpose(basis_in, (1, 2, 0)), jnp.transpose(basis_out, (1, 0, 2))], axis=1
    )
    bases = jnp.pad(bases, ((0, LAT_DEV - M_DEV), (0, 0), (0, 0)))
    bases, saved = lax.optimization_barrier((bases, saved))
    bases = lax.all_to_all(bases, "lat", 0, 0, tiled=True)
    weights = (w_in, b_in.reshape(1, -1), w_mid, b_mid.reshape(1, -1), w_out)
    held = [pltpu.VMEM(a.shape, a.dtype) for a in (saved, cotangent) + weights]
    pad = pltpu.VMEM((X_DEV, Y_PAD, CHAN), bf16)
    pieces = call(
        network_kernel,
        (LON_DEV, Y_MAIN, 128),
        bf16,
        held + [pad, pad, pltpu.SemaphoreType.DMA((7,))],
        space=pltpu.HBM,
        flops=1_700_000_000,
        moved=4_000_000,
        limit=NETWORK_VMEM,
    )(saved, cotangent, *weights)
    bases, pieces = lax.optimization_barrier((bases, pieces))
    pieces = lax.all_to_all(pieces, LON, 0, 0, tiled=True)
    mode = M_DEV * lax.axis_index(LON) + lax.axis_index("lat")
    place = jnp.stack([mode, lax.axis_index("core")]).astype(jnp.int32)
    tables = call(bases_kernel, (2, NL, NLAT), bf16, smem=1, flops=600_000_000, moved=3_000_000)(
        place, bases
    )
    others = lax.ppermute(tables, "core", [(0, 1), (1, 0)])
    coeffs = call(zonal_kernel, (2 * DEVS, 128), bf16, flops=300_000_000)(
        pieces, jnp.asarray(forward)
    )
    coeffs = lax.all_to_all(coeffs.reshape(DEVS // 2, 4, 128), LONG, 0, 0, tiled=True)
    coeffs = call(
        legendre_kernel,
        (2 * DEVS, 128),
        bf16,
        (pltpu.VMEM((2 * DEVS, 128), f32),),
        smem=1,
        flops=200_000_000,
    )(place, coeffs.reshape(2 * DEVS, 128), tables, others, spectral_gain)
    coeffs, back = lax.optimization_barrier((coeffs, jnp.asarray(back)))
    coeffs = lax.all_to_all(coeffs.reshape(DEVS // 2, 4, 128), LONG, 0, 0, tiled=True)
    pieces = call(inverse_kernel, (LON_DEV, Y_MAIN, 128), bf16, flops=300_000_000)(
        coeffs.reshape(2 * DEVS, 128), back
    )
    pieces = lax.all_to_all(pieces, LON, 0, 0, tiled=True)
    return call(grid_kernel, (X_DEV, Y_DEV, CHAN), f32)(pieces)


def solution(mesh):
    grid = P("lat", LON, None)
    placed = (grid, grid, P(), P(), P(), P(), P(), P(), P(None, LON, "lat"), grid)
    fine = Mesh(mesh.devices.reshape(LAT_DEV, PAIRS, 2), ("lat",) + LON)
    return jax.shard_map(on_device, mesh=fine, in_specs=placed, out_specs=grid, check_vma=False)
```

```python
import numpy as np
import jax
import jax.numpy as jnp
from jax import lax
from jax.experimental import pallas as pl
from jax.experimental.pallas import tpu as pltpu
from jax.sharding import Mesh, PartitionSpec as P

bf16 = jnp.bfloat16
f32 = jnp.float32

LAT_DEV, LON_DEV = 32, 16
PAIRS = LON_DEV // 2
X_DEV, Y_DEV = 12, 90
Y_PAD = 96
Y_MAIN, Y_EXT = 72, 24
NLAT, NLON, NM, NL, CHAN = 384, 1440, 368, 384, 128
M_DEV = 23
X_SUB, C_SUB = 3, 32
CG = CHAN // C_SUB
XG = X_DEV // X_SUB
DEVS = LAT_DEV * LON_DEV
ROWS = 2 * NM
LON = ("pair", "core")
LONG = ("pair", "lat")
KEPT = 96
VMEM = 16 * 1024 * 1024
NETWORK_VMEM = 59 * 1024 * 1024


def zonal_tables():
    k, i, h = np.meshgrid(np.arange(PAIRS), np.arange(M_DEV), np.arange(2), indexing="ij")
    order = (M_DEV * (2 * k + h) + i).reshape(-1)
    turns = (order[:, None] * np.arange(NLON)[None, :]) % NLON
    angles = turns.astype(np.float64) * (2.0 * np.pi / NLON)
    table = np.stack([np.cos(angles), -np.sin(angles)], 1).reshape(ROWS, NLON)
    weight = np.where(order == 0, 1.0, 2.0) / NLON
    back = table * np.repeat(weight, 2)[:, None]

    def split_y(t):
        t = np.pad(t.reshape(PAIRS, ROWS // PAIRS, NLON), ((0, 0), (0, KEPT - ROWS // PAIRS), (0, 0)))
        t = t.reshape(PAIRS * KEPT, LON_DEV, Y_DEV)
        t = np.pad(t, ((0, 0), (0, 0), (0, Y_PAD - Y_DEV)))
        main = t[:, :, :Y_MAIN].reshape(PAIRS * KEPT, LON_DEV * Y_MAIN)
        extra = t[:, :, Y_MAIN:].reshape(PAIRS * KEPT, LON_DEV * Y_EXT)
        return np.concatenate([main, extra], 1)

    return (
        np.asarray(split_y(table), dtype=jnp.bfloat16),
        np.ascontiguousarray(split_y(back).T).astype(jnp.bfloat16),
    )


def owner(xg, cg):
    return CG * xg + 2 * (cg % 2) + cg // 2


def dot(a, b):
    return lax.dot_general(a, b, (((1,), (0,)), ((), ())), preferred_element_type=f32)


def dot_t(a, b):
    return lax.dot_general(a, b, (((1,), (1,)), ((), ())), preferred_element_type=f32)


def sigmoid(v):
    return 0.5 * jnp.tanh(0.5 * v) + 0.5


def network_kernel(
    saved_h, cotan_h, w_in_h, b_in_h, w_mid_h, b_mid_h, w_out_h, out,
    saved, cotan, w_in, b_in, w_mid, b_mid, w_out, rows_s, rows_c, sems,
):
    pairs = (
        (saved_h, saved), (w_in_h, w_in), (b_in_h, b_in), (w_mid_h, w_mid),
        (b_mid_h, b_mid), (cotan_h, cotan), (w_out_h, w_out),
    )
    copies = [pltpu.make_async_copy(a, b, sems.at[k]) for k, (a, b) in enumerate(pairs)]
    for copy in copies:
        copy.start()
    got = dict(zip(("saved", "w_in", "b_in", "w_mid", "b_mid", "cotan", "w_out"), copies))
    edge = jnp.zeros((X_DEV, 16, CHAN), bf16)
    rows_s[:, Y_PAD - 16 :, :] = edge
    rows_c[:, Y_PAD - 16 :, :] = edge
    got["saved"].wait()
    for x in range(X_DEV):
        rows_s[x, 0:Y_DEV, :] = saved[x]
    got["w_in"].wait()
    got["b_in"].wait()
    for xg in range(XG):
        s = rows_s[X_SUB * xg : X_SUB * (xg + 1)].reshape(X_SUB * Y_PAD, CHAN)
        first = dot(s, w_in[...]) + b_in[...]
        sig = sigmoid(first)
        act = first * sig
        slope_one = sig + act * (1.0 - sig)
        if xg == 0:
            got["w_mid"].wait()
            got["b_mid"].wait()
        second = dot(act.astype(bf16), w_mid[...]) + b_mid[...]
        sig = sigmoid(second)
        slope_two = sig * (1.0 + second * (1.0 - sig))
        if xg == 0:
            got["cotan"].wait()
            got["w_out"].wait()
            for x in range(X_DEV):
                rows_c[x, 0:Y_DEV, :] = cotan[x]
        c = rows_c[X_SUB * xg : X_SUB * (xg + 1)].reshape(X_SUB * Y_PAD, CHAN)
        back_two = (dot_t(c, w_out[...]) * slope_two).astype(bf16)
        back_one = (dot_t(back_two, w_mid[...]) * slope_one).astype(bf16)
        grad = c.astype(f32) + dot_t(back_one, w_in[...])
        grad = grad.reshape(X_SUB, Y_PAD, CHAN)
        for cg in range(CG):
            parts = [grad[xx][:, C_SUB * cg : C_SUB * (cg + 1)] for xx in range(X_SUB)]
            parts = [p[0:Y_MAIN] for p in parts] + [
                jnp.concatenate([p[Y_MAIN:] for p in parts], axis=0)
            ]
            out[owner(xg, cg)] = jnp.concatenate(parts, axis=1).astype(bf16)


def zonal_kernel(circles, table, out):
    main, extra = [], []
    for j in range(LON_DEV):
        piece = circles[j].astype(f32)
        main.append(piece)
        parts = [piece[Y_EXT * xx : Y_EXT * (xx + 1), 96:128] for xx in range(X_SUB)]
        extra.append(jnp.concatenate(parts + [jnp.zeros((Y_EXT, C_SUB), f32)], axis=1))
    g = jnp.concatenate(main + extra, axis=0).astype(bf16)
    spectrum = dot(table[...], g).astype(bf16)
    for k in range(PAIRS):
        out[128 * k : 128 * k + KEPT, :] = spectrum[KEPT * k : KEPT * (k + 1)]
        out[128 * k + KEPT : 128 * (k + 1), :] = jnp.zeros((128 - KEPT, 128), bf16)


def bases_kernel(place, bases, out):
    m = place[0]

    def index(shape, axis):
        return lax.broadcasted_iota(jnp.int32, shape, axis)

    def pick(mask):
        return jnp.where(mask, 1.0, 0.0).astype(bf16)

    rows = bases[...].astype(f32).reshape(LAT_DEV * 24, NL).astype(bf16)
    wave = index((NL, 1), 0)
    tile = lax.shift_right_logical(wave * 5462, 16)
    chosen = pick(index((NL, LAT_DEV * 24), 1) == wave + 12 * tile)
    table = dot(chosen, rows)
    table = jnp.where(index((NL, NLAT), 0) >= m, table, 0.0).astype(bf16)
    spot = index((1, NLAT), 1)
    x = 12 * (spot & 31) + X_SUB * ((spot >> 5) & 3) + (spot >> 7)
    columns = pick(index((NLAT, NLAT), 0) == x)
    out[0] = dot(table, columns).astype(bf16)
    spot = index((NLAT, 1), 0)
    row = 24 * (spot & 31) + 12 + X_SUB * ((spot >> 5) & 3) + (spot >> 7)
    chosen = pick(index((NLAT, LAT_DEV * 24), 1) == row)
    table = dot(chosen, rows)
    out[1] = jnp.where(index((NLAT, NL), 1) >= m, table, 0.0).astype(bf16)


def legendre_kernel(place, coeffs, tables, others, gain, out, rows):
    core = place[1]

    def swapped(pair):
        return jnp.where(core == 0, pair[0], pair[1]), jnp.where(core == 0, pair[1], pair[0])

    rows[...] = coeffs[...].astype(f32)
    blocks = [
        [rows[pl.ds(128 * k + n, LAT_DEV, stride=4), :] for n in range(4)] for k in range(PAIRS)
    ]
    modes = []
    for h in range(2):
        stack = []
        for xx in range(X_SUB):
            for xg in range(XG):
                parts = [
                    blocks[2 * xg + cq][2 * h + r][:, C_SUB * xx : C_SUB * (xx + 1)]
                    for r in range(2)
                    for cq in range(2)
                ]
                stack.append(jnp.concatenate(parts, axis=1))
        modes.append(jnp.concatenate(stack, axis=0))
    half = jnp.where(core == 0, gain[:, 0:64], gain[:, 64:128])
    gains = jnp.concatenate([half, half], axis=1)
    results = []
    for fourier, table in zip(swapped(modes), (tables, others)):
        filtered = (dot(table[0], fourier.astype(bf16)) * gains).astype(bf16)
        results.append(dot(table[1], filtered))
    results = swapped(results)
    for k in range(PAIRS):
        xg, cq = k // 2, k % 2
        for h in range(2):
            for r in range(2):
                first = 64 * r + C_SUB * cq
                parts = [
                    results[h][32 * (XG * xx + xg) : 32 * (XG * xx + xg + 1), first : first + C_SUB]
                    for xx in range(X_SUB)
                ]
                parts.append(jnp.zeros((LAT_DEV, C_SUB), f32))
                rows[pl.ds(128 * k + 2 * h + r, LAT_DEV, stride=4), :] = jnp.concatenate(parts, axis=1)
    out[...] = rows[...].astype(bf16)


def inverse_kernel(coeffs, table, out):
    z = jnp.concatenate([coeffs[128 * k : 128 * k + KEPT, :] for k in range(PAIRS)], axis=0)
    g = dot(table[...], z)
    for j in range(LON_DEV):
        main = g[Y_MAIN * j : Y_MAIN * (j + 1), 0:96]
        first = LON_DEV * Y_MAIN + Y_EXT * j
        extra = g[first : first + Y_EXT]
        parts = [extra[:, C_SUB * xx : C_SUB * (xx + 1)] for xx in range(X_SUB)]
        out[j] = jnp.concatenate([main, jnp.concatenate(parts, axis=0)], axis=1).astype(bf16)


def grid_kernel(pieces, out_h, out, sems):
    copies = []
    for xg in range(XG):
        blocks = [pieces[owner(xg, cg)].astype(f32) for cg in range(CG)]
        for xx in range(X_SUB):
            main = [b[:, C_SUB * xx : C_SUB * (xx + 1)] for b in blocks]
            extra = [b[Y_EXT * xx : Y_EXT * (xx + 1), 96:128] for b in blocks]
            out[X_SUB * xg + xx, 0:Y_MAIN, :] = jnp.concatenate(main, axis=1)
            out[X_SUB * xg + xx, Y_MAIN:, :] = jnp.concatenate(extra, axis=1)[0 : Y_DEV - Y_MAIN]
        rows = pl.ds(X_SUB * xg, X_SUB)
        copies.append(pltpu.make_async_copy(out.at[rows], out_h.at[rows], sems.at[xg]))
        copies[-1].start()
    for copy in copies:
        copy.wait()


def call(
    kernel, shape, dtype, scratch=(), smem=0, space=pltpu.VMEM, flops=0, moved=0, limit=VMEM, out_space=pltpu.VMEM
):
    outs = [jax.ShapeDtypeStruct(s, dtype) for s in (shape if isinstance(shape, list) else [shape])]
    places = [pl.BlockSpec(memory_space=out_space) for _ in outs]
    single = not isinstance(shape, list)

    def run(*args):
        specs = [
            pl.BlockSpec(memory_space=pltpu.SMEM if k < smem else space) for k in range(len(args))
        ]
        return pl.pallas_call(
            kernel,
            out_shape=outs[0] if single else outs,
            in_specs=specs,
            out_specs=places[0] if single else places,
            scratch_shapes=list(scratch),
            compiler_params=pltpu.CompilerParams(vmem_limit_bytes=limit),
            cost_estimate=pl.CostEstimate(flops=flops, bytes_accessed=moved, transcendentals=0),
        )(*args)

    return run


def on_device(
    saved, cotangent, w_in, b_in, w_mid, b_mid, w_out, spectral_gain, basis_in, basis_out
):
    forward, back = zonal_tables()
    bases = jnp.concatenate(
        [jnp.transpose(basis_in, (1, 2, 0)), jnp.transpose(basis_out, (1, 0, 2))], axis=1
    )
    bases = jnp.pad(bases, ((0, LAT_DEV - M_DEV), (0, 0), (0, 0)))
    bases, saved = lax.optimization_barrier((bases, saved))
    bases = lax.all_to_all(bases, "lat", 0, 0, tiled=True)
    weights = (w_in, b_in.reshape(1, -1), w_mid, b_mid.reshape(1, -1), w_out)
    held = [pltpu.VMEM(a.shape, a.dtype) for a in (saved, cotangent) + weights]
    pad = pltpu.VMEM((X_DEV, Y_PAD, CHAN), bf16)
    pieces = call(
        network_kernel,
        (LON_DEV, Y_MAIN, 128),
        bf16,
        held + [pad, pad, pltpu.SemaphoreType.DMA((7,))],
        space=pltpu.HBM,
        flops=1_700_000_000,
        moved=4_000_000,
        limit=NETWORK_VMEM,
    )(saved, cotangent, *weights)
    bases, pieces = lax.optimization_barrier((bases, pieces))
    pieces = lax.all_to_all(pieces, LON, 0, 0, tiled=True)
    mode = M_DEV * lax.axis_index(LON) + lax.axis_index("lat")
    place = jnp.stack([mode, lax.axis_index("core")]).astype(jnp.int32)
    tables = call(bases_kernel, (2, NL, NLAT), bf16, smem=1, flops=600_000_000, moved=3_000_000)(
        place, bases
    )
    others = lax.ppermute(tables, "core", [(0, 1), (1, 0)])
    coeffs = call(zonal_kernel, (2 * DEVS, 128), bf16, flops=300_000_000)(
        pieces, jnp.asarray(forward)
    )
    coeffs = lax.all_to_all(coeffs.reshape(DEVS // 2, 4, 128), LONG, 0, 0, tiled=True)
    coeffs = call(
        legendre_kernel,
        (2 * DEVS, 128),
        bf16,
        (pltpu.VMEM((2 * DEVS, 128), f32),),
        smem=1,
        flops=200_000_000,
    )(place, coeffs.reshape(2 * DEVS, 128), tables, others, spectral_gain)
    coeffs, back = lax.optimization_barrier((coeffs, jnp.asarray(back)))
    coeffs = lax.all_to_all(coeffs.reshape(DEVS // 2, 4, 128), LONG, 0, 0, tiled=True)
    pieces = call(inverse_kernel, (LON_DEV, Y_MAIN, 128), bf16, flops=300_000_000)(
        coeffs.reshape(2 * DEVS, 128), back
    )
    pieces = lax.all_to_all(pieces, LON, 0, 0, tiled=True)
    held = (pltpu.VMEM((X_DEV, Y_DEV, CHAN), f32), pltpu.SemaphoreType.DMA((XG,)))
    return call(grid_kernel, (X_DEV, Y_DEV, CHAN), f32, held, out_space=pltpu.HBM)(pieces)


def solution(mesh):
    grid = P("lat", LON, None)
    placed = (grid, grid, P(), P(), P(), P(), P(), P(), P(None, LON, "lat"), grid)
    fine = Mesh(mesh.devices.reshape(LAT_DEV, PAIRS, 2), ("lat",) + LON)
    return jax.shard_map(on_device, mesh=fine, in_specs=placed, out_specs=grid, check_vma=False)
```
